32 devices in a mesh: seq: 16 (over z, y, x), blk: 2 (over core).
Axes of the slice: x: 2, y: 2, z: 4, core: 2. Of those that a mesh axis runs over, the one named last changes fastest.
Arguments:
- inputs: bfloat16 [24576, 768], P(('seq', 'blk')), may hold values from -6 to 6
- segment_ids: int32 [24576], P(('seq', 'blk')), may hold values from 0 to 1027, as said below
- qkv_weight: bfloat16 [3, 4, 192, 192], replicated, may hold values from -0.4375 to 0.4375
- out_weight: bfloat16 [768, 768], replicated, may hold values from -1.75 to 1.75
- ffn_in_weight: bfloat16 [4, 192, 768], replicated, may hold values from -0.4375 to 0.4375
- ffn_out_weight: bfloat16 [4, 768, 192], replicated, may hold values from -0.21875 to 0.21875
- attn_gain: float32 [768], replicated, may hold values from 0.25 to 1.75
- attn_shift: float32 [768], replicated, may hold values from -3 to 3
- ffn_gain: float32 [768], replicated, may hold values from 0.25 to 1.75
- ffn_shift: float32 [768], replicated, may hold values from -3 to 3
- out_cotangent: bfloat16 [24576, 768], P(('seq', 'blk')), may hold values from -6 to 6
Outputs:
- output: bfloat16 [24576, 768], P(('seq', 'blk'))
- grad_input: bfloat16 [24576, 768], P(('seq', 'blk'))
- grad_qkv_weight: float32 [3, 4, 192, 192], replicated
- grad_out_weight: float32 [768, 768], replicated
- grad_ffn_in_weight: float32 [4, 192, 768], replicated
- grad_ffn_out_weight: float32 [4, 768, 192], replicated
- grad_attn_gain: float32 [768], replicated
- grad_attn_shift: float32 [768], replicated
- grad_ffn_gain: float32 [768], replicated
- grad_ffn_shift: float32 [768], replicated
The draws below stay inside these ranges and needn't reach their ends.
Inputs may be any that keep to these rules, and one draw needn't show every extreme that they name: `segment_ids`: on the two devices of one seq index, the first k * 256 rows of both devices hold k sequences of 512 tokens, k from 1 to 2 and varying between seq indices: rows j * 256 to (j + 1) * 256 - 1 of both devices carry id j. Each device's other rows hold runs of equal ids of 1 to 128 tokens, ids over 2 that appear in no other run of the pair; every device has a run of exactly 128 tokens, and the last run of the second device of every pair carries the largest id. Ids are compared only within one seq index.
All inputs are finite; a program needn't handle non-finite values.
Results may differ from the reference program's by a relative error of at most 0.014.
Values may be sent and summed in bfloat16 or wider, within the bound.
No kernel may reach another device: no remote copies, remote signals or barrier semaphores. Data moves between devices by JAX's collectives and lax.ppermute only.
A program may use at most 192 MiB of HBM per device.

```python
import jax
import jax.numpy as jnp
from jax import lax

D = 768
HEADS = 12
HEAD_DIM = 64
FF = 3072
GROUPS = 4
TOK_DEV = 768
LONG_LEN = 512
SHORT_LEN = 128
TOKENS = 24576
N_SEQ = 16
N_BLK = 2


def draw_segment_ids(key, part):
    key = jax.random.fold_in(key, 7)
    long_half = LONG_LEN // N_BLK
    long_max = TOK_DEV // long_half - 1
    top_id = long_max + 2 * (TOK_DEV - long_half) + 1
    key_count, key_start = jax.random.split(key)
    long_count = jax.random.randint(key_count, (N_SEQ, 1, 1), 1, long_max + 1)
    position = jnp.arange(TOK_DEV, dtype=jnp.int32)[None, None, :]
    device_side = jnp.arange(N_BLK, dtype=jnp.int32)[None, :, None]
    short_pos = position - long_count * long_half
    extra_start = jax.random.randint(key_start, (N_SEQ, N_BLK, TOK_DEV), 0, 64) == 0
    starts = (short_pos % SHORT_LEN == 0) | extra_start & (short_pos >= SHORT_LEN)
    starts = starts & (short_pos >= 0)
    running = jnp.cumsum(starts.astype(jnp.int32), axis=2)
    run_total = running[:, :, -1:]
    short_ids = top_id - 2 * (run_total - running) - (N_BLK - 1 - device_side)
    long_ids = jnp.broadcast_to(position // long_half, short_ids.shape)
    segment = jnp.where(short_pos < 0, long_ids, short_ids)
    return segment.reshape(N_SEQ * N_BLK * TOK_DEV).astype(jnp.int32)


def shard_levels(own_key, shape, shards, smallest, high):
    factor_of = 1.0
    for axis_at, shards_of in shards:
        draws = jax.random.uniform(jax.random.fold_in(jax.random.fold_in(own_key, 6), axis_at), (shards_of,), jnp.float32, smallest / len(shards), high / len(shards))
        factor_of = factor_of * jnp.repeat(jnp.exp(draws), shape[axis_at] // shards_of).reshape((-1,) + (1,) * (len(shape) - 1 - axis_at))
    return factor_of


def centred(rng, shape, scale, most, cuts=(), kind=jnp.bfloat16):
    level = shard_levels(rng, shape, cuts, -0.22, 0.18) if cuts else 1.0
    values = jax.random.normal(rng, shape, jnp.float32) * scale * level
    return jnp.minimum(jnp.maximum(values, -most), most).astype(kind)


def setup_inputs(seed: int = 0) -> dict:
    keys = jax.random.split(jax.random.key(seed), 12)
    return {
        "inputs": centred(keys[0], (TOKENS, D), 1.0, 6.0, ((0, 32),)),
        "segment_ids": draw_segment_ids(jax.random.fold_in(keys[11], 71), 0),
        "qkv_weight": centred(keys[2], (3, GROUPS, D // GROUPS, D // GROUPS), (D // GROUPS) ** -0.5, 0.4375),
        "out_weight": centred(keys[3], (D, D), (D // 64) ** -0.5, 1.75),
        "ffn_in_weight": centred(keys[4], (GROUPS, D // GROUPS, FF // GROUPS), (D // GROUPS) ** -0.5, 0.4375),
        "ffn_out_weight": centred(keys[5], (GROUPS, FF // GROUPS, D // GROUPS), (FF // GROUPS) ** -0.5, 0.21875),
        "attn_gain": jnp.clip(1.0 + 0.15 * jax.random.normal(keys[6], (D,), jnp.float32), 0.25, 1.75),
        "attn_shift": centred(keys[7], (D,), 0.3, 3.0, (), jnp.float32),
        "ffn_gain": jnp.clip(1.0 + 0.15 * jax.random.normal(keys[8], (D,), jnp.float32), 0.25, 1.75),
        "ffn_shift": centred(keys[9], (D,), 0.3, 3.0, (), jnp.float32),
        "out_cotangent": centred(keys[10], (TOKENS, D), 1.0, 6.0, ((0, 32),)),
    }


EPSILON = 1e-05
HIGHEST = lax.Precision.HIGHEST

@jax.custom_vjp
def low(v):
    return lax.optimization_barrier(v.astype(jnp.bfloat16)).astype(jnp.float32)

@jax.custom_vjp
def low_back(v):
    return v

def low_keep(v):
    return (low(v), None)

def low_pass(kept, grad):
    return (grad,)

def back_keep(v):
    return (v, None)

def back_low(kept, grad):
    return (low(grad),)
low.defvjp(low_keep, low_pass)
low_back.defvjp(back_keep, back_low)

def rounded_both(values):
    return low_back(low(values))

def layer_norm(residual, norm_gain, norm_shift):
    centre = residual - lax.optimization_barrier(jnp.mean(residual, -1, keepdims=True))
    spread = lax.optimization_barrier(jnp.mean(centre * centre, -1, keepdims=True))
    return centre * lax.rsqrt(spread + EPSILON) * norm_gain + norm_shift

def grouped(values, weight):
    row_count = values.shape[0]
    split_rows = values.reshape(row_count, weight.shape[0], weight.shape[1])
    return jnp.einsum('ngi,gio->ngo', split_rows, weight, precision=HIGHEST).reshape(row_count, -1)

def group_layer(parameters, token_rows, group_ids):
    qkv_weight, out_weight, ffn_in_weight, ffn_out_weight, attn_gain, attn_shift, ffn_gain, ffn_shift = parameters
    row_count = token_rows.shape[0]
    query_heads = rounded_both(grouped(token_rows, qkv_weight[0])).reshape(row_count, HEADS, HEAD_DIM)
    key_heads = rounded_both(grouped(token_rows, qkv_weight[1])).reshape(row_count, HEADS, HEAD_DIM)
    value_heads = rounded_both(grouped(token_rows, qkv_weight[2])).reshape(row_count, HEADS, HEAD_DIM)
    raw_scores = jnp.einsum('qhe,khe->hqk', query_heads, key_heads, precision=HIGHEST) * HEAD_DIM ** (-0.5)
    allowed = group_ids[:, None] == group_ids[None, :]
    scores = jnp.where(allowed[None], low_back(raw_scores), -1e+30)
    log_total = jax.nn.logsumexp(scores, -1, keepdims=True)
    softmax = low(jnp.exp(scores - log_total))
    context = jnp.einsum('hqk,khe->qhe', softmax, value_heads, precision=HIGHEST).reshape(row_count, D)
    context = rounded_both(context)
    attended = low_back(jnp.dot(context, out_weight, precision=HIGHEST))
    hidden = layer_norm(token_rows + attended, attn_gain, attn_shift)
    upward = low_back(grouped(low(hidden), ffn_in_weight))
    activated = low(jax.nn.gelu(upward, approximate=False))
    feed_out = low_back(grouped(activated, ffn_out_weight))
    return layer_norm(hidden + feed_out, ffn_gain, ffn_shift)

def reference(inputs, segment_ids, qkv_weight, out_weight, ffn_in_weight, ffn_out_weight, attn_gain, attn_shift, ffn_gain, ffn_shift, out_cotangent):
    group_rows = N_BLK * TOK_DEV
    token_rows = inputs.astype(jnp.float32).reshape(N_SEQ, group_rows, D)
    group_ids = segment_ids.reshape(N_SEQ, group_rows)
    parameters = tuple((weight.astype(jnp.float32) for weight in (qkv_weight, out_weight, ffn_in_weight, ffn_out_weight, attn_gain, attn_shift, ffn_gain, ffn_shift)))
    checked = jax.checkpoint(group_layer)

    def forward(params_in, rows_in):

        def one_group(pair_rows):
            return checked(params_in, pair_rows[0], pair_rows[1])
        return lax.map(one_group, (rows_in, group_ids))
    result, pullback = jax.vjp(forward, parameters, token_rows)
    grad_params, grad_rows = pullback(out_cotangent.astype(jnp.float32).reshape(result.shape))
    output = result.reshape(TOKENS, D).astype(jnp.bfloat16)
    grad_input = grad_rows.reshape(TOKENS, D).astype(jnp.bfloat16)
    return (output, grad_input, grad_params[0], grad_params[1], grad_params[2], grad_params[3], grad_params[4], grad_params[5], grad_params[6], grad_params[7])
```

```python
from functools import partial

import jax
import jax.numpy as jnp
from jax import lax
from jax.experimental import pallas as pl
from jax.experimental.pallas import tpu as pltpu
from jax.sharding import Mesh, PartitionSpec as P

F32 = jnp.float32
BF16 = jnp.bfloat16
EPSILON = 1e-05
HEADS = 12
HEAD_DIM = 64
D = 768
GROUPS = 4
GD = D // GROUPS
FF = 3072
GF = FF // GROUPS
TOK = 768
BLK = 256
EXT = 512
ALL = TOK + EXT
UNITS = 16
CHUNK = (144, 384)
QCHUNK = (24, 640)
VMEM_LIMIT = 61 * 1024 * 1024


def nn(a, b):
    return lax.dot_general(a, b, (((1,), (0,)), ((), ())), preferred_element_type=F32)


def nt(a, b):
    return lax.dot_general(a, b, (((1,), (1,)), ((), ())), preferred_element_type=F32)


def tn(a, b):
    return lax.dot_general(a, b, (((0,), (0,)), ((), ())), preferred_element_type=F32)


def gelu_parts(u):
    a = jnp.abs(u) * 0.7071067811865476
    t = 1.0 / (1.0 + 0.3275911 * a)
    e = jnp.exp(-0.5 * (u * u))
    poly = t * (
        0.254829592
        + t * (-0.284496736 + t * (1.421413741 + t * (-1.453152027 + t * 1.061405429)))
    )
    tail = 0.5 * poly * e
    phi = jnp.where(u < 0, tail, 1.0 - tail)
    return u * phi, phi + u * (e * 0.3989422804014327)


def layer_kernel(
    code_ref, x_ref, xp_ref, segr_ref, segc_ref, wqkv_ref, wo_ref, w1_ref, w2t_ref, norm_ref, cot_ref,
    out_ref, xt_ref, q_ref, k_ref, v_ref, gctx_ref, lse_ref, gfirst_ref, keep_ref, send_ref, gvec_ref,
    bias, wot, w1t, w2, ctx, hid, act, gup, gpr, gfeed, gatt, nb, gacc,
):
    core, low, far = code_ref[0], code_ref[1], code_ref[3]
    two = code_ref[2]
    xt_ref[:, :TOK] = x_ref[...].T
    xt_ref[:, TOK:] = xp_ref[...].T
    for j in range(4):
        nb[j] = jnp.broadcast_to(norm_ref[:, j : j + 1], (D, 128))
    wot[...] = wo_ref[...].T
    for g in range(GROUPS):
        w1t[g] = w1_ref[g].T
        w2[g] = w2t_ref[g].T
        rows = slice(g * GD, (g + 1) * GD)
        xg = xt_ref[rows, :]
        q_ref[rows, :] = (tn(wqkv_ref[0, g], xg[:, :TOK]).astype(BF16).astype(F32) * 0.125).astype(BF16)
        k_ref[rows, :] = tn(wqkv_ref[1, g], xg).astype(BF16)
        v_ref[rows, :] = tn(wqkv_ref[2, g], xg).astype(BF16)

    off = jnp.where(two == 1, 2 * BLK + BLK + BLK, 2 * BLK)
    segr = segr_ref[...]
    segc = segc_ref[...]

    def same(kb, qb):
        a = segc[kb * BLK : (kb + 1) * BLK]
        b = segr[:, qb * BLK : (qb + 1) * BLK]
        return jnp.where(a == b, 0.0, -1e30).astype(F32)

    bias[0, :BLK] = same(1, 1)
    bias[0, BLK:] = jnp.where(two == 1, 0.0, same(2, 1))
    bias[1, :BLK] = same(2, 2)
    bias[1, BLK:] = same(1, 2)

    def head(h, carry):
        hr = pl.ds(pl.multiple_of(h * HEAD_DIM, HEAD_DIM), HEAD_DIM)
        for b in range(3):
            if b == 0:
                ec = slice(TOK, TOK + BLK)
            elif b == 1:
                ec = pl.ds(pl.multiple_of(off, BLK), BLK)
            else:
                ec = slice(BLK, 2 * BLK)
            qc = slice(b * BLK, (b + 1) * BLK)
            kt = jnp.concatenate([k_ref[hr, qc], k_ref[hr, ec]], 1)
            vt = jnp.concatenate([v_ref[hr, qc], v_ref[hr, ec]], 1)
            s = tn(kt, q_ref[hr, qc])
            if b:
                s = s + bias[b - 1]
            top = jnp.max(s, 0, keepdims=True)
            p = jnp.exp(s - top)
            total = jnp.sum(p, 0, keepdims=True)
            c = nn(vt, p.astype(BF16))
            ctx[hr, qc] = (c * (1.0 / total)).astype(BF16)
            lse_ref[h, :, qc] = top + jnp.log(total)
        return carry

    lax.fori_loop(0, HEADS, head, 0)

    gacc[...] = jnp.zeros_like(gacc)

    def wide(j):
        return jnp.concatenate([nb[j], nb[j]], 1)

    def tile(t, carry):
        tc = pl.ds(pl.multiple_of(t * BLK, BLK), BLK)
        r = xt_ref[:, tc].astype(F32) + nn(wot[...], ctx[:, tc])
        centre = r - jnp.mean(r, 0, keepdims=True)
        inv1 = lax.rsqrt(jnp.mean(centre * centre, 0, keepdims=True) + EPSILON)
        n1 = centre * inv1
        hidden = n1 * wide(0) + wide(1)
        hid[:, tc] = hidden.astype(BF16)
        feeds = []
        for g in range(GROUPS):
            hg = hid[g * GD : (g + 1) * GD, tc]
            for j in range(GF // BLK):
                fr = slice(j * BLK, (j + 1) * BLK)
                a, d = gelu_parts(nn(w1t[g, fr], hg))
                act[g, fr, tc] = a.astype(BF16)
                gpr[g, fr] = d
            feeds.append(nn(w2t_ref[g], act[g, :, tc]))
        r2 = hidden + jnp.concatenate(feeds, 0)
        centre2 = r2 - jnp.mean(r2, 0, keepdims=True)
        inv2 = lax.rsqrt(jnp.mean(centre2 * centre2, 0, keepdims=True) + EPSILON)
        n2 = centre2 * inv2
        out_ref[tc, :] = (n2 * wide(2) + wide(3)).astype(BF16).T
        c = cot_ref[tc, :].T.astype(F32)
        cn = c * n2
        gacc[2] += cn[:, :128] + cn[:, 128:]
        gacc[3] += c[:, :128] + c[:, 128:]
        cg = c * wide(2)
        gsec = inv2 * (
            cg - jnp.mean(cg, 0, keepdims=True) - n2 * jnp.mean(cg * n2, 0, keepdims=True)
        )
        gfeed[:, tc] = gsec.astype(BF16)
        gh = []
        for g in range(GROUPS):
            fg = gfeed[g * GD : (g + 1) * GD, tc]
            for j in range(GF // BLK):
                fr = slice(j * BLK, (j + 1) * BLK)
                gup[g, fr, tc] = (nn(w2[g, fr], fg) * gpr[g, fr]).astype(BF16)
            gh.append(nn(w1_ref[g], gup[g, :, tc]))
        ghid = gsec + jnp.concatenate(gh, 0)
        gn = ghid * n1
        gacc[0] += gn[:, :128] + gn[:, 128:]
        gacc[1] += ghid[:, :128] + ghid[:, 128:]
        sc = ghid * wide(0)
        gfirst = inv1 * (
            sc - jnp.mean(sc, 0, keepdims=True) - n1 * jnp.mean(sc * n1, 0, keepdims=True)
        )
        gfirst_ref[:, tc] = gfirst
        gatt[:, tc] = gfirst.astype(BF16)
        gctx_ref[:, tc] = nn(wo_ref[...], gatt[:, tc]).astype(BF16)
        return carry

    lax.fori_loop(0, TOK // BLK, tile, 0)
    for j in range(4):
        gvec_ref[:, j : j + 1] = jnp.sum(gacc[j], 1, keepdims=True)

    for jj in range(GROUPS):
        g = jj ^ (2 * core)
        gr = pl.ds(pl.multiple_of(g * GD, GD), GD)
        parts = (
            nt(hid[gr, :], gup[g]),
            nt(gfeed[gr, :], act[g]),
            nt(ctx[gr, :], gatt[...]),
        )
        for i, part in enumerate(parts):
            for r in range(4):
                for lh in range(2):
                    piece = part[48 * r : 48 * (r + 1), 384 * lh : 384 * (lh + 1)]
                    pos = ((g & 1) * 8 + r * 2 + lh) ^ (low if jj < 2 else far)
                    if jj < 2:
                        keep_ref[pos, 48 * i : 48 * (i + 1)] = piece
                    else:
                        send_ref[pos, 48 * i : 48 * (i + 1)] = piece.astype(BF16)


def back_kernel(
    code_ref, q_ref, k_ref, v_ref, gctx_ref, lse_ref, segr_ref, segc_ref,
    dq_ref, dk_ref, dv_ref, dkp_ref, dvp_ref, bias, dk, dv,
):
    two = code_ref[2]
    off = jnp.where(two == 1, 2 * BLK + BLK + BLK, 2 * BLK)
    segr = segr_ref[...]
    segc = segc_ref[...]

    def same(kb, qb):
        a = segc[kb * BLK : (kb + 1) * BLK]
        b = segr[:, qb * BLK : (qb + 1) * BLK]
        return jnp.where(a == b, 0.0, -1e30).astype(F32)

    bias[0, :BLK] = same(1, 1)
    bias[0, BLK:] = jnp.where(two == 1, 0.0, same(2, 1))
    bias[1, :BLK] = same(2, 2)
    bias[1, BLK:] = same(1, 2)
    dk[...] = jnp.zeros_like(dk)
    dv[...] = jnp.zeros_like(dv)

    def head(h, carry):
        hr = pl.ds(pl.multiple_of(h * HEAD_DIM, HEAD_DIM), HEAD_DIM)
        for b in range(3):
            if b == 0:
                ec = slice(TOK, TOK + BLK)
            elif b == 1:
                ec = pl.ds(pl.multiple_of(off, BLK), BLK)
            else:
                ec = slice(BLK, 2 * BLK)
            qc = slice(b * BLK, (b + 1) * BLK)
            kt = jnp.concatenate([k_ref[hr, qc], k_ref[hr, ec]], 1)
            vt = jnp.concatenate([v_ref[hr, qc], v_ref[hr, ec]], 1)
            qt = q_ref[hr, qc]
            gt = gctx_ref[hr, qc]
            s = tn(kt, qt)
            if b:
                s = s + bias[b - 1]
            p = jnp.exp(s - lse_ref[h, :, qc])
            dp = tn(vt, gt)
            dots = jnp.sum(p * dp, 0, keepdims=True)
            ds = (p * (dp - dots)).astype(BF16)
            dq_ref[hr, qc] = (nn(kt, ds) * 0.125).astype(BF16)
            gk = nt(qt, ds)
            gv = nt(gt, p.astype(BF16))
            dk[hr, qc] += gk[:, :BLK]
            dk[hr, ec] += gk[:, BLK:]
            dv[hr, qc] += gv[:, :BLK]
            dv[hr, ec] += gv[:, BLK:]
        return carry

    lax.fori_loop(0, HEADS, head, 0)
    dk_ref[...] = dk[:, :TOK]
    dv_ref[...] = dv[:, :TOK]
    dkp_ref[...] = dk[:, TOK:].astype(BF16)
    dvp_ref[...] = dv[:, TOK:].astype(BF16)


def final_kernel(
    code_ref, xt_ref, dq_ref, dk_ref, dv_ref, rk_ref, rv_ref, wqkv_ref, gfirst_ref, gvec_ref,
    gin_ref, keep_ref, send_ref, gk, gv,
):
    core, low, far = code_ref[0], code_ref[1], code_ref[3]
    gk[:, :EXT] = (dk_ref[:, :EXT] + rk_ref[...].astype(F32)).astype(BF16)
    gk[:, EXT:] = dk_ref[:, EXT:].astype(BF16)
    gv[:, :EXT] = (dv_ref[:, :EXT] + rv_ref[...].astype(F32)).astype(BF16)
    gv[:, EXT:] = dv_ref[:, EXT:].astype(BF16)
    for g in range(GROUPS):
        gr = slice(g * GD, (g + 1) * GD)
        through = (
            nn(wqkv_ref[0, g], dq_ref[gr, :]) + nn(wqkv_ref[1, g], gk[gr, :]) + nn(wqkv_ref[2, g], gv[gr, :])
        )
        gin_ref[:, gr] = (gfirst_ref[gr, :] + through).astype(BF16).T
    for jj in range(GROUPS):
        g = jj ^ (2 * core)
        gr = pl.ds(pl.multiple_of(g * GD, GD), GD)
        xg = xt_ref[gr, :]
        parts = [nt(xg, dq_ref[gr, :]), nt(xg, gk[gr, :]), nt(xg, gv[gr, :])]
        pad = jnp.zeros((GD, QCHUNK[1] - 3 * GD - 4), F32)
        row = jnp.concatenate(parts + [gvec_ref[gr, :], pad], 1)
        for r in range(8):
            piece = row[24 * r : 24 * (r + 1)]
            pos = ((g & 1) * 8 + r) ^ (low if jj < 2 else far)
            if jj < 2:
                keep_ref[pos] = piece
            else:
                send_ref[pos] = piece.astype(BF16)


def finish_kernel(code_ref, m_ref, q_ref, g1_ref, g2_ref, go_ref, gq_ref, gvec_ref):
    core, low, far = code_ref[0], code_ref[1], code_ref[3]
    for half in range(2):
        base = half ^ core
        low_of = far if half else low
        for a in range(16):
            part = m_ref[half * 16 + (a ^ low_of)].astype(F32)
            g = base * 2 + a // 8
            rows = slice(48 * (a % 8 // 2), 48 * (a % 8 // 2 + 1))
            lanes = slice(384 * (a % 2), 384 * (a % 2 + 1))
            g1_ref[g, rows, lanes] = part[:48]
            g2_ref[g, rows, lanes] = part[48:96]
            go_ref[g, rows, lanes] = part[96:]
        for a in range(16):
            part = q_ref[half * 16 + (a ^ low_of)].astype(F32)
            g = base * 2 + a // 8
            rows = slice(24 * (a % 8), 24 * (a % 8 + 1))
            for t in range(3):
                gq_ref[t, g, rows] = part[:, t * GD : (t + 1) * GD]
            gvec_ref[g, rows] = part[:, 3 * GD : 3 * GD + 4]


def call(kernel, outs, scratch, *args, flops=0, name=None):
    smem = pl.BlockSpec(memory_space=pltpu.SMEM)
    vmem = pl.BlockSpec(memory_space=pltpu.VMEM)
    return pl.pallas_call(
        kernel,
        out_shape=[jax.ShapeDtypeStruct(s, d) for s, d in outs],
        in_specs=[smem] + [vmem] * (len(args) - 1),
        out_specs=[vmem] * len(outs),
        scratch_shapes=[pltpu.VMEM(s, d) for s, d in scratch],
        compiler_params=pltpu.CompilerParams(vmem_limit_bytes=VMEM_LIMIT),
        name=name,
    )(*args)


class Links:
    def __init__(self, n_seq):
        bits = max(n_seq.bit_length() - 1, 0)
        self.n = n_seq * 2
        orders = [list(range(bits)), [1, 0] + list(range(2, bits))] if bits > 1 else [list(range(bits))] * 2
        self.orders = orders
        self.halving = min(4, bits)
        self.bits = bits

    def pairs(self, step):
        if step < 0:
            return [(i, i ^ 1) for i in range(self.n)]
        return [(i, i ^ (2 << self.orders[i & 1][step])) for i in range(self.n)]

    def code(self, seq, core):
        def of(order):
            value = 0
            for step in range(4):
                value = value * 2 + (((seq >> order[step]) & 1) if step < self.halving else 0)
            return value

        return jnp.where(core == 0, of(self.orders[0]), of(self.orders[1]))


def swap(x, links, step):
    return lax.ppermute(x, "dev", links.pairs(step))


def all_sum(keep, send, links):
    total = keep + swap(send, links, -1).astype(F32)
    for step in range(links.halving):
        half = total.shape[0] // 2
        total = total[:half] + swap(total[half:].astype(BF16), links, step).astype(F32)
    piece = total.astype(BF16)
    for step in range(links.halving, links.bits):
        piece = (piece.astype(F32) + swap(piece, links, step).astype(F32)).astype(BF16)
    for step in reversed(range(-1, links.halving)):
        piece = jnp.concatenate([piece, swap(piece, links, step)], 0)
    return piece


def per_device(
    links, inputs, segment_ids, qkv_weight, out_weight, ffn_in_weight, ffn_out_weight,
    attn_gain, attn_shift, ffn_gain, ffn_shift, out_cotangent,
):
    me = lax.axis_index("dev")
    seq, core = me >> 1, me & 1
    code = jnp.stack([core, links.code(seq, core), (segment_ids[BLK] == 1).astype(jnp.int32), links.code(seq, 1 - core)]).astype(jnp.int32)
    partner = swap(inputs[:EXT], links, -1)
    segr = segment_ids[None, :]
    segc = segment_ids[:, None]
    norms = jnp.stack((attn_gain, attn_shift, ffn_gain, ffn_shift), 1)
    (output, xt, q, k, v, gctx, lse, gfirst, keep, send, gvec) = call(
        layer_kernel,
        [
            ((TOK, D), BF16), ((D, ALL), BF16), ((D, TOK), BF16), ((D, ALL), BF16), ((D, ALL), BF16),
            ((D, TOK), BF16), ((HEADS, 1, TOK), F32), ((D, TOK), F32),
            ((16,) + CHUNK, F32), ((16,) + CHUNK, BF16), ((D, 4), F32),
        ],
        [
            ((2, 2 * BLK, BLK), F32), ((D, D), BF16), ((GROUPS, GF, GD), BF16), ((GROUPS, GF, GD), BF16),
            ((D, TOK), BF16), ((D, TOK), BF16), ((GROUPS, GF, TOK), BF16), ((GROUPS, GF, TOK), BF16),
            ((GROUPS, GF, BLK), F32), ((D, TOK), BF16), ((D, TOK), BF16), ((4, D, 128), F32), ((4, D, 128), F32),
        ],
        code, inputs, partner, segr, segc, qkv_weight, out_weight, ffn_in_weight, jnp.swapaxes(ffn_out_weight, 1, 2), norms, out_cotangent,
        name="layer",
    )
    dq, dk, dv, dkp, dvp = call(
        back_kernel,
        [((D, TOK), BF16), ((D, TOK), F32), ((D, TOK), F32), ((D, EXT), BF16), ((D, EXT), BF16)],
        [((2, 2 * BLK, BLK), F32), ((D, ALL), F32), ((D, ALL), F32)],
        code, q, k, v, gctx, lse, segr, segc,
        name="attention_back",
    )
    rk = swap(dkp, links, -1)
    rv = swap(dvp, links, -1)
    two = code[2] == 1
    rk = jnp.where(two | (jnp.arange(EXT) < BLK)[None, :], rk, 0)
    rv = jnp.where(two | (jnp.arange(EXT) < BLK)[None, :], rv, 0)
    grad_input, keep_q, send_q = call(
        final_kernel,
        [((TOK, D), BF16), ((16,) + QCHUNK, F32), ((16,) + QCHUNK, BF16)],
        [((D, TOK), BF16), ((D, TOK), BF16)],
        code, xt[:, :TOK], dq, dk, dv, rk, rv, qkv_weight, gfirst, gvec,
        name="through_qkv",
    )
    m = all_sum(keep, send, links)
    mq = all_sum(keep_q, send_q, links)
    g1, g2, go, gq, gv = call(
        finish_kernel,
        [((GROUPS, GD, GF), F32), ((GROUPS, GD, GF), F32), ((GROUPS, GD, D), F32), ((3, GROUPS, GD, GD), F32), ((GROUPS, GD, 4), F32)],
        [],
        code, m, mq,
        name="finish",
    )
    gv = gv.reshape(D, 4)
    return (output, grad_input, gq, go.reshape(D, D), g1, jnp.swapaxes(g2, 1, 2), gv[:, 0], gv[:, 1], gv[:, 2], gv[:, 3])


def solution(mesh):
    flat = Mesh(mesh.devices.reshape(-1), ("dev",))
    links = Links(mesh.shape["seq"])
    split, copied = P("dev"), P()
    return jax.shard_map(
        partial(per_device, links),
        mesh=flat,
        in_specs=(split, split) + (copied,) * 8 + (split,),
        out_specs=(split, split) + (copied,) * 8,
        check_vma=False,
    )
```

```python
from functools import partial

import jax
import jax.numpy as jnp
from jax import lax
from jax.experimental import pallas as pl
from jax.experimental.pallas import tpu as pltpu
from jax.sharding import Mesh, PartitionSpec as P

F32 = jnp.float32
BF16 = jnp.bfloat16
EPSILON = 1e-05
HEADS = 12
HEAD_DIM = 64
D = 768
GROUPS = 4
GD = D // GROUPS
FF = 3072
GF = FF // GROUPS
TOK = 768
BLK = 256
EXT = 512
QCHUNK = (24, 640)
HALF = D // 2


def nn(a, b):
    return lax.dot_general(a, b, (((1,), (0,)), ((), ())), preferred_element_type=F32)


def nt(a, b):
    return lax.dot_general(a, b, (((1,), (1,)), ((), ())), preferred_element_type=F32)


def tn(a, b):
    return lax.dot_general(a, b, (((0,), (0,)), ((), ())), preferred_element_type=F32)


def gelu_parts(u):
    a = jnp.abs(u) * 0.7071067811865476
    t = 1.0 / (1.0 + 0.3275911 * a)
    e = jnp.exp(-0.5 * (u * u))
    poly = t * (
        0.254829592
        + t * (-0.284496736 + t * (1.421413741 + t * (-1.453152027 + t * 1.061405429)))
    )
    tail = 0.5 * poly * e
    phi = jnp.where(u < 0, tail, 1.0 - tail)
    return u * phi, phi + u * (e * 0.3989422804014327)


def pipelined(items, first, second, third, lag, last):
    n = len(items)
    for t in range(n + last):
        if t < n:
            first(items[t])
        if 0 <= t - lag < n:
            second(items[t - lag])
        if 0 <= t - last < n:
            third(items[t - last])


def project_kernel(
    seg_ref, x_ref, ids_ref, wqkv_ref,
    xt_ref, q_ref, k_ref, v_ref, bias_ref,
):
    two = seg_ref[BLK] == 1
    xt_ref[...] = x_ref[...].T
    for g in range(GROUPS):
        rows = slice(g * GD, (g + 1) * GD)
        xg = xt_ref[rows, :]
        q_ref[rows, :] = (tn(wqkv_ref[0, g], xg).astype(BF16).astype(F32) * 0.125).astype(BF16)
        k_ref[rows, :] = tn(wqkv_ref[1, g], xg).astype(BF16)
        v_ref[rows, :] = tn(wqkv_ref[2, g], xg).astype(BF16)
    row = ids_ref[...].reshape(1, TOK)

    def lanes(b):
        return jnp.broadcast_to(row[:, b * BLK : (b + 1) * BLK], (BLK, BLK))

    def same(kb, qb):
        return jnp.where(lanes(kb).T == lanes(qb), 0.0, -1e30).astype(BF16)

    bias_ref[0, :BLK] = same(1, 1)
    bias_ref[0, BLK:] = jnp.where(two, jnp.zeros((BLK, BLK), BF16), same(2, 1))
    bias_ref[1, :BLK] = same(2, 2)
    bias_ref[1, BLK:] = same(1, 2)


def pick(ref, far_ref, hr, b, two):
    if b == 0:
        other = far_ref[hr, :BLK]
    elif b == 1:
        other = jnp.where(two, far_ref[hr, BLK:], ref[hr, 2 * BLK :])
    else:
        other = ref[hr, BLK : 2 * BLK]
    return jnp.concatenate([ref[hr, b * BLK : (b + 1) * BLK], other], 1)


def attend_kernel(
    seg_ref, xp_ref, wqkv_ref, q_ref, k_ref, v_ref, bias_ref,
    kp_ref, vp_ref, ctx_ref, lse_ref,
):
    two = seg_ref[BLK] == 1
    xpt = xp_ref[:EXT, :].T
    for g in range(GROUPS):
        rows = slice(g * GD, (g + 1) * GD)
        kp_ref[rows, :] = tn(wqkv_ref[1, g], xpt[rows]).astype(BF16)
        vp_ref[rows, :] = tn(wqkv_ref[2, g], xpt[rows]).astype(BF16)

    def heads(i, carry):
        items = []
        for u in range(4):
            h = i * 4 + u
            hr = pl.ds(pl.multiple_of(h * HEAD_DIM, HEAD_DIM), HEAD_DIM)
            items += [{"h": h, "hr": hr, "b": b, "qc": slice(b * BLK, (b + 1) * BLK)} for b in range(3)]

        def scores(d):
            s = tn(pick(k_ref, kp_ref, d["hr"], d["b"], two), q_ref[d["hr"], d["qc"]])
            if d["b"]:
                s = s + bias_ref[d["b"] - 1].astype(F32)
            d["s"] = s

        def weights(d):
            s = d.pop("s")
            d["top"] = jnp.max(s, 0, keepdims=True)
            p = jnp.exp(s - d["top"])
            d["total"] = jnp.sum(p, 0, keepdims=True)
            d["p"] = p.astype(BF16)

        def mix(d):
            c = nn(pick(v_ref, vp_ref, d["hr"], d["b"], two), d.pop("p"))
            ctx_ref[d["hr"], d["qc"]] = (c * (1.0 / d["total"])).astype(BF16)
            lse_ref[d["h"], :, d["qc"]] = d["top"] + jnp.log(d["total"])

        pipelined(items, scores, weights, mix, 2, 3)
        return carry

    lax.fori_loop(0, HEADS // 4, heads, 0)


PARTS = [(g, slice(j * BLK, (j + 1) * BLK)) for g in range(GROUPS) for j in range(GF // BLK)]


def columns(ref):
    wide = jnp.broadcast_to(ref[...].reshape(1, D), (128, D)).T
    return jnp.concatenate([wide, wide], 1)


def halves(x):
    return x[:, :128] + x[:, 128:]


def scatter(part, jj, g, keep_ref, send_ref, at, low, far):
    for r in range(4):
        for lh in range(2):
            piece = part[48 * r : 48 * (r + 1), 384 * lh : 384 * (lh + 1)].astype(BF16)
            pos = ((g & 1) * 8 + r * 2 + lh) ^ (low if jj < 2 else far)
            ref = keep_ref if jj < 2 else send_ref
            ref[pos, at : at + 48] = piece


def forward_kernel(
    code_ref, xt_ref, ctx_ref, wo_ref, w1_ref, w2t_ref, cot_ref, ag_ref, as_ref, fg_ref, fs_ref,
    out_ref, hid_ref, n1_ref, inv1_ref, gpr_ref, gsec_ref, gfeed_ref, keep_ref, send_ref, gvec_ref,
    wot, w1t, act, nb, gacc,
):
    core, low, far = code_ref[0], code_ref[1], code_ref[2]
    for j, ref in enumerate((ag_ref, as_ref, fg_ref, fs_ref)):
        nb[j] = columns(ref)
    wot[...] = wo_ref[...].T
    for g in range(GROUPS):
        w1t[g] = w1_ref[g].T
    gacc[...] = jnp.zeros_like(gacc)

    def tile(t, carry):
        tc = pl.ds(pl.multiple_of(t * BLK, BLK), BLK)
        r = xt_ref[:, tc].astype(F32) + nn(wot[...], ctx_ref[:, tc])
        centre = r - jnp.mean(r, 0, keepdims=True)
        inv1 = lax.rsqrt(jnp.mean(centre * centre, 0, keepdims=True) + EPSILON)
        n1 = centre * inv1
        n1_ref[:, tc] = n1
        inv1_ref[:, tc] = inv1
        hidden = n1 * nb[0] + nb[1]
        hid_ref[:, tc] = hidden.astype(BF16)
        up, feeds = {}, []

        def rise(p):
            g, fr = p
            up[g, fr.start] = nn(w1t[g, fr], hid_ref[g * GD : (g + 1) * GD, tc])

        def bend(p):
            g, fr = p
            a, d = gelu_parts(up.pop((g, fr.start)))
            act[g, fr, tc] = a.astype(BF16)
            gpr_ref[g, fr, tc] = d.astype(BF16)

        def fall(p):
            if p[1].stop == GF:
                feeds.append(nn(w2t_ref[p[0]], act[p[0], :, tc]))

        pipelined(PARTS, rise, bend, fall, 2, 3)
        r2 = hidden + jnp.concatenate(feeds, 0)
        centre2 = r2 - jnp.mean(r2, 0, keepdims=True)
        inv2 = lax.rsqrt(jnp.mean(centre2 * centre2, 0, keepdims=True) + EPSILON)
        n2 = centre2 * inv2
        out_ref[tc, :] = (n2 * nb[2] + nb[3]).astype(BF16).T
        c = cot_ref[tc, :].T.astype(F32)
        gacc[0] += halves(c * n2)
        gacc[1] += halves(c)
        cg = c * nb[2]
        gsec = inv2 * (
            cg - jnp.mean(cg, 0, keepdims=True) - n2 * jnp.mean(cg * n2, 0, keepdims=True)
        )
        gsec_ref[:, tc] = gsec
        gfeed_ref[:, tc] = gsec.astype(BF16)
        return carry

    lax.fori_loop(0, TOK // BLK, tile, 0)
    for j in range(2):
        gvec_ref[:, j : j + 1] = jnp.sum(gacc[j], 1, keepdims=True)
    for jj in (2, 3, 0, 1):
        g = jj ^ (2 * core)
        gr = pl.ds(pl.multiple_of(g * GD, GD), GD)
        scatter(nt(gfeed_ref[gr, :], act[g]), jj, g, keep_ref, send_ref, 0, low, far)


def backward_kernel(
    code_ref, ctx_ref, wo_ref, w1_ref, w2t_ref, hid_ref, n1_ref, inv1_ref, gpr_ref, gsec_ref, gfeed_ref, ag_ref,
    gctx_ref, gfirst_ref, keep_ref, send_ref, gvec_ref,
    w2, gup, gatt, nb, gacc,
):
    core, low, far = code_ref[0], code_ref[1], code_ref[2]
    nb[...] = columns(ag_ref)
    for g in range(GROUPS):
        w2[g] = w2t_ref[g].T
    gacc[...] = jnp.zeros_like(gacc)

    def tile(t, carry):
        tc = pl.ds(pl.multiple_of(t * BLK, BLK), BLK)
        back, gh = {}, []

        def lift(p):
            g, fr = p
            back[g, fr.start] = nn(w2[g, fr], gfeed_ref[g * GD : (g + 1) * GD, tc])

        def scale(p):
            g, fr = p
            gup[g, fr, tc] = (back.pop((g, fr.start)) * gpr_ref[g, fr, tc].astype(F32)).astype(BF16)

        def drop(p):
            if p[1].stop == GF:
                gh.append(nn(w1_ref[p[0]], gup[p[0], :, tc]))

        pipelined(PARTS, lift, scale, drop, 2, 3)
        ghid = gsec_ref[:, tc] + jnp.concatenate(gh, 0)
        n1 = n1_ref[:, tc]
        gacc[0] += halves(ghid * n1)
        gacc[1] += halves(ghid)
        sc = ghid * nb[...]
        gfirst = inv1_ref[:, tc] * (
            sc - jnp.mean(sc, 0, keepdims=True) - n1 * jnp.mean(sc * n1, 0, keepdims=True)
        )
        gfirst_ref[:, tc] = gfirst
        gatt[:, tc] = gfirst.astype(BF16)
        gctx_ref[:, tc] = nn(wo_ref[...], gatt[:, tc]).astype(BF16)
        return carry

    lax.fori_loop(0, TOK // BLK, tile, 0)
    for j in range(2):
        gvec_ref[:, j : j + 1] = jnp.sum(gacc[j], 1, keepdims=True)
    for jj in (2, 3, 0, 1):
        g = jj ^ (2 * core)
        gr = pl.ds(pl.multiple_of(g * GD, GD), GD)
        scatter(nt(hid_ref[gr, :], gup[g]), jj, g, keep_ref, send_ref, 0, low, far)
        scatter(nt(ctx_ref[gr, :], gatt[...]), jj, g, keep_ref, send_ref, 48, low, far)


def back_kernel(
    seg_ref, q_ref, k_ref, v_ref, kp_ref, vp_ref, gctx_ref, lse_ref, bias_ref,
    dq_ref, dk_ref, dv_ref, far_ref, dk, dv,
):
    two = seg_ref[BLK] == 1
    scale = jnp.where(two, 1.0, 0.0)
    dk[...] = jnp.zeros_like(dk)
    dv[...] = jnp.zeros_like(dv)

    items = []
    for h in range(3):
        hr = slice(h * HEAD_DIM, (h + 1) * HEAD_DIM)
        items += [{"h": h, "hr": hr, "b": b, "qc": slice(b * BLK, (b + 1) * BLK)} for b in range(3)]

    def scores(d):
        hr, qc, b = d["hr"], d["qc"], d["b"]
        s = tn(pick(k_ref, kp_ref, hr, b, two), q_ref[hr, qc])
        if b:
            s = s + bias_ref[b - 1].astype(F32)
        d["s"] = s
        d["dp"] = tn(pick(v_ref, vp_ref, hr, b, two), gctx_ref[hr, qc])

    def weights(d):
        p = jnp.exp(d.pop("s") - lse_ref[d["h"], :, d["qc"]])
        dp = d.pop("dp")
        dots = jnp.sum(p * dp, 0, keepdims=True)
        d["ds"] = (p * (dp - dots)).astype(BF16)
        d["p"] = p.astype(BF16)

    def mix(d):
        hr, qc, b = d["hr"], d["qc"], d["b"]
        ds = d.pop("ds")
        dq_ref[hr, qc] = (nn(pick(k_ref, kp_ref, hr, b, two), ds) * 0.125).astype(BF16)
        gk = nt(q_ref[hr, qc], ds)
        gv = nt(gctx_ref[hr, qc], d.pop("p"))
        for acc, grad, slot in ((dk, gk, 0), (dv, gv, 1)):
            acc[hr, qc] += grad[:, :BLK]
            other = grad[:, BLK:]
            if b == 0:
                far_ref[slot, hr, :BLK] = other.astype(BF16)
            elif b == 1:
                far_ref[slot, hr, BLK:] = (other * scale).astype(BF16)
                acc[hr, 2 * BLK :] += other * (1.0 - scale)
            else:
                acc[hr, BLK : 2 * BLK] += other

    pipelined(items, scores, weights, mix, 1, 2)
    dk_ref[...] = dk[...]
    dv_ref[...] = dv[...]


def through_kernel(
    code_ref, xt_ref, dqa_ref, dka_ref, dva_ref, ba_ref, dqb_ref, dkb_ref, dvb_ref, bb_ref, wqkv_ref,
    gfirst_ref, gvec1_ref, gvec2_ref, *refs, half,
):
    core = code_ref[0]
    order = jnp.where(core == half, code_ref[1], code_ref[2])
    if half:
        first_ref, _, gin_ref, keep_ref, send_ref, piece_ref = refs
    else:
        gin_ref, piece_ref = refs
    through = []
    groups = ((dqa_ref, dka_ref, dva_ref, ba_ref), (dqb_ref, dkb_ref, dvb_ref, bb_ref))
    for i, (dq_ref, dk_ref, dv_ref, b_ref) in enumerate(groups):
        rows = slice(i * GD, (i + 1) * GD)
        grads = [dq_ref[...]]
        for slot, ref in ((0, dk_ref), (1, dv_ref)):
            own = ref[...]
            own = jnp.concatenate([own[:, :EXT] + b_ref[slot].astype(F32), own[:, EXT:]], 1)
            grads.append(own.astype(BF16))
        through.append(sum(nn(wqkv_ref[t, i], grads[t]) for t in range(3)))
        row = jnp.concatenate(
            [nt(xt_ref[rows], grad) for grad in grads]
            + [gvec1_ref[rows], gvec2_ref[rows], jnp.zeros((GD, QCHUNK[1] - 3 * GD - 4), F32)],
            1,
        )
        for r in range(8):
            piece_ref[(i * 8 + r) ^ order] = row[24 * r : 24 * (r + 1)]
    if half:
        mine, other = piece_ref[...], first_ref[...]
        keep_ref[...] = jnp.where(core == 1, mine, other)
        send_ref[...] = jnp.where(core == 1, other, mine).astype(BF16)
    gin_ref[...] = (gfirst_ref[...] + jnp.concatenate(through, 0)).astype(BF16).T


def finish_kernel(code_ref, m_ref, *outs):
    core, low, far = code_ref[0], code_ref[1], code_ref[2]
    for half in range(2):
        for a in range(16):
            part = m_ref[half * 16 + (a ^ (far if half else low))].astype(F32)
            g = (half ^ core) * 2 + a // 8
            rows = slice(48 * (a % 8 // 2), 48 * (a % 8 // 2 + 1))
            lanes = slice(384 * (a % 2), 384 * (a % 2 + 1))
            for i, ref in enumerate(outs):
                ref[g, rows, lanes] = part[48 * i : 48 * (i + 1)]


def finish_qkv_kernel(code_ref, m_ref, gq_ref, ag_ref, as_ref, fg_ref, fs_ref, vec):
    core, low, far = code_ref[0], code_ref[1], code_ref[2]
    for half in range(2):
        for a in range(16):
            part = m_ref[half * 16 + (a ^ (far if half else low))].astype(F32)
            g = (half ^ core) * 2 + a // 8
            rows = slice(24 * (a % 8), 24 * (a % 8 + 1))
            for t in range(3):
                gq_ref[t, g, rows] = part[:, t * GD : (t + 1) * GD]
            vec[g, rows] = part[:, 512:640]
    turned = vec[...].reshape(D, 128).T
    for i, ref in enumerate((ag_ref, as_ref, fg_ref, fs_ref)):
        ref[...] = turned[64 + i : 65 + i].reshape(D)


SMEM = pl.BlockSpec(memory_space=pltpu.SMEM)
VMEM = pl.BlockSpec(memory_space=pltpu.VMEM)
ANY = pl.BlockSpec(memory_space=pl.ANY)


def call(kernel, name, ins, outs, scratch, limit, work, grid=(), aliases=None):
    return pl.pallas_call(
        kernel,
        grid=grid,
        out_shape=[jax.ShapeDtypeStruct(s, d) for s, d, _ in outs],
        in_specs=[spec for _, spec in ins],
        out_specs=[spec for _, _, spec in outs],
        scratch_shapes=scratch,
        compiler_params=pltpu.CompilerParams(vmem_limit_bytes=limit << 20),
        cost_estimate=pl.CostEstimate(flops=work[0], bytes_accessed=work[1], transcendentals=0),
        input_output_aliases=aliases or {},
        name=name,
    )(*[array for array, _ in ins])


def block(shape, *at):
    return pl.BlockSpec(shape, lambda _: at)


class Links:
    def __init__(self, n_seq):
        bits = max(n_seq.bit_length() - 1, 0)
        self.n = n_seq * 2
        orders = [list(range(bits)), [1, 0] + list(range(2, bits))] if bits > 1 else [list(range(bits))] * 2
        self.orders = orders
        self.halving = min(4, bits)
        self.bits = bits

    def pairs(self, step):
        if step < 0:
            return [(i, i ^ 1) for i in range(self.n)]
        return [(i, i ^ (2 << self.orders[i & 1][step])) for i in range(self.n)]

    def code(self, seq, core):
        def of(order):
            value = 0
            for step in range(4):
                value = value * 2 + (((seq >> order[step]) & 1) if step < self.halving else 0)
            return value

        return jnp.where(core == 0, of(self.orders[0]), of(self.orders[1]))


def swap(x, links, step):
    return lax.ppermute(x, "dev", links.pairs(step))


def all_sum(keep, came, links):
    total = keep.astype(F32) + came.astype(F32)
    for step in range(links.halving):
        half = total.shape[0] // 2
        total = total[:half] + swap(total[half:].astype(BF16), links, step).astype(F32)
    piece = total.astype(BF16)
    for step in range(links.halving, links.bits):
        piece = (piece.astype(F32) + swap(piece, links, step).astype(F32)).astype(BF16)
    for step in reversed(range(-1, links.halving)):
        piece = jnp.concatenate([piece, swap(piece, links, step)], 0)
    return piece


def per_device(
    links, inputs, segment_ids, qkv_weight, out_weight, ffn_in_weight, ffn_out_weight,
    attn_gain, attn_shift, ffn_gain, ffn_shift, out_cotangent,
):
    me = lax.axis_index("dev")
    seq, core = me >> 1, me & 1
    code = jnp.stack([core, links.code(seq, core), links.code(seq, 1 - core)]).astype(jnp.int32)
    partner = swap(inputs, links, -1)
    square = (D, TOK)
    large = (GROUPS, GF, TOK)
    xt, q, k, v, bias = call(
        project_kernel,
        "project",
        [(segment_ids, SMEM), (inputs, VMEM), (segment_ids, VMEM), (qkv_weight, VMEM)],
        [(square, BF16, VMEM)] * 4 + [((2, 2 * BLK, BLK), BF16, VMEM)],
        [],
        12,
        (2_000_000_000, 7_000_000),
    )
    kp, vp, ctx, lse = call(
        attend_kernel,
        "attend",
        [(segment_ids, SMEM), (partner, VMEM), (qkv_weight, VMEM), (q, VMEM), (k, VMEM), (v, VMEM), (bias, VMEM)],
        [((D, EXT), BF16, VMEM), ((D, EXT), BF16, VMEM), (square, BF16, VMEM), ((HEADS, 1, TOK), F32, VMEM)],
        [],
        12,
        (8_000_000_000, 9_000_000),
    )
    weight2t = jnp.swapaxes(ffn_out_weight, 1, 2)
    output, hid, n1, inv1, gpr, gsec, gfeed, keep, send, gvec2 = call(
        forward_kernel,
        "forward",
        [(code, SMEM), (xt, VMEM), (ctx, VMEM), (out_weight, VMEM), (ffn_in_weight, VMEM), (weight2t, VMEM)]
        + [(out_cotangent, VMEM), (attn_gain, VMEM), (attn_shift, VMEM), (ffn_gain, VMEM), (ffn_shift, VMEM)],
        [((TOK, D), BF16, VMEM), (square, BF16, VMEM), (square, F32, VMEM), ((1, TOK), F32, VMEM), (large, BF16, VMEM)]
        + [(square, F32, VMEM), (square, BF16, VMEM), ((16, 48, 384), BF16, VMEM), ((16, 48, 384), BF16, VMEM)]
        + [((D, 2), F32, VMEM)],
        [
            pltpu.VMEM((D, D), BF16), pltpu.VMEM((GROUPS, GF, GD), BF16), pltpu.VMEM(large, BF16),
            pltpu.VMEM((4, D, BLK), F32), pltpu.VMEM((2, D, 128), F32),
        ],
        20,
        (10_000_000_000, 20_000_000),
    )
    came = swap(send, links, -1)
    gctx, gfirst, keep1, send1, gvec1 = call(
        backward_kernel,
        "backward",
        [(code, SMEM), (ctx, VMEM), (out_weight, VMEM), (ffn_in_weight, VMEM), (weight2t, VMEM), (hid, VMEM)]
        + [(n1, VMEM), (inv1, VMEM), (gpr, VMEM), (gsec, VMEM), (gfeed, VMEM), (attn_gain, VMEM)],
        [(square, BF16, VMEM), (square, F32, VMEM), ((16, 96, 384), BF16, VMEM), ((16, 96, 384), BF16, VMEM)]
        + [((D, 2), F32, VMEM)],
        [
            pltpu.VMEM((GROUPS, GF, GD), BF16), pltpu.VMEM(large, BF16), pltpu.VMEM(square, BF16),
            pltpu.VMEM((D, BLK), F32), pltpu.VMEM((2, D, 128), F32),
        ],
        18,
        (10_000_000_000, 20_000_000),
    )
    came1 = swap(send1, links, -1)

    def attention_back(g):
        rows = partial(lambda width: block((GD, width), g, 0))
        return call(
            back_kernel,
            "attention_back",
            [(segment_ids, SMEM), (q, rows(TOK)), (k, rows(TOK)), (v, rows(TOK)), (kp, rows(EXT)), (vp, rows(EXT))]
            + [(gctx, rows(TOK)), (lse, block((3, 1, TOK), g, 0, 0)), (bias, VMEM)],
            [((GD, TOK), BF16, VMEM), ((GD, TOK), F32, VMEM), ((GD, TOK), F32, VMEM), ((2, GD, EXT), BF16, VMEM)],
            [pltpu.VMEM((GD, TOK), F32), pltpu.VMEM((GD, TOK), F32)],
            10,
            (4_000_000_000, 4_000_000),
            (1,),
        )

    def through(half, parts, first):
        ins = [(code, SMEM), (xt, block((HALF, TOK), half, 0))]
        for dq, dk, dv, far in parts:
            ins += [(dq, VMEM), (dk, VMEM), (dv, VMEM), (swap(far, links, -1), VMEM)]
        ins += [(qkv_weight, block((3, 2, GD, GD), 0, half, 0, 0))]
        ins += [(gfirst, block((HALF, TOK), half, 0)), (gvec1, block((HALF, 2), half, 0))]
        ins += [(gvec2, block((HALF, 2), half, 0))]
        shape = (16,) + QCHUNK
        outs = [((TOK, D), BF16, block((TOK, HALF), 0, half))]
        if half:
            ins += [(first[1], VMEM), (first[0], ANY)]
            outs += [(shape, F32, VMEM), (shape, BF16, VMEM)]
        else:
            outs += [(shape, F32, VMEM)]
        return call(
            partial(through_kernel, half=half),
            "through_qkv",
            ins,
            outs,
            [pltpu.VMEM(shape, F32)] if half else [],
            10,
            (2_000_000_000, 6_000_000),
            (1,),
            {len(ins) - 1: 0} if half else None,
        )

    parts = [attention_back(g) for g in range(GROUPS)]
    first = through(0, parts[:2], None)
    grad_input, keep_q, send_q = through(1, parts[2:], first)
    m2 = all_sum(keep, came, links)
    m1 = all_sum(keep1, came1, links)
    mq = all_sum(keep_q, swap(send_q, links, -1), links)
    rows = (GROUPS, GD, D)
    (g2,) = call(finish_kernel, "finish", [(code, SMEM), (m2, VMEM)], [(rows, F32, VMEM)], [], 10, (0, 4_000_000))
    g1, go = call(
        finish_kernel, "finish", [(code, SMEM), (m1, VMEM)], [(rows, F32, VMEM)] * 2, [], 16, (0, 8_000_000)
    )
    gq, *vectors = call(
        finish_qkv_kernel,
        "finish_qkv",
        [(code, SMEM), (mq, VMEM)],
        [((3, GROUPS, GD, GD), F32, VMEM)] + [((D,), F32, VMEM)] * 4,
        [pltpu.VMEM((GROUPS, GD, 128), F32)],
        8,
        (0, 4_000_000),
    )
    return (output, grad_input, gq, go.reshape(D, D), g1, jnp.swapaxes(g2, 1, 2)) + tuple(vectors)


def solution(mesh):
    flat = Mesh(mesh.devices.reshape(-1), ("dev",))
    links = Links(mesh.shape["seq"])
    split, copied = P("dev"), P()
    return jax.shard_map(
        partial(per_device, links),
        mesh=flat,
        in_specs=(split, split) + (copied,) * 8 + (split,),
        out_specs=(split, split) + (copied,) * 8,
        check_vma=False,
    )
```

```python
from functools import partial

import jax
import jax.numpy as jnp
from jax import lax
from jax.experimental import pallas as pl
from jax.experimental.pallas import tpu as pltpu
from jax.sharding import Mesh, PartitionSpec as P

F32 = jnp.float32
BF16 = jnp.bfloat16
EPSILON = 1e-05
HEADS = 12
HEAD_DIM = 64
D = 768
GROUPS = 4
GD = D // GROUPS
FF = 3072
GF = FF // GROUPS
TOK = 768
BLK = 256
EXT = 512
WIDTH = 640
HALF = D // 2
COST = dict(project=3, attend=9, forward=19, backward=6, weights=4, attention=4, through=3, sum=9, finish=3)


def nn(a, b):
    return lax.dot_general(a, b, (((1,), (0,)), ((), ())), preferred_element_type=F32)


def nt(a, b):
    return lax.dot_general(a, b, (((1,), (1,)), ((), ())), preferred_element_type=F32)


def tn(a, b):
    return lax.dot_general(a, b, (((0,), (0,)), ((), ())), preferred_element_type=F32)


def gelu_parts(u):
    a = jnp.abs(u) * 0.7071067811865476
    t = 1.0 / (1.0 + 0.3275911 * a)
    e = jnp.exp(-0.5 * (u * u))
    poly = t * (
        0.254829592
        + t * (-0.284496736 + t * (1.421413741 + t * (-1.453152027 + t * 1.061405429)))
    )
    tail = 0.5 * poly * e
    phi = jnp.where(u < 0, tail, 1.0 - tail)
    return u * phi, phi + u * (e * 0.3989422804014327)


def pipelined(items, first, second, third, lag, last):
    n = len(items)
    for t in range(n + last):
        if t < n:
            first(items[t])
        if 0 <= t - lag < n:
            second(items[t - lag])
        if 0 <= t - last < n:
            third(items[t - last])


def project_kernel(
    seg_ref, x_hbm, ids_hbm, wqkv_hbm,
    xt_ref, q_ref, k_ref, v_ref, bias_ref,
    x_ref, ids_ref, wqkv_ref, sem,
):
    loads = [
        pltpu.make_async_copy(source, ref, sem.at[i])
        for i, (source, ref) in enumerate(((x_hbm, x_ref), (wqkv_hbm, wqkv_ref), (ids_hbm, ids_ref)))
    ]
    for copy in loads:
        copy.start()
    for copy in loads:
        copy.wait()
    two = seg_ref[BLK] == 1
    xt_ref[...] = x_ref[...].T
    for g in range(GROUPS):
        rows = slice(g * GD, (g + 1) * GD)
        xg = xt_ref[rows, :]
        q_ref[rows, :] = (tn(wqkv_ref[0, g], xg).astype(BF16).astype(F32) * 0.125).astype(BF16)
        k_ref[rows, :] = tn(wqkv_ref[1, g], xg).astype(BF16)
        v_ref[rows, :] = tn(wqkv_ref[2, g], xg).astype(BF16)
    row = ids_ref[...].reshape(1, TOK)

    def lanes(b):
        return jnp.broadcast_to(row[:, b * BLK : (b + 1) * BLK], (BLK, BLK))

    def same(kb, qb):
        return jnp.where(lanes(kb).T == lanes(qb), 0.0, -1e30).astype(BF16)

    bias_ref[0, :BLK] = same(1, 1)
    bias_ref[0, BLK:] = jnp.where(two, jnp.zeros((BLK, BLK), BF16), same(2, 1))
    bias_ref[1, :BLK] = same(2, 2)
    bias_ref[1, BLK:] = same(1, 2)


def pick(ref, far_ref, hr, b, two):
    if b == 0:
        other = far_ref[hr, :BLK]
    elif b == 1:
        other = jnp.where(two, far_ref[hr, BLK:], ref[hr, 2 * BLK :])
    else:
        other = ref[hr, BLK : 2 * BLK]
    return jnp.concatenate([ref[hr, b * BLK : (b + 1) * BLK], other], 1)


def attend_kernel(
    seg_ref, xp_ref, wqkv_ref, q_ref, k_ref, v_ref, bias_ref,
    kp_ref, vp_ref, ctx_ref, lse_ref,
):
    two = seg_ref[BLK] == 1
    xpt = xp_ref[:EXT, :].T
    for g in range(GROUPS):
        rows = slice(g * GD, (g + 1) * GD)
        kp_ref[rows, :] = tn(wqkv_ref[1, g], xpt[rows]).astype(BF16)
        vp_ref[rows, :] = tn(wqkv_ref[2, g], xpt[rows]).astype(BF16)

    def heads(i, carry):
        items = []
        for u in range(4):
            h = i * 4 + u
            hr = pl.ds(pl.multiple_of(h * HEAD_DIM, HEAD_DIM), HEAD_DIM)
            items += [{"h": h, "hr": hr, "b": b, "qc": slice(b * BLK, (b + 1) * BLK)} for b in range(3)]

        def scores(d):
            s = tn(pick(k_ref, kp_ref, d["hr"], d["b"], two), q_ref[d["hr"], d["qc"]])
            if d["b"]:
                s = s + bias_ref[d["b"] - 1].astype(F32)
            d["s"] = s

        def weights(d):
            s = d.pop("s")
            d["top"] = jnp.max(s, 0, keepdims=True)
            p = jnp.exp(s - d["top"])
            d["total"] = jnp.sum(p, 0, keepdims=True)
            d["p"] = p.astype(BF16)

        def mix(d):
            c = nn(pick(v_ref, vp_ref, d["hr"], d["b"], two), d.pop("p"))
            ctx_ref[d["hr"], d["qc"]] = (c * (1.0 / d["total"])).astype(BF16)
            lse_ref[d["h"], :, d["qc"]] = d["top"] + jnp.log(d["total"])

        pipelined(items, scores, weights, mix, 2, 3)
        return carry

    lax.fori_loop(0, HEADS // 4, heads, 0)


PARTS = [(g, slice(j * BLK, (j + 1) * BLK)) for g in range(GROUPS) for j in range(GF // BLK)]


def columns(ref):
    wide = jnp.broadcast_to(ref[...].reshape(1, D), (128, D)).T
    return jnp.concatenate([wide, wide], 1)


def halves(x):
    return x[:, :128] + x[:, 128:]


def scatter(part, jj, g, keep_ref, send_ref, at, low, far):
    for r in range(4):
        piece = part[48 * r : 48 * (r + 1)].astype(BF16)
        pos = ((g & 1) * 4 + r) ^ (low if jj < 2 else far)
        ref = keep_ref if jj < 2 else send_ref
        ref[pos, at : at + 48] = piece


def forward_kernel(
    code_ref, xt_ref, ctx_ref, wo_ref, w1_ref, w2t_ref, cot_ref, ag_ref, as_ref, fg_ref, fs_ref,
    out_ref, hid_ref, n1_ref, inv1_ref, gpr_ref, gsec_ref, gfeed_ref, keep_ref, send_ref, gvec_ref,
    wot, w1t, act, nb, gacc,
):
    core, low, far = code_ref[0], code_ref[3], code_ref[4]
    for j, ref in enumerate((ag_ref, as_ref, fg_ref, fs_ref)):
        nb[j] = columns(ref)
    wot[...] = wo_ref[...].T
    for g in range(GROUPS):
        w1t[g] = w1_ref[g].T
    gacc[...] = jnp.zeros_like(gacc)

    def tile(t, carry):
        tc = pl.ds(pl.multiple_of(t * BLK, BLK), BLK)
        r = xt_ref[:, tc].astype(F32) + nn(wot[...], ctx_ref[:, tc])
        centre = r - jnp.mean(r, 0, keepdims=True)
        inv1 = lax.rsqrt(jnp.mean(centre * centre, 0, keepdims=True) + EPSILON)
        n1 = centre * inv1
        n1_ref[:, tc] = n1
        inv1_ref[:, tc] = inv1
        hidden = n1 * nb[0] + nb[1]
        hid_ref[:, tc] = hidden.astype(BF16)
        up, feeds = {}, []

        def rise(p):
            g, fr = p
            up[g, fr.start] = nn(w1t[g, fr], hid_ref[g * GD : (g + 1) * GD, tc])

        def bend(p):
            g, fr = p
            a, d = gelu_parts(up.pop((g, fr.start)))
            act[g, fr, tc] = a.astype(BF16)
            gpr_ref[g, fr, tc] = d.astype(BF16)

        def fall(p):
            if p[1].stop == GF:
                feeds.append(nn(w2t_ref[p[0]], act[p[0], :, tc]))

        pipelined(PARTS, rise, bend, fall, 2, 3)
        r2 = hidden + jnp.concatenate(feeds, 0)
        centre2 = r2 - jnp.mean(r2, 0, keepdims=True)
        inv2 = lax.rsqrt(jnp.mean(centre2 * centre2, 0, keepdims=True) + EPSILON)
        n2 = centre2 * inv2
        out_ref[tc, :] = (n2 * nb[2] + nb[3]).astype(BF16).T
        c = cot_ref[tc, :].T.astype(F32)
        gacc[0] += halves(c * n2)
        gacc[1] += halves(c)
        cg = c * nb[2]
        gsec = inv2 * (
            cg - jnp.mean(cg, 0, keepdims=True) - n2 * jnp.mean(cg * n2, 0, keepdims=True)
        )
        gsec_ref[:, tc] = gsec
        gfeed_ref[:, tc] = gsec.astype(BF16)
        return carry

    lax.fori_loop(0, TOK // BLK, tile, 0)
    for j in range(2):
        gvec_ref[:, j : j + 1] = jnp.sum(gacc[j], 1, keepdims=True)
    for jj in (2, 3, 0, 1):
        g = jj ^ (2 * core)
        gr = pl.ds(pl.multiple_of(g * GD, GD), GD)
        scatter(nt(gfeed_ref[gr, :], act[g]), jj, g, keep_ref, send_ref, 0, low, far)


def backward_kernel(
    wo_ref, w1_ref, w2t_ref, n1_ref, inv1_ref, gpr_ref, gsec_ref, gfeed_ref, ag_ref,
    gctx_ref, gfirst_ref, gup, gatt, gvec_ref,
    w2, nb, gacc,
):
    nb[...] = columns(ag_ref)
    for g in range(GROUPS):
        w2[g] = w2t_ref[g].T
    gacc[...] = jnp.zeros_like(gacc)

    def tile(t, carry):
        tc = pl.ds(pl.multiple_of(t * BLK, BLK), BLK)
        back, gh = {}, []

        def lift(p):
            g, fr = p
            back[g, fr.start] = nn(w2[g, fr], gfeed_ref[g * GD : (g + 1) * GD, tc])

        def scale(p):
            g, fr = p
            gup[g, fr, tc] = (back.pop((g, fr.start)) * gpr_ref[g, fr, tc].astype(F32)).astype(BF16)

        def drop(p):
            if p[1].stop == GF:
                gh.append(nn(w1_ref[p[0]], gup[p[0], :, tc]))

        pipelined(PARTS, lift, scale, drop, 2, 3)
        ghid = gsec_ref[:, tc] + jnp.concatenate(gh, 0)
        n1 = n1_ref[:, tc]
        gacc[0] += halves(ghid * n1)
        gacc[1] += halves(ghid)
        sc = ghid * nb[...]
        gfirst = inv1_ref[:, tc] * (
            sc - jnp.mean(sc, 0, keepdims=True) - n1 * jnp.mean(sc * n1, 0, keepdims=True)
        )
        gfirst_ref[:, tc] = gfirst
        gatt[:, tc] = gfirst.astype(BF16)
        gctx_ref[:, tc] = nn(wo_ref[...], gatt[:, tc]).astype(BF16)
        return carry

    lax.fori_loop(0, TOK // BLK, tile, 0)
    for j in range(2):
        gvec_ref[:, j : j + 1] = jnp.sum(gacc[j], 1, keepdims=True)


def weights_kernel(code_ref, ctx_ref, hid_ref, gup_ref, gatt_ref, keep_ref, send_ref):
    core, low, far = code_ref[0], code_ref[1], code_ref[2]
    for jj in (2, 3, 0, 1):
        g = jj ^ (2 * core)
        gr = pl.ds(pl.multiple_of(g * GD, GD), GD)
        scatter(nt(hid_ref[gr, :], gup_ref[g]), jj, g, keep_ref, send_ref, 0, low, far)
        scatter(nt(ctx_ref[gr, :], gatt_ref[...]), jj, g, keep_ref, send_ref, 48, low, far)


def back_kernel(
    seg_ref, q_ref, k_ref, v_ref, kp_ref, vp_ref, gctx_ref, lse_ref, bias_ref,
    dq_ref, dk_ref, dv_ref, far_ref, dk, dv,
):
    two = seg_ref[BLK] == 1
    scale = jnp.where(two, 1.0, 0.0)
    dk[...] = jnp.zeros_like(dk)
    dv[...] = jnp.zeros_like(dv)

    items = []
    for h in range(3):
        hr = slice(h * HEAD_DIM, (h + 1) * HEAD_DIM)
        items += [{"h": h, "hr": hr, "b": b, "qc": slice(b * BLK, (b + 1) * BLK)} for b in range(3)]

    def scores(d):
        hr, qc, b = d["hr"], d["qc"], d["b"]
        s = tn(pick(k_ref, kp_ref, hr, b, two), q_ref[hr, qc])
        if b:
            s = s + bias_ref[b - 1].astype(F32)
        d["s"] = s
        d["dp"] = tn(pick(v_ref, vp_ref, hr, b, two), gctx_ref[hr, qc])

    def weights(d):
        p = jnp.exp(d.pop("s") - lse_ref[d["h"], :, d["qc"]])
        dp = d.pop("dp")
        dots = jnp.sum(p * dp, 0, keepdims=True)
        d["ds"] = (p * (dp - dots)).astype(BF16)
        d["p"] = p.astype(BF16)

    def mix(d):
        hr, qc, b = d["hr"], d["qc"], d["b"]
        ds = d.pop("ds")
        dq_ref[hr, qc] = (nn(pick(k_ref, kp_ref, hr, b, two), ds) * 0.125).astype(BF16)
        gk = nt(q_ref[hr, qc], ds)
        gv = nt(gctx_ref[hr, qc], d.pop("p"))
        for acc, grad, slot in ((dk, gk, 0), (dv, gv, 1)):
            acc[hr, qc] += grad[:, :BLK]
            other = grad[:, BLK:]
            if b == 0:
                far_ref[slot, hr, :BLK] = other.astype(BF16)
            elif b == 1:
                far_ref[slot, hr, BLK:] = (other * scale).astype(BF16)
                acc[hr, 2 * BLK :] += other * (1.0 - scale)
            else:
                acc[hr, BLK : 2 * BLK] += other

    pipelined(items, scores, weights, mix, 1, 2)
    dk_ref[...] = dk[...]
    dv_ref[...] = dv[...]


def through_kernel(
    code_ref, xt_ref, dqa_ref, dka_ref, dva_ref, ba_ref, dqb_ref, dkb_ref, dvb_ref, bb_ref, wqkv_ref,
    gfirst_ref, gvec1_ref, gvec2_ref, *refs, half,
):
    core = code_ref[0]
    order = jnp.where(core == half, code_ref[1], code_ref[2])
    if half:
        first_ref, _, gin_ref, keep_ref, send_ref, piece_ref = refs
    else:
        gin_ref, piece_ref = refs
    through = []
    groups = ((dqa_ref, dka_ref, dva_ref, ba_ref), (dqb_ref, dkb_ref, dvb_ref, bb_ref))
    for i, (dq_ref, dk_ref, dv_ref, b_ref) in enumerate(groups):
        rows = slice(i * GD, (i + 1) * GD)
        grads = [dq_ref[...]]
        for slot, ref in ((0, dk_ref), (1, dv_ref)):
            own = ref[...]
            own = jnp.concatenate([own[:, :EXT] + b_ref[slot].astype(F32), own[:, EXT:]], 1)
            grads.append(own.astype(BF16))
        through.append(sum(nn(wqkv_ref[t, i], grads[t]) for t in range(3)))
        row = jnp.concatenate(
            [nt(xt_ref[rows], grad) for grad in grads]
            + [gvec1_ref[rows], gvec2_ref[rows], jnp.zeros((GD, WIDTH - 3 * GD - 4), F32)],
            1,
        )
        for r in range(4):
            piece_ref[(i * 4 + r) ^ order] = row[48 * r : 48 * (r + 1)]
    if half:
        mine, other = piece_ref[...], first_ref[...]
        keep_ref[...] = jnp.where(core == 1, mine, other)
        send_ref[...] = jnp.where(core == 1, other, mine).astype(BF16)
    gin_ref[...] = (gfirst_ref[...] + jnp.concatenate(through, 0)).astype(BF16).T


def chunks(code_ref, near_ref, far_ref):
    core, low, far = code_ref[0], code_ref[1], code_ref[2]
    for other, ref in ((0, near_ref), (1, far_ref)):
        for a in range(8):
            g = (other ^ core) * 2 + a // 4
            rows = slice(48 * (a % 4), 48 * (a % 4 + 1))
            yield g, rows, ref[a ^ (far if other else low)].astype(F32)


def finish_kernel(code_ref, half_ref, *refs, far, way, outs):
    *refs, token_ref = refs
    token_ref[...] = jnp.zeros_like(token_ref)
    order = code_ref[1 + 2 * way + far]
    for a in range(8):
        part = half_ref[a ^ order].astype(F32)
        rows = slice(48 * (a % 4), 48 * (a % 4 + 1))
        for i, ref in enumerate(refs[-outs:]):
            ref[a // 4, rows] = part[48 * i : 48 * (i + 1)]


def finish_qkv_kernel(code_ref, near_ref, far_ref, gq_ref, ag_ref, as_ref, fg_ref, fs_ref, vec):
    for g, rows, part in chunks(code_ref, near_ref, far_ref):
        for t in range(3):
            gq_ref[t, g, rows] = part[:, t * GD : (t + 1) * GD]
        vec[g, rows] = part[:, 512:640]
    turned = vec[...].reshape(D, 128).T
    for i, ref in enumerate((ag_ref, as_ref, fg_ref, fs_ref)):
        ref[...] = turned[64 + i : 65 + i].reshape(D)


def fold_kernel(keep_ref, came_ref, kept_ref, send_ref):
    n = kept_ref.shape[0]
    kept_ref[...] = keep_ref[:n].astype(F32) + came_ref[:n].astype(F32)
    send_ref[...] = (keep_ref[n:].astype(F32) + came_ref[n:].astype(F32)).astype(BF16)


def meet_kernel(*refs):
    *ins, out_ref = refs
    at = 0
    for keep_ref, came_ref in zip(ins[::2], ins[1::2]):
        rows = keep_ref.shape[1]
        out_ref[:, at : at + rows] = (keep_ref[...].astype(F32) + came_ref[...].astype(F32)).astype(BF16)
        at += rows


def join_kernel(near_ref, far_ref, out_ref):
    n = near_ref.shape[0]
    out_ref[:n] = near_ref[...]
    out_ref[n:] = far_ref[...]


SMEM = pl.BlockSpec(memory_space=pltpu.SMEM)
VMEM = pl.BlockSpec(memory_space=pltpu.VMEM)
ANY = pl.BlockSpec(memory_space=pl.ANY)


class Steps:
    def __init__(self):
        self.last = None

    def __call__(self, kernel, name, ins, outs, scratch, limit, grid=(), code=None, aliases=None):
        n, free = len(ins) + (code is not None), self.last is None
        if not free:
            ins = ins + [(self.last, ANY)]
        specs = dict(
            grid=grid,
            in_specs=[spec for _, spec in ins],
            out_specs=[spec for _, _, spec in outs],
            scratch_shapes=scratch,
        )
        if code is not None:
            specs = dict(grid_spec=pltpu.PrefetchScalarGridSpec(num_scalar_prefetch=1, **specs))
        results = pl.pallas_call(
            kernel if free else lambda *refs: kernel(*refs[:n], *refs[n + 1 :]),
            out_shape=[jax.ShapeDtypeStruct(s, d) for s, d, _ in outs],
            compiler_params=pltpu.CompilerParams(vmem_limit_bytes=limit << 20),
            cost_estimate=pl.CostEstimate(flops=int(COST[name.split('_')[0]] * 1e9), bytes_accessed=1024, transcendentals=0),
            input_output_aliases=aliases or {},
            name=name,
            **specs,
        )(*([] if code is None else [code]), *[array for array, _ in ins])
        self.last = results[-1]
        return results


def block(shape, *at):
    return pl.BlockSpec(shape, lambda _: at)


class Links:
    def __init__(self, n_seq, orders):
        bits = n_seq.bit_length() - 1
        self.n = n_seq * 2
        self.orders = [order + list(range(3, bits)) for order in orders]
        self.bits = bits

    def pairs(self, step):
        if step < 0:
            return [(i, i ^ 1) for i in range(self.n)]
        return [(i, i ^ (2 << self.orders[i & 1][step])) for i in range(self.n)]

    def code(self, seq, core):
        first, second = [sum(((seq >> order[step]) & 1) << (2 - step) for step in range(3)) for order in self.orders]
        return jnp.where(core == 0, first, second)


def swap(x, links, step):
    return lax.ppermute(x, "dev", links.pairs(step))


class Total:
    def __init__(self, run, links, name, keep, came):
        self.run, self.links, self.name = run, links, name
        self.keep, self.came = keep, came
        self.step = 0

    def small(self, kernel, ins, outs):
        spec = [(x, VMEM) for x in ins]
        return self.run(kernel, self.name, spec, [o + (VMEM,) for o in outs], [], 4)

    def fold(self):
        shape = (self.keep.shape[0] // 2,) + self.keep.shape[1:]
        self.keep, send = self.small(fold_kernel, [self.keep, self.came], [(shape, F32), (shape, BF16)])
        self.came = swap(send, self.links, self.step)
        self.step += 1

    def meet(self, *others):
        parts = [*others, self]
        shape = (1, sum(p.keep.shape[1] for p in parts), self.keep.shape[2])
        ins = [x for p in parts for x in (p.keep, p.came)]
        (self.near,) = self.small(meet_kernel, ins, [(shape, BF16)])
        for step in range(3, self.links.bits - 1):
            (self.near,) = self.small(meet_kernel, [self.near, swap(self.near, self.links, step)], [(shape, BF16)])
        self.far = swap(self.near, self.links, self.links.bits - 1)

    def whole(self):
        (self.near,) = self.small(meet_kernel, [self.near, self.far], [(self.near.shape, BF16)])
        self.step = 2
        self.far = swap(self.near, self.links, self.step)

    def join(self):
        shape = (self.near.shape[0] * 2,) + self.near.shape[1:]
        (self.near,) = self.small(join_kernel, [self.near, self.far], [(shape, BF16)])
        self.step -= 1
        self.far = swap(self.near, self.links, self.step)


def per_device(
    links, upright, inputs, segment_ids, qkv_weight, out_weight, ffn_in_weight, ffn_out_weight,
    attn_gain, attn_shift, ffn_gain, ffn_shift, out_cotangent,
):
    me = lax.axis_index("dev")
    seq, core = me >> 1, me & 1
    codes = [core]
    for way in (links, upright):
        codes += [way.code(seq, core), way.code(seq, 1 - core)]
    code = jnp.stack(codes).astype(jnp.int32)
    partner = swap(inputs, links, -1)
    square = (D, TOK)
    large = (GROUPS, GF, TOK)
    run = Steps()
    xt, q, k, v, bias = run(
        project_kernel,
        "project",
        [(segment_ids, SMEM), (inputs, ANY), (segment_ids, ANY), (qkv_weight, ANY)],
        [(square, BF16, VMEM)] * 4 + [((2, 2 * BLK, BLK), BF16, VMEM)],
        [
            pltpu.VMEM((TOK, D), BF16), pltpu.VMEM((TOK,), jnp.int32), pltpu.VMEM((3, GROUPS, GD, GD), BF16),
            pltpu.SemaphoreType.DMA((3,)),
        ],
        12,
    )
    kp, vp, ctx, lse = run(
        attend_kernel,
        "attend",
        [(segment_ids, SMEM), (partner, VMEM), (qkv_weight, VMEM), (q, VMEM), (k, VMEM), (v, VMEM), (bias, VMEM)],
        [((D, EXT), BF16, VMEM), ((D, EXT), BF16, VMEM), (square, BF16, VMEM), ((HEADS, 1, TOK), F32, VMEM)],
        [],
        12,
    )
    weight2t = jnp.swapaxes(ffn_out_weight, 1, 2)
    output, hid, n1, inv1, gpr, gsec, gfeed, keep, send, gvec2 = run(
        forward_kernel,
        "forward",
        [(code, SMEM), (xt, VMEM), (ctx, VMEM), (out_weight, VMEM), (ffn_in_weight, VMEM), (weight2t, VMEM)]
        + [(out_cotangent, VMEM), (attn_gain, VMEM), (attn_shift, VMEM), (ffn_gain, VMEM), (ffn_shift, VMEM)],
        [((TOK, D), BF16, VMEM), (square, BF16, VMEM), (square, F32, VMEM), ((1, TOK), F32, VMEM), (large, BF16, VMEM)]
        + [(square, F32, VMEM), (square, BF16, VMEM), ((8, 48, D), BF16, VMEM), ((8, 48, D), BF16, VMEM)]
        + [((D, 2), F32, VMEM)],
        [
            pltpu.VMEM((D, D), BF16), pltpu.VMEM((GROUPS, GF, GD), BF16), pltpu.VMEM(large, BF16),
            pltpu.VMEM((4, D, BLK), F32), pltpu.VMEM((2, D, 128), F32),
        ],
        20,
    )
    ffn_out = Total(run, upright, "sum_ffn_out", keep, swap(send, links, -1))
    gctx, gfirst, gup, gatt, gvec1 = run(
        backward_kernel,
        "backward",
        [(out_weight, VMEM), (ffn_in_weight, VMEM), (weight2t, VMEM)]
        + [(n1, VMEM), (inv1, VMEM), (gpr, VMEM), (gsec, VMEM), (gfeed, VMEM), (attn_gain, VMEM)],
        [(square, BF16, VMEM), (square, F32, VMEM), (large, BF16, VMEM), (square, BF16, VMEM), ((D, 2), F32, VMEM)],
        [pltpu.VMEM((GROUPS, GF, GD), BF16), pltpu.VMEM((D, BLK), F32), pltpu.VMEM((2, D, 128), F32)],
        12,
    )
    ffn_out.fold()
    message = ((8, 96, D), BF16, VMEM)
    keep, send = run(
        weights_kernel,
        "weights",
        [(code, SMEM), (ctx, VMEM), (hid, VMEM), (gup, VMEM), (gatt, VMEM)],
        [message, message],
        [],
        12,
    )
    others = Total(run, links, "sum_others", keep, swap(send, links, -1))

    def attention_back(g):
        rows = partial(lambda width: block((GD, width), g, 0))
        return run(
            back_kernel,
            "attention_back",
            [(segment_ids, SMEM), (q, rows(TOK)), (k, rows(TOK)), (v, rows(TOK)), (kp, rows(EXT)), (vp, rows(EXT))]
            + [(gctx, rows(TOK)), (lse, block((3, 1, TOK), g, 0, 0)), (bias, VMEM)],
            [((GD, TOK), BF16, VMEM), ((GD, TOK), F32, VMEM), ((GD, TOK), F32, VMEM), ((2, GD, EXT), BF16, VMEM)],
            [pltpu.VMEM((GD, TOK), F32), pltpu.VMEM((GD, TOK), F32)],
            10,
            (1,),
        )

    def through(half, parts, first):
        ins = [(code, SMEM), (xt, block((HALF, TOK), half, 0))]
        for dq, dk, dv, far in parts:
            ins += [(dq, VMEM), (dk, VMEM), (dv, VMEM), (swap(far, links, -1), VMEM)]
        ins += [(qkv_weight, block((3, 2, GD, GD), 0, half, 0, 0))]
        ins += [(gfirst, block((HALF, TOK), half, 0)), (gvec1, block((HALF, 2), half, 0))]
        ins += [(gvec2, block((HALF, 2), half, 0))]
        shape = (8, 48, WIDTH)
        outs = [((TOK, D), BF16, block((TOK, HALF), 0, half))]
        if half:
            ins += [(first[1], VMEM), (first[0], ANY)]
            outs += [(shape, F32, VMEM), (shape, BF16, VMEM)]
        else:
            outs += [(shape, F32, VMEM)]
        return run(
            partial(through_kernel, half=half),
            "through_qkv",
            ins,
            outs,
            [pltpu.VMEM(shape, F32)] if half else [],
            10,
            (1,),
            None,
            {len(ins) - 1: 0} if half else None,
        )

    rows = (GROUPS, GD, D)

    def finish(total, far, into, way, n):
        def half(c):
            return (c[0] ^ far, 0, 0)

        outs = [(rows, F32, pl.BlockSpec((2, GD, D), lambda _, c: half(c)))] * n
        outs += [((8, 128), F32, pl.BlockSpec((8, 128), lambda _, c: (0, 0)))]
        ins = [(total.far if far else total.near, pl.BlockSpec((8, 48 * n, D), lambda _, c: (0, 0, 0)))]
        ins += [(x, ANY) for x in into]
        kernel = partial(finish_kernel, far=far, way=way, outs=n)
        return run(kernel, "finish", ins, outs, [], 12, (1,), code, {2 + i: i for i in range(len(into))})[:n]

    parts = [attention_back(0)]
    ffn_out.fold()
    others.fold()
    parts += [attention_back(1)]
    ffn_out.fold()
    parts += [attention_back(2)]
    others.fold()
    first = through(0, parts[:2], None)
    ffn_out.meet()
    parts += [attention_back(3)]
    others.fold()
    grad_input, keep, send = through(1, parts[2:], first)
    others.meet()
    qkv = Total(run, links, "sum_qkv", keep, swap(send, links, -1))
    qkv.fold()
    ffn_out.whole()
    qkv.fold()
    ffn_out.join()
    others.whole()
    qkv.fold()
    ffn_out.join()
    others.join()
    qkv.meet()
    others.join()
    qkv.whole()
    ffn_out.join()
    qkv.join()
    near_out = finish(ffn_out, 0, [], 1, 1)
    qkv.join()
    (g2,) = finish(ffn_out, 1, near_out, 1, 1)
    others.join()
    half_way = finish(others, 0, [], 0, 2)
    qkv.join()
    g1, go = finish(others, 1, half_way, 0, 2)
    gq, *vectors = run(
        finish_qkv_kernel,
        "finish_qkv",
        [(code, SMEM), (qkv.near, VMEM), (qkv.far, VMEM)],
        [((3, GROUPS, GD, GD), F32, VMEM)] + [((D,), F32, VMEM)] * 4,
        [pltpu.VMEM((GROUPS, GD, 128), F32)],
        8,
    )
    return (output, grad_input, gq, go.reshape(D, D), g1, jnp.swapaxes(g2, 1, 2)) + tuple(vectors)


def solution(mesh):
    flat = Mesh(mesh.devices.reshape(-1), ("dev",))
    links = Links(mesh.shape["seq"], [[0, 1, 2], [1, 2, 0]])
    upright = Links(mesh.shape["seq"], [[2, 0, 1], [0, 2, 1]])
    split, copied = P("dev"), P()
    return jax.shard_map(
        partial(per_device, links, upright),
        mesh=flat,
        in_specs=(split, split) + (copied,) * 8 + (split,),
        out_specs=(split, split) + (copied,) * 8,
        check_vma=False,
    )
```

```python
from functools import partial

import jax
import jax.numpy as jnp
from jax import lax
from jax.experimental import pallas as pl
from jax.experimental.pallas import tpu as pltpu
from jax.sharding import Mesh, PartitionSpec as P

F32 = jnp.float32
BF16 = jnp.bfloat16
EPSILON = 1e-05
HEADS = 12
HEAD_DIM = 64
D = 768
GROUPS = 4
GD = D // GROUPS
FF = 3072
GF = FF // GROUPS
TOK = 768
BLK = 256
SHORT = 128
EXT = 512
WIDTH = 640
HALF = D // 2
COST = dict(project=3, attend=9, forward=19, backward=6, weights=4, attention=4, through=3, sum=9, finish=3)


def nn(a, b):
    return lax.dot_general(a, b, (((1,), (0,)), ((), ())), preferred_element_type=F32)


def nt(a, b):
    return lax.dot_general(a, b, (((1,), (1,)), ((), ())), preferred_element_type=F32)


def tn(a, b):
    return lax.dot_general(a, b, (((0,), (0,)), ((), ())), preferred_element_type=F32)


def gelu_parts(u):
    a = jnp.abs(u) * 0.7071067811865476
    t = 1.0 / (1.0 + 0.3275911 * a)
    e = jnp.exp(-0.5 * (u * u))
    poly = t * (
        0.254829592
        + t * (-0.284496736 + t * (1.421413741 + t * (-1.453152027 + t * 1.061405429)))
    )
    tail = 0.5 * poly * e
    phi = jnp.where(u < 0, tail, 1.0 - tail)
    return u * phi, phi + u * (e * 0.3989422804014327)


def pipelined(items, first, second, third, lag, last):
    n = len(items)
    for t in range(n + last):
        if t < n:
            first(items[t])
        if 0 <= t - lag < n:
            second(items[t - lag])
        if 0 <= t - last < n:
            third(items[t - last])


def stages(items, first, second, third, lag, last):
    n = len(items)
    for t in range(n + last):
        if t < n:
            first(items[t])
        if 0 <= t - lag < n:
            second(items[t - lag])
        if 0 <= t - last < n:
            third(items[t - last])
        yield


def weave(*streams):
    streams = list(streams)
    while streams:
        for stream in list(streams):
            if next(stream, streams) is streams:
                streams.remove(stream)


def project_kernel(
    seg_ref, x_hbm, ids_hbm, wqkv_hbm,
    xt_ref, q_ref, k_ref, v_ref, bias_ref,
    x_ref, ids_ref, wqkv_ref, sem,
):
    loads = [
        pltpu.make_async_copy(source, ref, sem.at[i])
        for i, (source, ref) in enumerate(((x_hbm, x_ref), (wqkv_hbm, wqkv_ref), (ids_hbm, ids_ref)))
    ]
    for copy in loads:
        copy.start()
    for copy in loads:
        copy.wait()
    two = seg_ref[BLK] == 1
    xt_ref[...] = x_ref[...].T
    for g in range(GROUPS):
        rows = slice(g * GD, (g + 1) * GD)
        xg = xt_ref[rows, :]
        q_ref[rows, :] = (tn(wqkv_ref[0, g], xg).astype(BF16).astype(F32) * 0.125).astype(BF16)
        k_ref[rows, :] = tn(wqkv_ref[1, g], xg).astype(BF16)
        v_ref[rows, :] = tn(wqkv_ref[2, g], xg).astype(BF16)
    row = ids_ref[...].reshape(1, TOK)

    def lanes(b):
        return jnp.broadcast_to(row[:, b * BLK : (b + 1) * BLK], (BLK, BLK))

    def same(kb, qb):
        return jnp.where(lanes(kb).T == lanes(qb), 0.0, -1e30).astype(BF16)

    bias_ref[0, :BLK] = same(1, 1)
    bias_ref[0, BLK:] = jnp.where(two, jnp.zeros((BLK, BLK), BF16), same(2, 1))
    bias_ref[1, :BLK] = same(2, 2)
    bias_ref[1, BLK : BLK + SHORT] = same(1, 2)[SHORT:]


def pick(ref, far_ref, hr, b, two):
    if b == 0:
        other = far_ref[hr, :BLK]
    elif b == 1:
        other = jnp.where(two, far_ref[hr, BLK:], ref[hr, 2 * BLK :])
    else:
        other = ref[hr, BLK + SHORT : 2 * BLK]
    return jnp.concatenate([ref[hr, b * BLK : (b + 1) * BLK], other], 1)


def attend_kernel(
    seg_ref, xp_ref, wqkv_ref, q_ref, k_ref, v_ref, bias_ref,
    kp_ref, vp_ref, ctx_ref, lse_ref,
):
    two = seg_ref[BLK] == 1
    xpt = xp_ref[:EXT, :].T
    for g in range(GROUPS):
        rows = slice(g * GD, (g + 1) * GD)
        kp_ref[rows, :] = tn(wqkv_ref[1, g], xpt[rows]).astype(BF16)
        vp_ref[rows, :] = tn(wqkv_ref[2, g], xpt[rows]).astype(BF16)

    def heads(i, carry):
        items = []
        for u in range(4):
            h = i * 4 + u
            hr = pl.ds(pl.multiple_of(h * HEAD_DIM, HEAD_DIM), HEAD_DIM)
            items += [{"h": h, "hr": hr, "b": b, "qc": slice(b * BLK, (b + 1) * BLK)} for b in range(3)]

        def scores(d):
            s = tn(pick(k_ref, kp_ref, d["hr"], d["b"], two), q_ref[d["hr"], d["qc"]])
            if d["b"]:
                s = s + bias_ref[d["b"] - 1, : s.shape[0]].astype(F32)
            d["s"] = s

        def weights(d):
            s = d.pop("s")
            d["top"] = jnp.max(s, 0, keepdims=True)
            p = jnp.exp(s - d["top"])
            d["total"] = jnp.sum(p, 0, keepdims=True)
            d["p"] = p.astype(BF16)

        def mix(d):
            c = nn(pick(v_ref, vp_ref, d["hr"], d["b"], two), d.pop("p"))
            ctx_ref[d["hr"], d["qc"]] = (c * (1.0 / d["total"])).astype(BF16)
            lse_ref[d["h"], :, d["qc"]] = d["top"] + jnp.log(d["total"])

        pipelined(items, scores, weights, mix, 2, 3)
        return carry

    lax.fori_loop(0, HEADS // 4, heads, 0)


PARTS = [(g, slice(j * BLK, (j + 1) * BLK)) for g in range(GROUPS) for j in range(GF // BLK)]


def columns(ref):
    wide = jnp.broadcast_to(ref[...].reshape(1, D), (128, D)).T
    return jnp.concatenate([wide, wide], 1)


def halves(x):
    return x[:, :128] + x[:, 128:]


def scatter(part, jj, g, keep_ref, send_ref, at, low, far):
    for r in range(4):
        piece = part[48 * r : 48 * (r + 1)].astype(BF16)
        pos = ((g & 1) * 4 + r) ^ (low if jj < 2 else far)
        ref = keep_ref if jj < 2 else send_ref
        ref[pos, at : at + 48] = piece


def forward_kernel(
    code_ref, xt_ref, ctx_ref, wo_ref, w1_ref, w2t_ref, cot_ref, ag_ref, as_ref, fg_ref, fs_ref,
    out_ref, hid_ref, n1_ref, inv1_ref, gpr_ref, gsec_ref, gfeed_ref, keep_ref, send_ref, gvec_ref,
    wot, w1t, act, nb, gacc, held,
):
    core, low, far = code_ref[0], code_ref[3], code_ref[4]
    for j, ref in enumerate((ag_ref, as_ref, fg_ref, fs_ref)):
        nb[j] = columns(ref)
    wot[...] = wo_ref[...].T
    for g in range(GROUPS):
        w1t[g] = w1_ref[g].T
    gacc[...] = jnp.zeros_like(gacc)

    channels = [slice(g * GD, (g + 1) * GD) for g in range(GROUPS)]

    def at(t):
        return pl.ds(pl.multiple_of(t * BLK, BLK), BLK)

    def mean(pieces):
        return sum(jnp.sum(x, 0, keepdims=True) for x in pieces) * (1.0 / D)

    def enter(t):
        tc, r = at(t), []
        for ch in channels:
            r.append(xt_ref[ch, tc].astype(F32) + nn(wot[ch], ctx_ref[:, tc]))
            yield
        average = mean(r)
        centre = [x - average for x in r]
        yield
        inv1 = lax.rsqrt(mean([x * x for x in centre]) + EPSILON)
        inv1_ref[:, tc] = inv1
        yield
        for ch, x in zip(channels, centre):
            n1 = x * inv1
            n1_ref[ch, tc] = n1
            hidden = n1 * nb[0, ch] + nb[1, ch]
            hid_ref[ch, tc] = hidden.astype(BF16)
            held[t & 1, ch] = hidden
            yield

    def middle(t, feeds):
        tc, up = at(t), {}

        def rise(p):
            g, fr = p
            up[g, fr.start] = nn(w1t[g, fr], hid_ref[channels[g], tc])

        def bend(p):
            g, fr = p
            a, slope = gelu_parts(up.pop((g, fr.start)))
            act[g, fr, tc] = a.astype(BF16)
            gpr_ref[g, fr, tc] = slope.astype(BF16)

        def fall(p):
            if p[1].stop == GF:
                feeds.append(nn(w2t_ref[p[0]], act[p[0], :, tc]))

        yield from stages(PARTS, rise, bend, fall, 2, 3)

    def leave(t, feeds):
        tc = at(t)
        r2 = [held[t & 1, ch] + x for ch, x in zip(channels, feeds)]
        average = mean(r2)
        centre = [x - average for x in r2]
        yield
        inv2 = lax.rsqrt(mean([x * x for x in centre]) + EPSILON)
        yield
        n2, low = [], []
        for ch, x in zip(channels, centre):
            n2.append(x * inv2)
            low.append((n2[-1] * nb[2, ch] + nb[3, ch]).astype(BF16))
            yield
        out_ref[tc, :] = jnp.concatenate(low, 0).T
        turned = cot_ref[tc, :].T
        yield
        cg = []
        for ch, n in zip(channels, n2):
            c = turned[ch].astype(F32)
            gacc[0, ch] += halves(c * n)
            gacc[1, ch] += halves(c)
            cg.append(c * nb[2, ch])
            yield
        first = mean(cg)
        second = mean([x * n for x, n in zip(cg, n2)])
        yield
        for ch, x, n in zip(channels, cg, n2):
            gsec = inv2 * (x - first - n * second)
            gsec_ref[ch, tc] = gsec
            gfeed_ref[ch, tc] = gsec.astype(BF16)
            yield

    def tile(t, carry):
        feeds = []
        weave(middle(t, feeds), enter(jnp.minimum(t + 1, TOK // BLK - 1)))
        weave(leave(t, feeds))
        return carry

    weave(enter(0))
    lax.fori_loop(0, TOK // BLK, tile, 0)
    for j in range(2):
        gvec_ref[:, j : j + 1] = jnp.sum(gacc[j], 1, keepdims=True)
    for jj in (2, 3, 0, 1):
        g = jj ^ (2 * core)
        gr = pl.ds(pl.multiple_of(g * GD, GD), GD)
        scatter(nt(gfeed_ref[gr, :], act[g]), jj, g, keep_ref, send_ref, 0, low, far)


def backward_kernel(
    wo_ref, w1_ref, w2t_ref, n1_ref, inv1_ref, gpr_ref, gsec_ref, gfeed_ref, ag_ref,
    gctx_ref, gfirst_ref, gup, gatt, gvec_ref,
    w2, nb, gacc,
):
    nb[...] = columns(ag_ref)
    for g in range(GROUPS):
        w2[g] = w2t_ref[g].T
    gacc[...] = jnp.zeros_like(gacc)

    def tile(t, carry):
        tc = pl.ds(pl.multiple_of(t * BLK, BLK), BLK)
        back, gh = {}, []

        def lift(p):
            g, fr = p
            back[g, fr.start] = nn(w2[g, fr], gfeed_ref[g * GD : (g + 1) * GD, tc])

        def scale(p):
            g, fr = p
            gup[g, fr, tc] = (back.pop((g, fr.start)) * gpr_ref[g, fr, tc].astype(F32)).astype(BF16)

        def drop(p):
            if p[1].stop == GF:
                gh.append(nn(w1_ref[p[0]], gup[p[0], :, tc]))

        pipelined(PARTS, lift, scale, drop, 2, 3)
        ghid = gsec_ref[:, tc] + jnp.concatenate(gh, 0)
        n1 = n1_ref[:, tc]
        gacc[0] += halves(ghid * n1)
        gacc[1] += halves(ghid)
        sc = ghid * nb[...]
        gfirst = inv1_ref[:, tc] * (
            sc - jnp.mean(sc, 0, keepdims=True) - n1 * jnp.mean(sc * n1, 0, keepdims=True)
        )
        gfirst_ref[:, tc] = gfirst
        gatt[:, tc] = gfirst.astype(BF16)
        gctx_ref[:, tc] = nn(wo_ref[...], gatt[:, tc]).astype(BF16)
        return carry

    lax.fori_loop(0, TOK // BLK, tile, 0)
    for j in range(2):
        gvec_ref[:, j : j + 1] = jnp.sum(gacc[j], 1, keepdims=True)


def weights_kernel(code_ref, ctx_ref, hid_ref, gup_ref, gatt_ref, keep_ref, send_ref):
    core, low, far = code_ref[0], code_ref[1], code_ref[2]
    for jj in (2, 3, 0, 1):
        g = jj ^ (2 * core)
        gr = pl.ds(pl.multiple_of(g * GD, GD), GD)
        scatter(nt(hid_ref[gr, :], gup_ref[g]), jj, g, keep_ref, send_ref, 0, low, far)
        scatter(nt(ctx_ref[gr, :], gatt_ref[...]), jj, g, keep_ref, send_ref, 48, low, far)


def back_kernel(
    seg_ref, q_ref, k_ref, v_ref, kp_ref, vp_ref, gctx_ref, lse_ref, bias_ref,
    dq_ref, dk_ref, dv_ref, far_ref, dk, dv,
):
    two = seg_ref[BLK] == 1
    scale = jnp.where(two, 1.0, 0.0)
    dk[...] = jnp.zeros_like(dk)
    dv[...] = jnp.zeros_like(dv)

    items = []
    for h in range(3):
        hr = slice(h * HEAD_DIM, (h + 1) * HEAD_DIM)
        items += [{"h": h, "hr": hr, "b": b, "qc": slice(b * BLK, (b + 1) * BLK)} for b in range(3)]

    def scores(d):
        hr, qc, b = d["hr"], d["qc"], d["b"]
        s = tn(pick(k_ref, kp_ref, hr, b, two), q_ref[hr, qc])
        if b:
            s = s + bias_ref[b - 1, : s.shape[0]].astype(F32)
        d["s"] = s
        d["dp"] = tn(pick(v_ref, vp_ref, hr, b, two), gctx_ref[hr, qc])

    def weights(d):
        p = jnp.exp(d.pop("s") - lse_ref[d["h"], :, d["qc"]])
        dp = d.pop("dp")
        dots = jnp.sum(p * dp, 0, keepdims=True)
        d["ds"] = (p * (dp - dots)).astype(BF16)
        d["p"] = p.astype(BF16)

    def mix(d):
        hr, qc, b = d["hr"], d["qc"], d["b"]
        ds = d.pop("ds")
        dq_ref[hr, qc] = (nn(pick(k_ref, kp_ref, hr, b, two), ds) * 0.125).astype(BF16)
        gk = nt(q_ref[hr, qc], ds)
        gv = nt(gctx_ref[hr, qc], d.pop("p"))
        for acc, grad, slot in ((dk, gk, 0), (dv, gv, 1)):
            acc[hr, qc] += grad[:, :BLK]
            other = grad[:, BLK:]
            if b == 0:
                far_ref[slot, hr, :BLK] = other.astype(BF16)
            elif b == 1:
                far_ref[slot, hr, BLK:] = (other * scale).astype(BF16)
                acc[hr, 2 * BLK :] += other * (1.0 - scale)
            else:
                acc[hr, BLK + SHORT : 2 * BLK] += other

    pipelined(items, scores, weights, mix, 1, 2)
    dk_ref[...] = dk[...]
    dv_ref[...] = dv[...]


def through_kernel(
    code_ref, xt_ref, dqa_ref, dka_ref, dva_ref, ba_ref, dqb_ref, dkb_ref, dvb_ref, bb_ref, wqkv_ref,
    gfirst_ref, gvec1_ref, gvec2_ref, *refs, half,
):
    core = code_ref[0]
    order = jnp.where(core == half, code_ref[1], code_ref[2])
    if half:
        first_ref, _, gin_ref, keep_ref, send_ref, piece_ref = refs
    else:
        gin_ref, piece_ref = refs
    through = []
    groups = ((dqa_ref, dka_ref, dva_ref, ba_ref), (dqb_ref, dkb_ref, dvb_ref, bb_ref))
    for i, (dq_ref, dk_ref, dv_ref, b_ref) in enumerate(groups):
        rows = slice(i * GD, (i + 1) * GD)
        grads = [dq_ref[...]]
        for slot, ref in ((0, dk_ref), (1, dv_ref)):
            own = ref[...]
            own = jnp.concatenate([own[:, :EXT] + b_ref[slot].astype(F32), own[:, EXT:]], 1)
            grads.append(own.astype(BF16))
        through.append(sum(nn(wqkv_ref[t, i], grads[t]) for t in range(3)))
        row = jnp.concatenate(
            [nt(xt_ref[rows], grad) for grad in grads]
            + [gvec1_ref[rows], gvec2_ref[rows], jnp.zeros((GD, WIDTH - 3 * GD - 4), F32)],
            1,
        )
        for r in range(4):
            piece_ref[(i * 4 + r) ^ order] = row[48 * r : 48 * (r + 1)]
    if half:
        mine, other = piece_ref[...], first_ref[...]
        keep_ref[...] = jnp.where(core == 1, mine, other)
        send_ref[...] = jnp.where(core == 1, other, mine).astype(BF16)
    gin_ref[...] = (gfirst_ref[...] + jnp.concatenate(through, 0)).astype(BF16).T


def chunks(code_ref, near_ref, far_ref):
    core, low, far = code_ref[0], code_ref[1], code_ref[2]
    for other, ref in ((0, near_ref), (1, far_ref)):
        for a in range(8):
            g = (other ^ core) * 2 + a // 4
            rows = slice(48 * (a % 4), 48 * (a % 4 + 1))
            yield g, rows, ref[a ^ (far if other else low)].astype(F32)


def finish_kernel(code_ref, half_ref, *refs, far, way, outs):
    *refs, token_ref = refs
    token_ref[...] = jnp.zeros_like(token_ref)
    order = code_ref[1 + 2 * way + far]
    for a in range(8):
        part = half_ref[a ^ order].astype(F32)
        rows = slice(48 * (a % 4), 48 * (a % 4 + 1))
        for i, ref in enumerate(refs[-outs:]):
            ref[a // 4, rows] = part[48 * i : 48 * (i + 1)]


def finish_qkv_kernel(code_ref, near_ref, far_ref, gq_ref, ag_ref, as_ref, fg_ref, fs_ref, vec):
    for g, rows, part in chunks(code_ref, near_ref, far_ref):
        for t in range(3):
            gq_ref[t, g, rows] = part[:, t * GD : (t + 1) * GD]
        vec[g, rows] = part[:, 512:640]
    turned = vec[...].reshape(D, 128).T
    for i, ref in enumerate((ag_ref, as_ref, fg_ref, fs_ref)):
        ref[...] = turned[64 + i : 65 + i].reshape(D)


def fold_kernel(keep_ref, came_ref, kept_ref, send_ref):
    n = kept_ref.shape[0]
    kept_ref[...] = keep_ref[:n].astype(F32) + came_ref[:n].astype(F32)
    send_ref[...] = (keep_ref[n:].astype(F32) + came_ref[n:].astype(F32)).astype(BF16)


def meet_kernel(*refs):
    *ins, out_ref = refs
    at = 0
    for keep_ref, came_ref in zip(ins[::2], ins[1::2]):
        rows = keep_ref.shape[1]
        out_ref[:, at : at + rows] = (keep_ref[...].astype(F32) + came_ref[...].astype(F32)).astype(BF16)
        at += rows


def join_kernel(near_ref, far_ref, out_ref):
    n = near_ref.shape[0]
    out_ref[:n] = near_ref[...]
    out_ref[n:] = far_ref[...]


SMEM = pl.BlockSpec(memory_space=pltpu.SMEM)
VMEM = pl.BlockSpec(memory_space=pltpu.VMEM)
ANY = pl.BlockSpec(memory_space=pl.ANY)


class Steps:
    def __init__(self):
        self.last = None

    def __call__(self, kernel, name, ins, outs, scratch, limit, grid=(), code=None, aliases=None):
        n, free = len(ins) + (code is not None), self.last is None
        if not free:
            ins = ins + [(self.last, ANY)]
        specs = dict(
            grid=grid,
            in_specs=[spec for _, spec in ins],
            out_specs=[spec for _, _, spec in outs],
            scratch_shapes=scratch,
        )
        if code is not None:
            specs = dict(grid_spec=pltpu.PrefetchScalarGridSpec(num_scalar_prefetch=1, **specs))
        results = pl.pallas_call(
            kernel if free else lambda *refs: kernel(*refs[:n], *refs[n + 1 :]),
            out_shape=[jax.ShapeDtypeStruct(s, d) for s, d, _ in outs],
            compiler_params=pltpu.CompilerParams(vmem_limit_bytes=limit << 20),
            cost_estimate=pl.CostEstimate(flops=int(COST[name.split('_')[0]] * 1e9), bytes_accessed=1024, transcendentals=0),
            input_output_aliases=aliases or {},
            name=name,
            **specs,
        )(*([] if code is None else [code]), *[array for array, _ in ins])
        self.last = results[-1]
        return results


def block(shape, *at):
    return pl.BlockSpec(shape, lambda _: at)


class Links:
    def __init__(self, n_seq, orders):
        bits = n_seq.bit_length() - 1
        self.n = n_seq * 2
        self.orders = [order + list(range(3, bits)) for order in orders]
        self.bits = bits

    def pairs(self, step):
        if step < 0:
            return [(i, i ^ 1) for i in range(self.n)]
        return [(i, i ^ (2 << self.orders[i & 1][step])) for i in range(self.n)]

    def code(self, seq, core):
        first, second = [sum(((seq >> order[step]) & 1) << (2 - step) for step in range(3)) for order in self.orders]
        return jnp.where(core == 0, first, second)


def swap(x, links, step):
    return lax.ppermute(x, "dev", links.pairs(step))


class Total:
    def __init__(self, run, links, name, keep, came):
        self.run, self.links, self.name = run, links, name
        self.keep, self.came = keep, came
        self.step = 0

    def small(self, kernel, ins, outs):
        spec = [(x, VMEM) for x in ins]
        return self.run(kernel, self.name, spec, [o + (VMEM,) for o in outs], [], 4)

    def fold(self):
        shape = (self.keep.shape[0] // 2,) + self.keep.shape[1:]
        self.keep, send = self.small(fold_kernel, [self.keep, self.came], [(shape, F32), (shape, BF16)])
        self.came = swap(send, self.links, self.step)
        self.step += 1

    def meet(self, *others):
        parts = [*others, self]
        shape = (1, sum(p.keep.shape[1] for p in parts), self.keep.shape[2])
        ins = [x for p in parts for x in (p.keep, p.came)]
        (self.near,) = self.small(meet_kernel, ins, [(shape, BF16)])
        for step in range(3, self.links.bits - 1):
            (self.near,) = self.small(meet_kernel, [self.near, swap(self.near, self.links, step)], [(shape, BF16)])
        self.far = swap(self.near, self.links, self.links.bits - 1)

    def whole(self):
        (self.near,) = self.small(meet_kernel, [self.near, self.far], [(self.near.shape, BF16)])
        self.step = 2
        self.far = swap(self.near, self.links, self.step)

    def join(self):
        shape = (self.near.shape[0] * 2,) + self.near.shape[1:]
        (self.near,) = self.small(join_kernel, [self.near, self.far], [(shape, BF16)])
        self.step -= 1
        self.far = swap(self.near, self.links, self.step)


def per_device(
    links, upright, inputs, segment_ids, qkv_weight, out_weight, ffn_in_weight, ffn_out_weight,
    attn_gain, attn_shift, ffn_gain, ffn_shift, out_cotangent,
):
    me = lax.axis_index("dev")
    seq, core = me >> 1, me & 1
    codes = [core]
    for way in (links, upright):
        codes += [way.code(seq, core), way.code(seq, 1 - core)]
    code = jnp.stack(codes).astype(jnp.int32)
    partner = swap(inputs, links, -1)
    square = (D, TOK)
    large = (GROUPS, GF, TOK)
    run = Steps()
    xt, q, k, v, bias = run(
        project_kernel,
        "project",
        [(segment_ids, SMEM), (inputs, ANY), (segment_ids, ANY), (qkv_weight, ANY)],
        [(square, BF16, VMEM)] * 4 + [((2, 2 * BLK, BLK), BF16, VMEM)],
        [
            pltpu.VMEM((TOK, D), BF16), pltpu.VMEM((TOK,), jnp.int32), pltpu.VMEM((3, GROUPS, GD, GD), BF16),
            pltpu.SemaphoreType.DMA((3,)),
        ],
        12,
    )
    kp, vp, ctx, lse = run(
        attend_kernel,
        "attend",
        [(segment_ids, SMEM), (partner, VMEM), (qkv_weight, VMEM), (q, VMEM), (k, VMEM), (v, VMEM), (bias, VMEM)],
        [((D, EXT), BF16, VMEM), ((D, EXT), BF16, VMEM), (square, BF16, VMEM), ((HEADS, 1, TOK), F32, VMEM)],
        [],
        12,
    )
    weight2t = jnp.swapaxes(ffn_out_weight, 1, 2)
    output, hid, n1, inv1, gpr, gsec, gfeed, keep, send, gvec2 = run(
        forward_kernel,
        "forward",
        [(code, SMEM), (xt, VMEM), (ctx, VMEM), (out_weight, VMEM), (ffn_in_weight, VMEM), (weight2t, VMEM)]
        + [(out_cotangent, VMEM), (attn_gain, VMEM), (attn_shift, VMEM), (ffn_gain, VMEM), (ffn_shift, VMEM)],
        [((TOK, D), BF16, VMEM), (square, BF16, VMEM), (square, F32, VMEM), ((1, TOK), F32, VMEM), (large, BF16, VMEM)]
        + [(square, F32, VMEM), (square, BF16, VMEM), ((8, 48, D), BF16, VMEM), ((8, 48, D), BF16, VMEM)]
        + [((D, 2), F32, VMEM)],
        [
            pltpu.VMEM((D, D), BF16), pltpu.VMEM((GROUPS, GF, GD), BF16), pltpu.VMEM(large, BF16),
            pltpu.VMEM((4, D, BLK), F32), pltpu.VMEM((2, D, 128), F32), pltpu.VMEM((2, D, BLK), F32),
        ],
        20,
    )
    ffn_out = Total(run, upright, "sum_ffn_out", keep, swap(send, links, -1))
    gctx, gfirst, gup, gatt, gvec1 = run(
        backward_kernel,
        "backward",
        [(out_weight, VMEM), (ffn_in_weight, VMEM), (weight2t, VMEM)]
        + [(n1, VMEM), (inv1, VMEM), (gpr, VMEM), (gsec, VMEM), (gfeed, VMEM), (attn_gain, VMEM)],
        [(square, BF16, VMEM), (square, F32, VMEM), (large, BF16, VMEM), (square, BF16, VMEM), ((D, 2), F32, VMEM)],
        [pltpu.VMEM((GROUPS, GF, GD), BF16), pltpu.VMEM((D, BLK), F32), pltpu.VMEM((2, D, 128), F32)],
        12,
    )
    ffn_out.fold()
    message = ((8, 96, D), BF16, VMEM)
    keep, send = run(
        weights_kernel,
        "weights",
        [(code, SMEM), (ctx, VMEM), (hid, VMEM), (gup, VMEM), (gatt, VMEM)],
        [message, message],
        [],
        12,
    )
    others = Total(run, links, "sum_others", keep, swap(send, links, -1))

    def attention_back(g):
        rows = partial(lambda width: block((GD, width), g, 0))
        return run(
            back_kernel,
            "attention_back",
            [(segment_ids, SMEM), (q, rows(TOK)), (k, rows(TOK)), (v, rows(TOK)), (kp, rows(EXT)), (vp, rows(EXT))]
            + [(gctx, rows(TOK)), (lse, block((3, 1, TOK), g, 0, 0)), (bias, VMEM)],
            [((GD, TOK), BF16, VMEM), ((GD, TOK), F32, VMEM), ((GD, TOK), F32, VMEM), ((2, GD, EXT), BF16, VMEM)],
            [pltpu.VMEM((GD, TOK), F32), pltpu.VMEM((GD, TOK), F32)],
            10,
            (1,),
        )

    def through(half, parts, first):
        ins = [(code, SMEM), (xt, block((HALF, TOK), half, 0))]
        for dq, dk, dv, far in parts:
            ins += [(dq, VMEM), (dk, VMEM), (dv, VMEM), (swap(far, links, -1), VMEM)]
        ins += [(qkv_weight, block((3, 2, GD, GD), 0, half, 0, 0))]
        ins += [(gfirst, block((HALF, TOK), half, 0)), (gvec1, block((HALF, 2), half, 0))]
        ins += [(gvec2, block((HALF, 2), half, 0))]
        shape = (8, 48, WIDTH)
        outs = [((TOK, D), BF16, block((TOK, HALF), 0, half))]
        if half:
            ins += [(first[1], VMEM), (first[0], ANY)]
            outs += [(shape, F32, VMEM), (shape, BF16, VMEM)]
        else:
            outs += [(shape, F32, VMEM)]
        return run(
            partial(through_kernel, half=half),
            "through_qkv",
            ins,
            outs,
            [pltpu.VMEM(shape, F32)] if half else [],
            10,
            (1,),
            None,
            {len(ins) - 1: 0} if half else None,
        )

    rows = (GROUPS, GD, D)

    def finish(total, far, into, way, n):
        def half(c):
            return (c[0] ^ far, 0, 0)

        outs = [(rows, F32, pl.BlockSpec((2, GD, D), lambda _, c: half(c)))] * n
        outs += [((8, 128), F32, pl.BlockSpec((8, 128), lambda _, c: (0, 0)))]
        ins = [(total.far if far else total.near, pl.BlockSpec((8, 48 * n, D), lambda _, c: (0, 0, 0)))]
        ins += [(x, ANY) for x in into]
        kernel = partial(finish_kernel, far=far, way=way, outs=n)
        return run(kernel, "finish", ins, outs, [], 12, (1,), code, {2 + i: i for i in range(len(into))})[:n]

    parts = [attention_back(0)]
    ffn_out.fold()
    others.fold()
    parts += [attention_back(1)]
    ffn_out.fold()
    parts += [attention_back(2)]
    others.fold()
    first = through(0, parts[:2], None)
    ffn_out.meet()
    parts += [attention_back(3)]
    others.fold()
    grad_input, keep, send = through(1, parts[2:], first)
    others.meet()
    qkv = Total(run, links, "sum_qkv", keep, swap(send, links, -1))
    qkv.fold()
    ffn_out.whole()
    ffn_out.join()
    qkv.fold()
    others.whole()
    qkv.fold()
    others.join()
    qkv.meet()
    ffn_out.join()
    others.join()
    qkv.whole()
    ffn_out.join()
    qkv.join()
    near_out = finish(ffn_out, 0, [], 1, 1)
    qkv.join()
    others.join()
    (g2,) = finish(ffn_out, 1, near_out, 1, 1)
    half_way = finish(others, 0, [], 0, 2)
    qkv.join()
    g1, go = finish(others, 1, half_way, 0, 2)
    gq, *vectors = run(
        finish_qkv_kernel,
        "finish_qkv",
        [(code, SMEM), (qkv.near, VMEM), (qkv.far, VMEM)],
        [((3, GROUPS, GD, GD), F32, VMEM)] + [((D,), F32, VMEM)] * 4,
        [pltpu.VMEM((GROUPS, GD, 128), F32)],
        8,
    )
    return (output, grad_input, gq, go.reshape(D, D), g1, jnp.swapaxes(g2, 1, 2)) + tuple(vectors)


def solution(mesh):
    flat = Mesh(mesh.devices.reshape(-1), ("dev",))
    links = Links(mesh.shape["seq"], [[0, 1, 2], [1, 2, 0]])
    upright = Links(mesh.shape["seq"], [[2, 0, 1], [0, 2, 1]])
    split, copied = P("dev"), P()
    return jax.shard_map(
        partial(per_device, links, upright),
        mesh=flat,
        in_specs=(split, split) + (copied,) * 8 + (split,),
        out_specs=(split, split) + (copied,) * 8,
        check_vma=False,
    )
```

```python
from functools import partial

import jax
import jax.numpy as jnp
from jax import lax
from jax.experimental import pallas as pl
from jax.experimental.pallas import tpu as pltpu
from jax.sharding import Mesh, PartitionSpec as P

F32 = jnp.float32
BF16 = jnp.bfloat16
EPSILON = 1e-05
HEADS = 12
HEAD_DIM = 64
D = 768
GROUPS = 4
GD = D // GROUPS
FF = 3072
GF = FF // GROUPS
TOK = 768
BLK = 256
SHORT = 128
EXT = 512
WIDTH = 640
HALF = D // 2
COST = dict(project=3, attend=9, forward=19, backward=6, weights=4, attention=4, through=3, sum=9, finish=3)


def nn(a, b):
    return lax.dot_general(a, b, (((1,), (0,)), ((), ())), preferred_element_type=F32)


def nt(a, b):
    return lax.dot_general(a, b, (((1,), (1,)), ((), ())), preferred_element_type=F32)


def tn(a, b):
    return lax.dot_general(a, b, (((0,), (0,)), ((), ())), preferred_element_type=F32)


def gelu_parts(u):
    a = jnp.abs(u) * 0.7071067811865476
    t = 1.0 / (1.0 + 0.3275911 * a)
    e = jnp.exp(-0.5 * (u * u))
    poly = t * (
        0.254829592
        + t * (-0.284496736 + t * (1.421413741 + t * (-1.453152027 + t * 1.061405429)))
    )
    tail = 0.5 * poly * e
    phi = jnp.where(u < 0, tail, 1.0 - tail)
    return u * phi, phi + u * (e * 0.3989422804014327)


def pipelined(items, first, second, third, lag, last):
    n = len(items)
    for t in range(n + last):
        if t < n:
            first(items[t])
        if 0 <= t - lag < n:
            second(items[t - lag])
        if 0 <= t - last < n:
            third(items[t - last])


def stages(items, first, second, third, lag, last):
    n = len(items)
    for t in range(n + last):
        if t < n:
            first(items[t])
        if 0 <= t - lag < n:
            second(items[t - lag])
        if 0 <= t - last < n:
            third(items[t - last])
        yield


def weave(*streams):
    streams = list(streams)
    while streams:
        for stream in list(streams):
            if next(stream, streams) is streams:
                streams.remove(stream)


def project_kernel(x_ref, wqkv_ref, xt_ref, q_ref, k_ref, v_ref):
    xt_ref[...] = x_ref[...].T
    for g in range(GROUPS):
        rows = slice(g * GD, (g + 1) * GD)
        xg = xt_ref[rows, :]
        q_ref[rows, :] = (tn(wqkv_ref[0, g], xg).astype(BF16).astype(F32) * 0.125).astype(BF16)
        k_ref[rows, :] = tn(wqkv_ref[1, g], xg).astype(BF16)
        v_ref[rows, :] = tn(wqkv_ref[2, g], xg).astype(BF16)


def pick(ref, far_ref, hr, b, two):
    if b == 0:
        other = far_ref[hr, :BLK]
    elif b == 1:
        other = jnp.where(two, far_ref[hr, BLK:], ref[hr, 2 * BLK :])
    else:
        other = ref[hr, BLK + SHORT : 2 * BLK]
    return jnp.concatenate([ref[hr, b * BLK : (b + 1) * BLK], other], 1)


def attend_kernel(
    seg_ref, ids_ref, xp_ref, wqkv_ref, q_ref, k_ref, v_ref,
    kp_ref, vp_ref, ctx_ref, lse_ref, bias_ref,
):
    two = seg_ref[BLK] == 1
    row = ids_ref[...].reshape(1, TOK)

    def lanes(b):
        return jnp.broadcast_to(row[:, b * BLK : (b + 1) * BLK], (BLK, BLK))

    def same(kb, qb):
        return jnp.where(lanes(kb).T == lanes(qb), 0.0, -1e30).astype(BF16)

    bias_ref[0, :BLK] = same(1, 1)
    bias_ref[0, BLK:] = jnp.where(two, jnp.zeros((BLK, BLK), BF16), same(2, 1))
    bias_ref[1, :BLK] = same(2, 2)
    bias_ref[1, BLK : BLK + SHORT] = same(1, 2)[SHORT:]
    xpt = xp_ref[:EXT, :].T
    for g in range(GROUPS):
        rows = slice(g * GD, (g + 1) * GD)
        kp_ref[rows, :] = tn(wqkv_ref[1, g], xpt[rows]).astype(BF16)
        vp_ref[rows, :] = tn(wqkv_ref[2, g], xpt[rows]).astype(BF16)

    def heads(i, carry):
        items = []
        for u in range(6):
            h = i * 6 + u
            hr = pl.ds(pl.multiple_of(h * HEAD_DIM, HEAD_DIM), HEAD_DIM)
            items += [{"h": h, "hr": hr, "b": b, "qc": slice(b * BLK, (b + 1) * BLK)} for b in range(3)]

        def scores(d):
            s = tn(pick(k_ref, kp_ref, d["hr"], d["b"], two), q_ref[d["hr"], d["qc"]])
            if d["b"]:
                s = s + bias_ref[d["b"] - 1, : s.shape[0]].astype(F32)
            d["s"] = s

        def weights(d):
            s = d.pop("s")
            d["top"] = jnp.max(s, 0, keepdims=True)
            p = jnp.exp(s - d["top"])
            d["total"] = jnp.sum(p, 0, keepdims=True)
            d["p"] = p.astype(BF16)

        def mix(d):
            c = nn(pick(v_ref, vp_ref, d["hr"], d["b"], two), d.pop("p"))
            ctx_ref[d["hr"], d["qc"]] = (c * (1.0 / d["total"])).astype(BF16)
            lse_ref[d["h"], :, d["qc"]] = d["top"] + jnp.log(d["total"])

        pipelined(items, scores, weights, mix, 2, 3)
        return carry

    lax.fori_loop(0, HEADS // 6, heads, 0)


PARTS = [(g, slice(j * BLK, (j + 1) * BLK)) for g in range(GROUPS) for j in range(GF // BLK)]


def columns(ref):
    wide = jnp.broadcast_to(ref[...].reshape(1, D), (128, D)).T
    return jnp.concatenate([wide, wide], 1)


def halves(x):
    return x[:, :128] + x[:, 128:]


def scatter(part, jj, g, keep_ref, send_ref, at, low, far):
    for r in range(4):
        piece = part[48 * r : 48 * (r + 1)].astype(BF16)
        pos = ((g & 1) * 4 + r) ^ (low if jj < 2 else far)
        ref = keep_ref if jj < 2 else send_ref
        ref[pos, at : at + 48] = piece


def forward_kernel(
    code_ref, xt_ref, ctx_ref, wo_ref, w1_ref, w2t_ref, cot_ref, ag_ref, as_ref, fg_ref, fs_ref,
    out_ref, hid_ref, n1_ref, inv1_ref, gpr_ref, gsec_ref, gfeed_ref, keep_ref, send_ref, gvec_ref,
    wot, w1t, act, nb, gacc, held,
):
    core, low, far = code_ref[0], code_ref[3], code_ref[4]
    for j, ref in enumerate((ag_ref, as_ref, fg_ref, fs_ref)):
        nb[j] = columns(ref)
    wot[...] = wo_ref[...].T
    for g in range(GROUPS):
        w1t[g] = w1_ref[g].T
    gacc[...] = jnp.zeros_like(gacc)

    channels = [slice(g * GD, (g + 1) * GD) for g in range(GROUPS)]

    def at(t):
        return pl.ds(pl.multiple_of(t * BLK, BLK), BLK)

    def mean(pieces):
        return sum(jnp.sum(x, 0, keepdims=True) for x in pieces) * (1.0 / D)

    def enter(t):
        tc, r = at(t), []
        for ch in channels:
            r.append(xt_ref[ch, tc].astype(F32) + nn(wot[ch], ctx_ref[:, tc]))
            yield
        average = mean(r)
        centre = [x - average for x in r]
        yield
        inv1 = lax.rsqrt(mean([x * x for x in centre]) + EPSILON)
        inv1_ref[:, tc] = inv1
        yield
        for ch, x in zip(channels, centre):
            n1 = x * inv1
            n1_ref[ch, tc] = n1
            hidden = n1 * nb[0, ch] + nb[1, ch]
            hid_ref[ch, tc] = hidden.astype(BF16)
            held[t & 1, ch] = hidden
            yield

    def middle(t, feeds):
        tc, up = at(t), {}

        def rise(p):
            g, fr = p
            up[g, fr.start] = nn(w1t[g, fr], hid_ref[channels[g], tc])

        def bend(p):
            g, fr = p
            a, slope = gelu_parts(up.pop((g, fr.start)))
            act[g, fr, tc] = a.astype(BF16)
            gpr_ref[g, fr, tc] = slope.astype(BF16)

        def fall(p):
            if p[1].stop == GF:
                feeds.append(nn(w2t_ref[p[0]], act[p[0], :, tc]))

        yield from stages(PARTS, rise, bend, fall, 2, 3)

    def leave(t, feeds):
        tc = at(t)
        r2 = [held[t & 1, ch] + x for ch, x in zip(channels, feeds)]
        average = mean(r2)
        centre = [x - average for x in r2]
        yield
        inv2 = lax.rsqrt(mean([x * x for x in centre]) + EPSILON)
        yield
        n2, low = [], []
        for ch, x in zip(channels, centre):
            n2.append(x * inv2)
            low.append((n2[-1] * nb[2, ch] + nb[3, ch]).astype(BF16))
            yield
        out_ref[tc, :] = jnp.concatenate(low, 0).T
        turned = cot_ref[tc, :].T
        yield
        cg = []
        for ch, n in zip(channels, n2):
            c = turned[ch].astype(F32)
            gacc[0, ch] += halves(c * n)
            gacc[1, ch] += halves(c)
            cg.append(c * nb[2, ch])
            yield
        first = mean(cg)
        second = mean([x * n for x, n in zip(cg, n2)])
        yield
        for ch, x, n in zip(channels, cg, n2):
            gsec = inv2 * (x - first - n * second)
            gsec_ref[ch, tc] = gsec
            gfeed_ref[ch, tc] = gsec.astype(BF16)
            yield

    def tile(t, carry):
        feeds = []
        weave(middle(t, feeds), enter(jnp.minimum(t + 1, TOK // BLK - 1)))
        weave(leave(t, feeds))
        return carry

    weave(enter(0))
    lax.fori_loop(0, TOK // BLK, tile, 0)
    for j in range(2):
        gvec_ref[:, j : j + 1] = jnp.sum(gacc[j], 1, keepdims=True)
    for jj in (2, 3, 0, 1):
        g = jj ^ (2 * core)
        gr = pl.ds(pl.multiple_of(g * GD, GD), GD)
        scatter(nt(gfeed_ref[gr, :], act[g]), jj, g, keep_ref, send_ref, 0, low, far)


def backward_kernel(
    wo_ref, w1_ref, w2t_ref, n1_ref, inv1_ref, gpr_ref, gsec_ref, gfeed_ref, ag_ref,
    gctx_ref, gfirst_ref, gup, gatt, gvec_ref,
    w2, nb, gacc,
):
    nb[...] = columns(ag_ref)
    for g in range(GROUPS):
        w2[g] = w2t_ref[g].T
    gacc[...] = jnp.zeros_like(gacc)

    def tile(t, carry):
        tc = pl.ds(pl.multiple_of(t * BLK, BLK), BLK)
        back, gh = {}, []

        def lift(p):
            g, fr = p
            back[g, fr.start] = nn(w2[g, fr], gfeed_ref[g * GD : (g + 1) * GD, tc])

        def scale(p):
            g, fr = p
            gup[g, fr, tc] = (back.pop((g, fr.start)) * gpr_ref[g, fr, tc].astype(F32)).astype(BF16)

        def drop(p):
            if p[1].stop == GF:
                gh.append(nn(w1_ref[p[0]], gup[p[0], :, tc]))

        pipelined(PARTS, lift, scale, drop, 2, 3)
        ghid = gsec_ref[:, tc] + jnp.concatenate(gh, 0)
        n1 = n1_ref[:, tc]
        gacc[0] += halves(ghid * n1)
        gacc[1] += halves(ghid)
        sc = ghid * nb[...]
        gfirst = inv1_ref[:, tc] * (
            sc - jnp.mean(sc, 0, keepdims=True) - n1 * jnp.mean(sc * n1, 0, keepdims=True)
        )
        gfirst_ref[:, tc] = gfirst
        gatt[:, tc] = gfirst.astype(BF16)
        gctx_ref[:, tc] = nn(wo_ref[...], gatt[:, tc]).astype(BF16)
        return carry

    lax.fori_loop(0, TOK // BLK, tile, 0)
    for j in range(2):
        gvec_ref[:, j : j + 1] = jnp.sum(gacc[j], 1, keepdims=True)


def weights_kernel(code_ref, ctx_ref, hid_ref, gup_ref, gatt_ref, keep_ref, send_ref):
    core, low, far = code_ref[0], code_ref[1], code_ref[2]
    for jj in (2, 3, 0, 1):
        g = jj ^ (2 * core)
        gr = pl.ds(pl.multiple_of(g * GD, GD), GD)
        scatter(nt(hid_ref[gr, :], gup_ref[g]), jj, g, keep_ref, send_ref, 0, low, far)
        if jj & 1 == 0:
            rows = pl.ds(pl.multiple_of((jj // 2 ^ core) * HALF, HALF), HALF)
            both = nt(ctx_ref[rows, :], gatt_ref[...])
        mine = both[:GD] if jj & 1 == 0 else both[GD:]
        scatter(mine, jj, g, keep_ref, send_ref, 48, low, far)


def back_kernel(
    seg_ref, q_ref, k_ref, v_ref, kp_ref, vp_ref, gctx_ref, lse_ref, bias_ref,
    dq_ref, dk_ref, dv_ref, far_ref, dk, dv,
):
    two = seg_ref[BLK] == 1
    scale = jnp.where(two, 1.0, 0.0)
    dk[...] = jnp.zeros_like(dk)
    dv[...] = jnp.zeros_like(dv)

    items = []
    for h in range(3):
        hr = slice(h * HEAD_DIM, (h + 1) * HEAD_DIM)
        items += [{"h": h, "hr": hr, "b": b, "qc": slice(b * BLK, (b + 1) * BLK)} for b in range(3)]

    def scores(d):
        hr, qc, b = d["hr"], d["qc"], d["b"]
        s = tn(pick(k_ref, kp_ref, hr, b, two), q_ref[hr, qc])
        if b:
            s = s + bias_ref[b - 1, : s.shape[0]].astype(F32)
        d["s"] = s
        d["dp"] = tn(pick(v_ref, vp_ref, hr, b, two), gctx_ref[hr, qc])

    def weights(d):
        p = jnp.exp(d.pop("s") - lse_ref[d["h"], :, d["qc"]])
        dp = d.pop("dp")
        dots = jnp.sum(p * dp, 0, keepdims=True)
        d["ds"] = (p * (dp - dots)).astype(BF16)
        d["p"] = p.astype(BF16)

    def mix(d):
        hr, qc, b = d["hr"], d["qc"], d["b"]
        ds = d.pop("ds")
        dq_ref[hr, qc] = (nn(pick(k_ref, kp_ref, hr, b, two), ds) * 0.125).astype(BF16)
        gk = nt(q_ref[hr, qc], ds)
        gv = nt(gctx_ref[hr, qc], d.pop("p"))
        for acc, grad, slot in ((dk, gk, 0), (dv, gv, 1)):
            acc[hr, qc] += grad[:, :BLK]
            other = grad[:, BLK:]
            if b == 0:
                far_ref[slot, hr, :BLK] = other.astype(BF16)
            elif b == 1:
                far_ref[slot, hr, BLK:] = (other * scale).astype(BF16)
                acc[hr, 2 * BLK :] += other * (1.0 - scale)
            else:
                acc[hr, BLK + SHORT : 2 * BLK] += other

    pipelined(items, scores, weights, mix, 1, 2)
    dk_ref[...] = dk[...]
    dv_ref[...] = dv[...]


def through_kernel(
    code_ref, xt_ref, dqa_ref, dka_ref, dva_ref, ba_ref, dqb_ref, dkb_ref, dvb_ref, bb_ref, wqkv_ref,
    gfirst_ref, gvec1_ref, gvec2_ref, *refs, half,
):
    core = code_ref[0]
    order = jnp.where(core == half, code_ref[1], code_ref[2])
    if half:
        first_ref, _, gin_ref, keep_ref, send_ref, piece_ref = refs
    else:
        gin_ref, piece_ref = refs
    through = []
    groups = ((dqa_ref, dka_ref, dva_ref, ba_ref), (dqb_ref, dkb_ref, dvb_ref, bb_ref))
    for i, (dq_ref, dk_ref, dv_ref, b_ref) in enumerate(groups):
        rows = slice(i * GD, (i + 1) * GD)
        grads = [dq_ref[...]]
        for slot, ref in ((0, dk_ref), (1, dv_ref)):
            own = ref[...]
            own = jnp.concatenate([own[:, :EXT] + b_ref[slot].astype(F32), own[:, EXT:]], 1)
            grads.append(own.astype(BF16))
        through.append(sum(nn(wqkv_ref[t, i], grads[t]) for t in range(3)))
        row = jnp.concatenate(
            [nt(xt_ref[rows], grad) for grad in grads]
            + [gvec1_ref[rows], gvec2_ref[rows], jnp.zeros((GD, WIDTH - 3 * GD - 4), F32)],
            1,
        )
        for r in range(4):
            piece_ref[(i * 4 + r) ^ order] = row[48 * r : 48 * (r + 1)]
    if half:
        mine, other = piece_ref[...], first_ref[...]
        keep_ref[...] = jnp.where(core == 1, mine, other)
        send_ref[...] = jnp.where(core == 1, other, mine).astype(BF16)
    gin_ref[...] = (gfirst_ref[...] + jnp.concatenate(through, 0)).astype(BF16).T


def chunks(code_ref, near_ref, far_ref):
    core, low, far = code_ref[0], code_ref[1], code_ref[2]
    for other, ref in ((0, near_ref), (1, far_ref)):
        for a in range(8):
            g = (other ^ core) * 2 + a // 4
            rows = slice(48 * (a % 4), 48 * (a % 4 + 1))
            yield g, rows, ref[a ^ (far if other else low)].astype(F32)


def finish_kernel(code_ref, half_ref, *refs, far, way, outs):
    *refs, token_ref = refs
    token_ref[...] = jnp.zeros_like(token_ref)
    order = code_ref[1 + 2 * way + far]
    for a in range(8):
        part = half_ref[a ^ order].astype(F32)
        rows = slice(48 * (a % 4), 48 * (a % 4 + 1))
        for i, ref in enumerate(refs[-outs:]):
            ref[a // 4, rows] = part[48 * i : 48 * (i + 1)]


def finish_qkv_kernel(code_ref, near_ref, far_ref, gq_ref, ag_ref, as_ref, fg_ref, fs_ref, vec):
    for g, rows, part in chunks(code_ref, near_ref, far_ref):
        for t in range(3):
            gq_ref[t, g, rows] = part[:, t * GD : (t + 1) * GD]
        vec[g, rows] = part[:, 512:640]
    turned = vec[...].reshape(D, 128).T
    for i, ref in enumerate((ag_ref, as_ref, fg_ref, fs_ref)):
        ref[...] = turned[64 + i : 65 + i].reshape(D)


def fold_kernel(keep_ref, came_ref, kept_ref, send_ref):
    n = kept_ref.shape[0]
    kept_ref[...] = keep_ref[:n].astype(F32) + came_ref[:n].astype(F32)
    send_ref[...] = (keep_ref[n:].astype(F32) + came_ref[n:].astype(F32)).astype(BF16)


def meet_kernel(*refs):
    *ins, out_ref = refs
    at = 0
    for keep_ref, came_ref in zip(ins[::2], ins[1::2]):
        rows = keep_ref.shape[1]
        out_ref[:, at : at + rows] = (keep_ref[...].astype(F32) + came_ref[...].astype(F32)).astype(BF16)
        at += rows


def join_kernel(near_ref, far_ref, out_ref):
    n = near_ref.shape[0]
    out_ref[:n] = near_ref[...]
    out_ref[n:] = far_ref[...]


SMEM = pl.BlockSpec(memory_space=pltpu.SMEM)
VMEM = pl.BlockSpec(memory_space=pltpu.VMEM)
ANY = pl.BlockSpec(memory_space=pl.ANY)


class Steps:
    def __init__(self):
        self.last = None

    def __call__(self, kernel, name, ins, outs, scratch, limit, grid=(), code=None, aliases=None):
        n, free = len(ins) + (code is not None), self.last is None
        if not free:
            ins = ins + [(self.last, ANY)]
        specs = dict(
            grid=grid,
            in_specs=[spec for _, spec in ins],
            out_specs=[spec for _, _, spec in outs],
            scratch_shapes=scratch,
        )
        if code is not None:
            specs = dict(grid_spec=pltpu.PrefetchScalarGridSpec(num_scalar_prefetch=1, **specs))
        results = pl.pallas_call(
            kernel if free else lambda *refs: kernel(*refs[:n], *refs[n + 1 :]),
            out_shape=[jax.ShapeDtypeStruct(s, d) for s, d, _ in outs],
            compiler_params=pltpu.CompilerParams(vmem_limit_bytes=limit << 20),
            cost_estimate=pl.CostEstimate(flops=int(COST[name.split('_')[0]] * 1e9), bytes_accessed=1024, transcendentals=0),
            input_output_aliases=aliases or {},
            name=name,
            **specs,
        )(*([] if code is None else [code]), *[array for array, _ in ins])
        self.last = results[-1]
        return results


def block(shape, *at):
    return pl.BlockSpec(shape, lambda _: at)


class Links:
    def __init__(self, n_seq, orders):
        bits = n_seq.bit_length() - 1
        self.n = n_seq * 2
        self.orders = [order + list(range(3, bits)) for order in orders]
        self.bits = bits

    def pairs(self, step):
        if step < 0:
            return [(i, i ^ 1) for i in range(self.n)]
        return [(i, i ^ (2 << self.orders[i & 1][step])) for i in range(self.n)]

    def code(self, seq, core):
        first, second = [sum(((seq >> order[step]) & 1) << (2 - step) for step in range(3)) for order in self.orders]
        return jnp.where(core == 0, first, second)


def swap(x, links, step):
    return lax.ppermute(x, "dev", links.pairs(step))


class Total:
    def __init__(self, run, links, name, keep, came):
        self.run, self.links, self.name = run, links, name
        self.keep, self.came = keep, came
        self.step = 0

    def small(self, kernel, ins, outs):
        spec = [(x, VMEM) for x in ins]
        return self.run(kernel, self.name, spec, [o + (VMEM,) for o in outs], [], 4)

    def fold(self):
        shape = (self.keep.shape[0] // 2,) + self.keep.shape[1:]
        self.keep, send = self.small(fold_kernel, [self.keep, self.came], [(shape, F32), (shape, BF16)])
        self.came = swap(send, self.links, self.step)
        self.step += 1

    def meet(self, *others):
        parts = [*others, self]
        shape = (1, sum(p.keep.shape[1] for p in parts), self.keep.shape[2])
        ins = [x for p in parts for x in (p.keep, p.came)]
        (self.near,) = self.small(meet_kernel, ins, [(shape, BF16)])
        for step in range(3, self.links.bits - 1):
            (self.near,) = self.small(meet_kernel, [self.near, swap(self.near, self.links, step)], [(shape, BF16)])
        self.far = swap(self.near, self.links, self.links.bits - 1)

    def whole(self):
        (self.near,) = self.small(meet_kernel, [self.near, self.far], [(self.near.shape, BF16)])
        self.step = 2
        self.far = swap(self.near, self.links, self.step)

    def join(self):
        shape = (self.near.shape[0] * 2,) + self.near.shape[1:]
        (self.near,) = self.small(join_kernel, [self.near, self.far], [(shape, BF16)])
        self.step -= 1
        self.far = swap(self.near, self.links, self.step)


def per_device(
    links, upright, inputs, segment_ids, qkv_weight, out_weight, ffn_in_weight, ffn_out_weight,
    attn_gain, attn_shift, ffn_gain, ffn_shift, out_cotangent,
):
    me = lax.axis_index("dev")
    seq, core = me >> 1, me & 1
    codes = [core]
    for way in (links, upright):
        codes += [way.code(seq, core), way.code(seq, 1 - core)]
    code = jnp.stack(codes).astype(jnp.int32)
    partner = swap(inputs, links, -1)
    square = (D, TOK)
    large = (GROUPS, GF, TOK)
    run = Steps()
    xt, q, k, v = run(
        project_kernel,
        "project",
        [(inputs, VMEM), (qkv_weight, VMEM)],
        [(square, BF16, VMEM)] * 4,
        [],
        12,
    )
    kp, vp, ctx, lse, bias = run(
        attend_kernel,
        "attend",
        [(segment_ids, SMEM), (segment_ids, VMEM), (partner, VMEM), (qkv_weight, VMEM)]
        + [(q, VMEM), (k, VMEM), (v, VMEM)],
        [((D, EXT), BF16, VMEM), ((D, EXT), BF16, VMEM), (square, BF16, VMEM), ((HEADS, 1, TOK), F32, VMEM)]
        + [((2, 2 * BLK, BLK), BF16, VMEM)],
        [],
        12,
    )
    weight2t = jnp.swapaxes(ffn_out_weight, 1, 2)
    output, hid, n1, inv1, gpr, gsec, gfeed, keep, send, gvec2 = run(
        forward_kernel,
        "forward",
        [(code, SMEM), (xt, VMEM), (ctx, VMEM), (out_weight, VMEM), (ffn_in_weight, VMEM), (weight2t, VMEM)]
        + [(out_cotangent, VMEM), (attn_gain, VMEM), (attn_shift, VMEM), (ffn_gain, VMEM), (ffn_shift, VMEM)],
        [((TOK, D), BF16, VMEM), (square, BF16, VMEM), (square, F32, VMEM), ((1, TOK), F32, VMEM), (large, BF16, VMEM)]
        + [(square, F32, VMEM), (square, BF16, VMEM), ((8, 48, D), BF16, VMEM), ((8, 48, D), BF16, VMEM)]
        + [((D, 2), F32, VMEM)],
        [
            pltpu.VMEM((D, D), BF16), pltpu.VMEM((GROUPS, GF, GD), BF16), pltpu.VMEM(large, BF16),
            pltpu.VMEM((4, D, BLK), F32), pltpu.VMEM((2, D, 128), F32), pltpu.VMEM((2, D, BLK), F32),
        ],
        20,
    )
    ffn_out = Total(run, upright, "sum_ffn_out", keep, swap(send, links, -1))
    gctx, gfirst, gup, gatt, gvec1 = run(
        backward_kernel,
        "backward",
        [(out_weight, VMEM), (ffn_in_weight, VMEM), (weight2t, VMEM)]
        + [(n1, VMEM), (inv1, VMEM), (gpr, VMEM), (gsec, VMEM), (gfeed, VMEM), (attn_gain, VMEM)],
        [(square, BF16, VMEM), (square, F32, VMEM), (large, BF16, VMEM), (square, BF16, VMEM), ((D, 2), F32, VMEM)],
        [pltpu.VMEM((GROUPS, GF, GD), BF16), pltpu.VMEM((D, BLK), F32), pltpu.VMEM((2, D, 128), F32)],
        12,
    )
    ffn_out.fold()
    message = ((8, 96, D), BF16, VMEM)
    keep, send = run(
        weights_kernel,
        "weights",
        [(code, SMEM), (ctx, VMEM), (hid, VMEM), (gup, VMEM), (gatt, VMEM)],
        [message, message],
        [],
        12,
    )
    others = Total(run, links, "sum_others", keep, swap(send, links, -1))

    def attention_back(g):
        rows = partial(lambda width: block((GD, width), g, 0))
        return run(
            back_kernel,
            "attention_back",
            [(segment_ids, SMEM), (q, rows(TOK)), (k, rows(TOK)), (v, rows(TOK)), (kp, rows(EXT)), (vp, rows(EXT))]
            + [(gctx, rows(TOK)), (lse, block((3, 1, TOK), g, 0, 0)), (bias, VMEM)],
            [((GD, TOK), BF16, VMEM), ((GD, TOK), F32, VMEM), ((GD, TOK), F32, VMEM), ((2, GD, EXT), BF16, VMEM)],
            [pltpu.VMEM((GD, TOK), F32), pltpu.VMEM((GD, TOK), F32)],
            10,
            (1,),
        )

    def through(half, parts, first):
        ins = [(code, SMEM), (xt, block((HALF, TOK), half, 0))]
        for dq, dk, dv, far in parts:
            ins += [(dq, VMEM), (dk, VMEM), (dv, VMEM), (swap(far, links, -1), VMEM)]
        ins += [(qkv_weight, block((3, 2, GD, GD), 0, half, 0, 0))]
        ins += [(gfirst, block((HALF, TOK), half, 0)), (gvec1, block((HALF, 2), half, 0))]
        ins += [(gvec2, block((HALF, 2), half, 0))]
        shape = (8, 48, WIDTH)
        outs = [((TOK, D), BF16, block((TOK, HALF), 0, half))]
        if half:
            ins += [(first[1], VMEM), (first[0], ANY)]
            outs += [(shape, F32, VMEM), (shape, BF16, VMEM)]
        else:
            outs += [(shape, F32, VMEM)]
        return run(
            partial(through_kernel, half=half),
            "through_qkv",
            ins,
            outs,
            [pltpu.VMEM(shape, F32)] if half else [],
            10,
            (1,),
            None,
            {len(ins) - 1: 0} if half else None,
        )

    rows = (GROUPS, GD, D)

    def finish(total, far, into, way, n):
        def half(c):
            return (c[0] ^ far, 0, 0)

        outs = [(rows, F32, pl.BlockSpec((2, GD, D), lambda _, c: half(c)))] * n
        outs += [((8, 128), F32, pl.BlockSpec((8, 128), lambda _, c: (0, 0)))]
        ins = [(total.far if far else total.near, pl.BlockSpec((8, 48 * n, D), lambda _, c: (0, 0, 0)))]
        ins += [(x, ANY) for x in into]
        kernel = partial(finish_kernel, far=far, way=way, outs=n)
        return run(kernel, "finish", ins, outs, [], 12, (1,), code, {2 + i: i for i in range(len(into))})[:n]

    parts = [attention_back(0)]
    ffn_out.fold()
    others.fold()
    parts += [attention_back(1)]
    ffn_out.fold()
    parts += [attention_back(2)]
    others.fold()
    first = through(0, parts[:2], None)
    ffn_out.meet()
    parts += [attention_back(3)]
    others.fold()
    grad_input, keep, send = through(1, parts[2:], first)
    others.meet()
    qkv = Total(run, links, "sum_qkv", keep, swap(send, links, -1))
    qkv.fold()
    ffn_out.whole()
    ffn_out.join()
    qkv.fold()
    others.whole()
    qkv.fold()
    others.join()
    qkv.meet()
    ffn_out.join()
    others.join()
    qkv.whole()
    ffn_out.join()
    qkv.join()
    near_out = finish(ffn_out, 0, [], 1, 1)
    qkv.join()
    others.join()
    (g2,) = finish(ffn_out, 1, near_out, 1, 1)
    half_way = finish(others, 0, [], 0, 2)
    qkv.join()
    g1, go = finish(others, 1, half_way, 0, 2)
    gq, *vectors = run(
        finish_qkv_kernel,
        "finish_qkv",
        [(code, SMEM), (qkv.near, VMEM), (qkv.far, VMEM)],
        [((3, GROUPS, GD, GD), F32, VMEM)] + [((D,), F32, VMEM)] * 4,
        [pltpu.VMEM((GROUPS, GD, 128), F32)],
        8,
    )
    return (output, grad_input, gq, go.reshape(D, D), g1, jnp.swapaxes(g2, 1, 2)) + tuple(vectors)


def solution(mesh):
    flat = Mesh(mesh.devices.reshape(-1), ("dev",))
    links = Links(mesh.shape["seq"], [[0, 1, 2], [1, 2, 0]])
    upright = Links(mesh.shape["seq"], [[2, 0, 1], [0, 2, 1]])
    split, copied = P("dev"), P()
    return jax.shard_map(
        partial(per_device, links, upright),
        mesh=flat,
        in_specs=(split, split) + (copied,) * 8 + (split,),
        out_specs=(split, split) + (copied,) * 8,
        check_vma=False,
    )
```

```python
from functools import partial

import jax
import jax.numpy as jnp
from jax import lax
from jax.experimental import pallas as pl
from jax.experimental.pallas import tpu as pltpu
from jax.sharding import Mesh, PartitionSpec as P

F32 = jnp.float32
BF16 = jnp.bfloat16
EPSILON = 1e-05
HEADS = 12
HEAD_DIM = 64
D = 768
GROUPS = 4
GD = D // GROUPS
FF = 3072
GF = FF // GROUPS
TOK = 768
BLK = 256
SHORT = 128
EXT = 512
WIDTH = 640
HALF = D // 2
COST = dict(project=3, attend=9, forward=19, backward=6, weights=4, attention=4, through=3, sum=9, finish=3)


def nn(a, b):
    return lax.dot_general(a, b, (((1,), (0,)), ((), ())), preferred_element_type=F32)


def nt(a, b):
    return lax.dot_general(a, b, (((1,), (1,)), ((), ())), preferred_element_type=F32)


def tn(a, b):
    return lax.dot_general(a, b, (((0,), (0,)), ((), ())), preferred_element_type=F32)


def gelu_parts(u):
    a = jnp.abs(u) * 0.7071067811865476
    t = 1.0 / (1.0 + 0.3275911 * a)
    e = jnp.exp(-0.5 * (u * u))
    poly = t * (
        0.254829592
        + t * (-0.284496736 + t * (1.421413741 + t * (-1.453152027 + t * 1.061405429)))
    )
    tail = 0.5 * poly * e
    phi = jnp.where(u < 0, tail, 1.0 - tail)
    return u * phi, phi + u * (e * 0.3989422804014327)


def pipelined(items, first, second, third, lag, last):
    n = len(items)
    for t in range(n + last):
        if t < n:
            first(items[t])
        if 0 <= t - lag < n:
            second(items[t - lag])
        if 0 <= t - last < n:
            third(items[t - last])


def stages(items, first, second, third, lag, last):
    n = len(items)
    for t in range(n + last):
        if t < n:
            first(items[t])
        if 0 <= t - lag < n:
            second(items[t - lag])
        if 0 <= t - last < n:
            third(items[t - last])
        yield


def weave(*streams):
    streams = list(streams)
    while streams:
        for stream in list(streams):
            if next(stream, streams) is streams:
                streams.remove(stream)


def project_kernel(x_ref, wqkv_ref, xt_ref, q_ref, k_ref, v_ref):
    xt_ref[...] = x_ref[...].T
    for g in range(GROUPS):
        rows = slice(g * GD, (g + 1) * GD)
        xg = xt_ref[rows, :]
        q_ref[rows, :] = (tn(wqkv_ref[0, g], xg).astype(BF16).astype(F32) * 0.125).astype(BF16)
        k_ref[rows, :] = tn(wqkv_ref[1, g], xg).astype(BF16)
        v_ref[rows, :] = tn(wqkv_ref[2, g], xg).astype(BF16)


def pick(ref, far_ref, hr, b, two):
    if b == 0:
        other = far_ref[hr, :BLK]
    elif b == 1:
        other = jnp.where(two, far_ref[hr, BLK:], ref[hr, 2 * BLK :])
    else:
        other = ref[hr, BLK + SHORT : 2 * BLK]
    return jnp.concatenate([ref[hr, b * BLK : (b + 1) * BLK], other], 1)


def attend_kernel(
    seg_ref, ids_ref, xp_ref, wqkv_ref, q_ref, k_ref, v_ref,
    kp_ref, vp_ref, ctx_ref, lse_ref, bias_ref,
):
    two = seg_ref[BLK] == 1
    row = ids_ref[...].reshape(1, TOK)

    def lanes(b):
        return jnp.broadcast_to(row[:, b * BLK : (b + 1) * BLK], (BLK, BLK))

    def same(kb, qb):
        return jnp.where(lanes(kb).T == lanes(qb), 0.0, -1e30).astype(BF16)

    bias_ref[0, :BLK] = same(1, 1)
    bias_ref[0, BLK:] = jnp.where(two, jnp.zeros((BLK, BLK), BF16), same(2, 1))
    bias_ref[1, :BLK] = same(2, 2)
    bias_ref[1, BLK : BLK + SHORT] = same(1, 2)[SHORT:]
    xpt = xp_ref[:EXT, :].T
    for g in range(GROUPS):
        rows = slice(g * GD, (g + 1) * GD)
        kp_ref[rows, :] = tn(wqkv_ref[1, g], xpt[rows]).astype(BF16)
        vp_ref[rows, :] = tn(wqkv_ref[2, g], xpt[rows]).astype(BF16)

    def heads(i, carry):
        items = []
        for u in range(6):
            h = i * 6 + u
            hr = pl.ds(pl.multiple_of(h * HEAD_DIM, HEAD_DIM), HEAD_DIM)
            items += [{"h": h, "hr": hr, "b": b, "qc": slice(b * BLK, (b + 1) * BLK)} for b in range(3)]

        def scores(d):
            s = tn(pick(k_ref, kp_ref, d["hr"], d["b"], two), q_ref[d["hr"], d["qc"]])
            if d["b"]:
                s = s + bias_ref[d["b"] - 1, : s.shape[0]].astype(F32)
            d["s"] = s

        def weights(d):
            s = d.pop("s")
            d["top"] = jnp.max(s, 0, keepdims=True)
            p = jnp.exp(s - d["top"])
            d["total"] = jnp.sum(p, 0, keepdims=True)
            d["p"] = p.astype(BF16)

        def mix(d):
            c = nn(pick(v_ref, vp_ref, d["hr"], d["b"], two), d.pop("p"))
            ctx_ref[d["hr"], d["qc"]] = (c * (1.0 / d["total"])).astype(BF16)
            lse_ref[d["h"], :, d["qc"]] = d["top"] + jnp.log(d["total"])

        pipelined(items, scores, weights, mix, 2, 3)
        return carry

    lax.fori_loop(0, HEADS // 6, heads, 0)


PARTS = [(g, slice(j * BLK, (j + 1) * BLK)) for g in range(GROUPS) for j in range(GF // BLK)]


def columns(ref):
    wide = jnp.broadcast_to(ref[...].reshape(1, D), (128, D)).T
    return jnp.concatenate([wide, wide], 1)


def halves(x):
    return x[:, :128] + x[:, 128:]


def scatter(part, jj, g, keep_ref, send_ref, at, low, far):
    for r in range(4):
        piece = part[48 * r : 48 * (r + 1)].astype(BF16)
        pos = ((g & 1) * 4 + r) ^ (low if jj < 2 else far)
        ref = keep_ref if jj < 2 else send_ref
        ref[pos, at : at + 48] = piece


def forward_kernel(
    code_ref, xt_ref, ctx_ref, wo_ref, w1_ref, w2t_ref, cot_ref, ag_ref, as_ref, fg_ref, fs_ref,
    out_ref, hid_ref, n1_ref, inv1_ref, gpr_ref, gsec_ref, gfeed_ref, keep_ref, send_ref, gvec_ref,
    wot, w1t, act, nb, gacc, held,
):
    core, low, far = code_ref[0], code_ref[3], code_ref[4]
    for j, ref in enumerate((ag_ref, as_ref, fg_ref, fs_ref)):
        nb[j] = columns(ref)
    wot[...] = wo_ref[...].T
    for g in range(GROUPS):
        w1t[g] = w1_ref[g].T
    gacc[...] = jnp.zeros_like(gacc)

    channels = [slice(g * GD, (g + 1) * GD) for g in range(GROUPS)]

    def at(t):
        return pl.ds(pl.multiple_of(t * BLK, BLK), BLK)

    def mean(pieces):
        return sum(jnp.sum(x, 0, keepdims=True) for x in pieces) * (1.0 / D)

    def enter(t):
        tc, r = at(t), []
        for ch in channels:
            r.append(xt_ref[ch, tc].astype(F32) + nn(wot[ch], ctx_ref[:, tc]))
            yield
        average = mean(r)
        centre = [x - average for x in r]
        yield
        inv1 = lax.rsqrt(mean([x * x for x in centre]) + EPSILON)
        inv1_ref[:, tc] = inv1
        yield
        for ch, x in zip(channels, centre):
            n1 = x * inv1
            n1_ref[ch, tc] = n1
            hidden = n1 * nb[0, ch] + nb[1, ch]
            hid_ref[ch, tc] = hidden.astype(BF16)
            held[t & 1, ch] = hidden
            yield

    def middle(t, feeds):
        tc, up = at(t), {}

        def rise(p):
            g, fr = p
            up[g, fr.start] = nn(w1t[g, fr], hid_ref[channels[g], tc])

        def bend(p):
            g, fr = p
            a, slope = gelu_parts(up.pop((g, fr.start)))
            act[g, fr, tc] = a.astype(BF16)
            gpr_ref[g, fr, tc] = slope.astype(BF16)

        def fall(p):
            if p[1].stop == GF:
                feeds.append(nn(w2t_ref[p[0]], act[p[0], :, tc]))

        yield from stages(PARTS, rise, bend, fall, 2, 3)

    def leave(t, feeds):
        tc = at(t)
        r2 = [held[t & 1, ch] + x for ch, x in zip(channels, feeds)]
        average = mean(r2)
        centre = [x - average for x in r2]
        yield
        inv2 = lax.rsqrt(mean([x * x for x in centre]) + EPSILON)
        yield
        n2, low = [], []
        for ch, x in zip(channels, centre):
            n2.append(x * inv2)
            low.append((n2[-1] * nb[2, ch] + nb[3, ch]).astype(BF16))
            yield
        out_ref[tc, :] = jnp.concatenate(low, 0).T
        turned = cot_ref[tc, :].T
        yield
        cg = []
        for ch, n in zip(channels, n2):
            c = turned[ch].astype(F32)
            gacc[0, ch] += halves(c * n)
            gacc[1, ch] += halves(c)
            cg.append(c * nb[2, ch])
            yield
        first = mean(cg)
        second = mean([x * n for x, n in zip(cg, n2)])
        yield
        for ch, x, n in zip(channels, cg, n2):
            gsec = inv2 * (x - first - n * second)
            gsec_ref[ch, tc] = gsec
            gfeed_ref[ch, tc] = gsec.astype(BF16)
            yield

    def tile(t, carry):
        feeds = []
        weave(middle(t, feeds), enter(jnp.minimum(t + 1, TOK // BLK - 1)))
        weave(leave(t, feeds))
        return carry

    weave(enter(0))
    lax.fori_loop(0, TOK // BLK, tile, 0)
    for j in range(2):
        gvec_ref[:, j : j + 1] = jnp.sum(gacc[j], 1, keepdims=True)
    for jj in (2, 3, 0, 1):
        g = jj ^ (2 * core)
        gr = pl.ds(pl.multiple_of(g * GD, GD), GD)
        scatter(nt(gfeed_ref[gr, :], act[g]), jj, g, keep_ref, send_ref, 0, low, far)


def backward_kernel(
    wo_ref, w1_ref, w2t_ref, n1_ref, inv1_ref, gpr_ref, gsec_ref, gfeed_ref, ag_ref,
    gctx_ref, gfirst_ref, gup, gatt, gvec_ref,
    w2, nb, gacc, held,
):
    nb[...] = columns(ag_ref)
    for g in range(GROUPS):
        w2[g] = w2t_ref[g].T
    gacc[...] = jnp.zeros_like(gacc)

    channels = [slice(g * GD, (g + 1) * GD) for g in range(GROUPS)]

    def at(t):
        return pl.ds(pl.multiple_of(t * BLK, BLK), BLK)

    def mean(pieces):
        return sum(jnp.sum(x, 0, keepdims=True) for x in pieces) * (1.0 / D)

    def feed_back(t):
        tc, back = at(t), {}

        def lift(p):
            g, fr = p
            back[g, fr.start] = nn(w2[g, fr], gfeed_ref[channels[g], tc])

        def scale(p):
            g, fr = p
            gup[g, fr, tc] = (back.pop((g, fr.start)) * gpr_ref[g, fr, tc].astype(F32)).astype(BF16)

        def drop(p):
            g, fr = p
            if fr.stop == GF:
                held[t & 1, channels[g]] = gsec_ref[channels[g], tc] + nn(w1_ref[g], gup[g, :, tc])

        yield from stages(PARTS, lift, scale, drop, 2, 3)

    def norm_back(t):
        tc, sc = at(t), []
        for ch in channels:
            ghid = held[t & 1, ch]
            gacc[0, ch] += halves(ghid * n1_ref[ch, tc])
            gacc[1, ch] += halves(ghid)
            sc.append(ghid * nb[ch])
            yield
        first = mean(sc)
        second = mean([x * n1_ref[ch, tc] for ch, x in zip(channels, sc)])
        yield
        for ch, x in zip(channels, sc):
            gfirst = inv1_ref[:, tc] * (x - first - n1_ref[ch, tc] * second)
            gfirst_ref[ch, tc] = gfirst
            gatt[ch, tc] = gfirst.astype(BF16)
            yield
        for ch in channels:
            gctx_ref[ch, tc] = nn(wo_ref[ch, :], gatt[:, tc]).astype(BF16)
            yield

    def tile(t, carry):
        weave(feed_back(t + 1), norm_back(t))
        return carry

    weave(feed_back(0))
    lax.fori_loop(0, TOK // BLK - 1, tile, 0)
    weave(norm_back(TOK // BLK - 1))
    for j in range(2):
        gvec_ref[:, j : j + 1] = jnp.sum(gacc[j], 1, keepdims=True)


def weights_kernel(code_ref, ctx_ref, hid_ref, gup_ref, gatt_ref, keep_ref, send_ref):
    core, low, far = code_ref[0], code_ref[1], code_ref[2]
    for jj in (2, 3, 0, 1):
        g = jj ^ (2 * core)
        gr = pl.ds(pl.multiple_of(g * GD, GD), GD)
        scatter(nt(hid_ref[gr, :], gup_ref[g]), jj, g, keep_ref, send_ref, 0, low, far)
        if jj & 1 == 0:
            rows = pl.ds(pl.multiple_of((jj // 2 ^ core) * HALF, HALF), HALF)
            both = nt(ctx_ref[rows, :], gatt_ref[...])
        mine = both[:GD] if jj & 1 == 0 else both[GD:]
        scatter(mine, jj, g, keep_ref, send_ref, 48, low, far)


def back_kernel(
    seg_ref, q_ref, k_ref, v_ref, kp_ref, vp_ref, gctx_ref, lse_ref, bias_ref,
    dq_ref, dk_ref, dv_ref, far_ref, dk, dv,
):
    two = seg_ref[BLK] == 1
    scale = jnp.where(two, 1.0, 0.0)
    dk[...] = jnp.zeros_like(dk)
    dv[...] = jnp.zeros_like(dv)

    items = []
    for h in range(3):
        hr = slice(h * HEAD_DIM, (h + 1) * HEAD_DIM)
        items += [{"h": h, "hr": hr, "b": b, "qc": slice(b * BLK, (b + 1) * BLK)} for b in range(3)]

    def scores(d):
        hr, qc, b = d["hr"], d["qc"], d["b"]
        s = tn(pick(k_ref, kp_ref, hr, b, two), q_ref[hr, qc])
        if b:
            s = s + bias_ref[b - 1, : s.shape[0]].astype(F32)
        d["s"] = s
        d["dp"] = tn(pick(v_ref, vp_ref, hr, b, two), gctx_ref[hr, qc])

    def weights(d):
        p = jnp.exp(d.pop("s") - lse_ref[d["h"], :, d["qc"]])
        dp = d.pop("dp")
        dots = jnp.sum(p * dp, 0, keepdims=True)
        d["ds"] = (p * (dp - dots)).astype(BF16)
        d["p"] = p.astype(BF16)

    def mix(d):
        hr, qc, b = d["hr"], d["qc"], d["b"]
        ds = d.pop("ds")
        dq_ref[hr, qc] = (nn(pick(k_ref, kp_ref, hr, b, two), ds) * 0.125).astype(BF16)
        gk = nt(q_ref[hr, qc], ds)
        gv = nt(gctx_ref[hr, qc], d.pop("p"))
        for acc, grad, slot in ((dk, gk, 0), (dv, gv, 1)):
            acc[hr, qc] += grad[:, :BLK]
            other = grad[:, BLK:]
            if b == 0:
                far_ref[slot, hr, :BLK] = other.astype(BF16)
            elif b == 1:
                far_ref[slot, hr, BLK:] = (other * scale).astype(BF16)
                acc[hr, 2 * BLK :] += other * (1.0 - scale)
            else:
                acc[hr, BLK + SHORT : 2 * BLK] += other

    pipelined(items, scores, weights, mix, 1, 2)
    dk_ref[...] = dk[...]
    dv_ref[...] = dv[...]


def through_kernel(
    code_ref, xt_ref, dqa_ref, dka_ref, dva_ref, ba_ref, dqb_ref, dkb_ref, dvb_ref, bb_ref, wqkv_ref,
    gfirst_ref, gvec1_ref, gvec2_ref, *refs, half,
):
    core = code_ref[0]
    order = jnp.where(core == half, code_ref[1], code_ref[2])
    if half:
        first_ref, _, gin_ref, keep_ref, send_ref, piece_ref = refs
    else:
        gin_ref, piece_ref = refs
    through = []
    groups = ((dqa_ref, dka_ref, dva_ref, ba_ref), (dqb_ref, dkb_ref, dvb_ref, bb_ref))
    for i, (dq_ref, dk_ref, dv_ref, b_ref) in enumerate(groups):
        rows = slice(i * GD, (i + 1) * GD)
        grads = [dq_ref[...]]
        for slot, ref in ((0, dk_ref), (1, dv_ref)):
            own = ref[...]
            own = jnp.concatenate([own[:, :EXT] + b_ref[slot].astype(F32), own[:, EXT:]], 1)
            grads.append(own.astype(BF16))
        through.append(sum(nn(wqkv_ref[t, i], grads[t]) for t in range(3)))
        row = jnp.concatenate(
            [nt(xt_ref[rows], grad) for grad in grads]
            + [gvec1_ref[rows], gvec2_ref[rows], jnp.zeros((GD, WIDTH - 3 * GD - 4), F32)],
            1,
        )
        for r in range(4):
            piece_ref[(i * 4 + r) ^ order] = row[48 * r : 48 * (r + 1)]
    if half:
        mine, other = piece_ref[...], first_ref[...]
        keep_ref[...] = jnp.where(core == 1, mine, other)
        send_ref[...] = jnp.where(core == 1, other, mine).astype(BF16)
    gin_ref[...] = (gfirst_ref[...] + jnp.concatenate(through, 0)).astype(BF16).T


def chunks(code_ref, near_ref, far_ref):
    core, low, far = code_ref[0], code_ref[1], code_ref[2]
    for other, ref in ((0, near_ref), (1, far_ref)):
        for a in range(8):
            g = (other ^ core) * 2 + a // 4
            rows = slice(48 * (a % 4), 48 * (a % 4 + 1))
            yield g, rows, ref[a ^ (far if other else low)].astype(F32)


def finish_kernel(code_ref, half_ref, *refs, far, way, outs):
    *refs, token_ref = refs
    token_ref[...] = jnp.zeros_like(token_ref)
    order = code_ref[1 + 2 * way + far]
    for a in range(8):
        part = half_ref[a ^ order].astype(F32)
        rows = slice(48 * (a % 4), 48 * (a % 4 + 1))
        for i, ref in enumerate(refs[-outs:]):
            ref[a // 4, rows] = part[48 * i : 48 * (i + 1)]


def finish_qkv_kernel(code_ref, near_ref, far_ref, gq_ref, ag_ref, as_ref, fg_ref, fs_ref, vec):
    for g, rows, part in chunks(code_ref, near_ref, far_ref):
        for t in range(3):
            gq_ref[t, g, rows] = part[:, t * GD : (t + 1) * GD]
        vec[g, rows] = part[:, 512:640]
    turned = vec[...].reshape(D, 128).T
    for i, ref in enumerate((ag_ref, as_ref, fg_ref, fs_ref)):
        ref[...] = turned[64 + i : 65 + i].reshape(D)


def fold_kernel(keep_ref, came_ref, kept_ref, send_ref):
    n = kept_ref.shape[0]
    kept_ref[...] = keep_ref[:n].astype(F32) + came_ref[:n].astype(F32)
    send_ref[...] = (keep_ref[n:].astype(F32) + came_ref[n:].astype(F32)).astype(BF16)


def meet_kernel(*refs):
    *ins, out_ref = refs
    at = 0
    for keep_ref, came_ref in zip(ins[::2], ins[1::2]):
        rows = keep_ref.shape[1]
        out_ref[:, at : at + rows] = (keep_ref[...].astype(F32) + came_ref[...].astype(F32)).astype(BF16)
        at += rows


def join_kernel(near_ref, far_ref, out_ref):
    n = near_ref.shape[0]
    out_ref[:n] = near_ref[...]
    out_ref[n:] = far_ref[...]


SMEM = pl.BlockSpec(memory_space=pltpu.SMEM)
VMEM = pl.BlockSpec(memory_space=pltpu.VMEM)
ANY = pl.BlockSpec(memory_space=pl.ANY)


class Steps:
    def __init__(self):
        self.last = None

    def __call__(self, kernel, name, ins, outs, scratch, limit, grid=(), code=None, aliases=None):
        n, free = len(ins) + (code is not None), self.last is None
        if not free:
            ins = ins + [(self.last, ANY)]
        specs = dict(
            grid=grid,
            in_specs=[spec for _, spec in ins],
            out_specs=[spec for _, _, spec in outs],
            scratch_shapes=scratch,
        )
        if code is not None:
            specs = dict(grid_spec=pltpu.PrefetchScalarGridSpec(num_scalar_prefetch=1, **specs))
        results = pl.pallas_call(
            kernel if free else lambda *refs: kernel(*refs[:n], *refs[n + 1 :]),
            out_shape=[jax.ShapeDtypeStruct(s, d) for s, d, _ in outs],
            compiler_params=pltpu.CompilerParams(vmem_limit_bytes=limit << 20),
            cost_estimate=pl.CostEstimate(flops=int(COST[name.split('_')[0]] * 1e9), bytes_accessed=1024, transcendentals=0),
            input_output_aliases=aliases or {},
            name=name,
            **specs,
        )(*([] if code is None else [code]), *[array for array, _ in ins])
        self.last = results[-1]
        return results


def block(shape, *at):
    return pl.BlockSpec(shape, lambda _: at)


class Links:
    def __init__(self, n_seq, orders):
        bits = n_seq.bit_length() - 1
        self.n = n_seq * 2
        self.orders = [order + list(range(3, bits)) for order in orders]
        self.bits = bits

    def pairs(self, step):
        if step < 0:
            return [(i, i ^ 1) for i in range(self.n)]
        return [(i, i ^ (2 << self.orders[i & 1][step])) for i in range(self.n)]

    def code(self, seq, core):
        first, second = [sum(((seq >> order[step]) & 1) << (2 - step) for step in range(3)) for order in self.orders]
        return jnp.where(core == 0, first, second)


def swap(x, links, step):
    return lax.ppermute(x, "dev", links.pairs(step))


class Total:
    def __init__(self, run, links, name, keep, came):
        self.run, self.links, self.name = run, links, name
        self.keep, self.came = keep, came
        self.step = 0

    def small(self, kernel, ins, outs):
        spec = [(x, VMEM) for x in ins]
        return self.run(kernel, self.name, spec, [o + (VMEM,) for o in outs], [], 4)

    def fold(self):
        shape = (self.keep.shape[0] // 2,) + self.keep.shape[1:]
        self.keep, send = self.small(fold_kernel, [self.keep, self.came], [(shape, F32), (shape, BF16)])
        self.came = swap(send, self.links, self.step)
        self.step += 1

    def meet(self, *others):
        parts = [*others, self]
        shape = (1, sum(p.keep.shape[1] for p in parts), self.keep.shape[2])
        ins = [x for p in parts for x in (p.keep, p.came)]
        (self.near,) = self.small(meet_kernel, ins, [(shape, BF16)])
        for step in range(3, self.links.bits - 1):
            (self.near,) = self.small(meet_kernel, [self.near, swap(self.near, self.links, step)], [(shape, BF16)])
        self.far = swap(self.near, self.links, self.links.bits - 1)

    def whole(self):
        (self.near,) = self.small(meet_kernel, [self.near, self.far], [(self.near.shape, BF16)])
        self.step = 2
        self.far = swap(self.near, self.links, self.step)

    def join(self):
        shape = (self.near.shape[0] * 2,) + self.near.shape[1:]
        (self.near,) = self.small(join_kernel, [self.near, self.far], [(shape, BF16)])
        self.step -= 1
        self.far = swap(self.near, self.links, self.step)


def per_device(
    links, upright, inputs, segment_ids, qkv_weight, out_weight, ffn_in_weight, ffn_out_weight,
    attn_gain, attn_shift, ffn_gain, ffn_shift, out_cotangent,
):
    me = lax.axis_index("dev")
    seq, core = me >> 1, me & 1
    codes = [core]
    for way in (links, upright):
        codes += [way.code(seq, core), way.code(seq, 1 - core)]
    code = jnp.stack(codes).astype(jnp.int32)
    partner = swap(inputs, links, -1)
    square = (D, TOK)
    large = (GROUPS, GF, TOK)
    run = Steps()
    xt, q, k, v = run(
        project_kernel,
        "project",
        [(inputs, VMEM), (qkv_weight, VMEM)],
        [(square, BF16, VMEM)] * 4,
        [],
        12,
    )
    kp, vp, ctx, lse, bias = run(
        attend_kernel,
        "attend",
        [(segment_ids, SMEM), (segment_ids, VMEM), (partner, VMEM), (qkv_weight, VMEM)]
        + [(q, VMEM), (k, VMEM), (v, VMEM)],
        [((D, EXT), BF16, VMEM), ((D, EXT), BF16, VMEM), (square, BF16, VMEM), ((HEADS, 1, TOK), F32, VMEM)]
        + [((2, 2 * BLK, BLK), BF16, VMEM)],
        [],
        12,
    )
    weight2t = jnp.swapaxes(ffn_out_weight, 1, 2)
    output, hid, n1, inv1, gpr, gsec, gfeed, keep, send, gvec2 = run(
        forward_kernel,
        "forward",
        [(code, SMEM), (xt, VMEM), (ctx, VMEM), (out_weight, VMEM), (ffn_in_weight, VMEM), (weight2t, VMEM)]
        + [(out_cotangent, VMEM), (attn_gain, VMEM), (attn_shift, VMEM), (ffn_gain, VMEM), (ffn_shift, VMEM)],
        [((TOK, D), BF16, VMEM), (square, BF16, VMEM), (square, F32, VMEM), ((1, TOK), F32, VMEM), (large, BF16, VMEM)]
        + [(square, F32, VMEM), (square, BF16, VMEM), ((8, 48, D), BF16, VMEM), ((8, 48, D), BF16, VMEM)]
        + [((D, 2), F32, VMEM)],
        [
            pltpu.VMEM((D, D), BF16), pltpu.VMEM((GROUPS, GF, GD), BF16), pltpu.VMEM(large, BF16),
            pltpu.VMEM((4, D, BLK), F32), pltpu.VMEM((2, D, 128), F32), pltpu.VMEM((2, D, BLK), F32),
        ],
        20,
    )
    ffn_out = Total(run, upright, "sum_ffn_out", keep, swap(send, links, -1))
    gctx, gfirst, gup, gatt, gvec1 = run(
        backward_kernel,
        "backward",
        [(out_weight, VMEM), (ffn_in_weight, VMEM), (weight2t, VMEM)]
        + [(n1, VMEM), (inv1, VMEM), (gpr, VMEM), (gsec, VMEM), (gfeed, VMEM), (attn_gain, VMEM)],
        [(square, BF16, VMEM), (square, F32, VMEM), (large, BF16, VMEM), (square, BF16, VMEM), ((D, 2), F32, VMEM)],
        [
            pltpu.VMEM((GROUPS, GF, GD), BF16), pltpu.VMEM((D, BLK), F32), pltpu.VMEM((2, D, 128), F32),
            pltpu.VMEM((2, D, BLK), F32),
        ],
        12,
    )
    ffn_out.fold()
    message = ((8, 96, D), BF16, VMEM)
    keep, send = run(
        weights_kernel,
        "weights",
        [(code, SMEM), (ctx, VMEM), (hid, VMEM), (gup, VMEM), (gatt, VMEM)],
        [message, message],
        [],
        12,
    )
    others = Total(run, links, "sum_others", keep, swap(send, links, -1))

    def attention_back(g):
        rows = partial(lambda width: block((GD, width), g, 0))
        return run(
            back_kernel,
            "attention_back",
            [(segment_ids, SMEM), (q, rows(TOK)), (k, rows(TOK)), (v, rows(TOK)), (kp, rows(EXT)), (vp, rows(EXT))]
            + [(gctx, rows(TOK)), (lse, block((3, 1, TOK), g, 0, 0)), (bias, VMEM)],
            [((GD, TOK), BF16, VMEM), ((GD, TOK), F32, VMEM), ((GD, TOK), F32, VMEM), ((2, GD, EXT), BF16, VMEM)],
            [pltpu.VMEM((GD, TOK), F32), pltpu.VMEM((GD, TOK), F32)],
            10,
            (1,),
        )

    def through(half, parts, first):
        ins = [(code, SMEM), (xt, block((HALF, TOK), half, 0))]
        for dq, dk, dv, far in parts:
            ins += [(dq, VMEM), (dk, VMEM), (dv, VMEM), (swap(far, links, -1), VMEM)]
        ins += [(qkv_weight, block((3, 2, GD, GD), 0, half, 0, 0))]
        ins += [(gfirst, block((HALF, TOK), half, 0)), (gvec1, block((HALF, 2), half, 0))]
        ins += [(gvec2, block((HALF, 2), half, 0))]
        shape = (8, 48, WIDTH)
        outs = [((TOK, D), BF16, block((TOK, HALF), 0, half))]
        if half:
            ins += [(first[1], VMEM), (first[0], ANY)]
            outs += [(shape, F32, VMEM), (shape, BF16, VMEM)]
        else:
            outs += [(shape, F32, VMEM)]
        return run(
            partial(through_kernel, half=half),
            "through_qkv",
            ins,
            outs,
            [pltpu.VMEM(shape, F32)] if half else [],
            10,
            (1,),
            None,
            {len(ins) - 1: 0} if half else None,
        )

    rows = (GROUPS, GD, D)

    def finish(total, far, into, way, n):
        def half(c):
            return (c[0] ^ far, 0, 0)

        outs = [(rows, F32, pl.BlockSpec((2, GD, D), lambda _, c: half(c)))] * n
        outs += [((8, 128), F32, pl.BlockSpec((8, 128), lambda _, c: (0, 0)))]
        ins = [(total.far if far else total.near, pl.BlockSpec((8, 48 * n, D), lambda _, c: (0, 0, 0)))]
        ins += [(x, ANY) for x in into]
        kernel = partial(finish_kernel, far=far, way=way, outs=n)
        return run(kernel, "finish", ins, outs, [], 12, (1,), code, {2 + i: i for i in range(len(into))})[:n]

    parts = [attention_back(0)]
    ffn_out.fold()
    others.fold()
    parts += [attention_back(1)]
    ffn_out.fold()
    parts += [attention_back(2)]
    others.fold()
    first = through(0, parts[:2], None)
    ffn_out.meet()
    parts += [attention_back(3)]
    others.fold()
    grad_input, keep, send = through(1, parts[2:], first)
    others.meet()
    qkv = Total(run, links, "sum_qkv", keep, swap(send, links, -1))
    qkv.fold()
    ffn_out.whole()
    ffn_out.join()
    qkv.fold()
    others.whole()
    qkv.fold()
    others.join()
    qkv.meet()
    ffn_out.join()
    others.join()
    qkv.whole()
    ffn_out.join()
    qkv.join()
    near_out = finish(ffn_out, 0, [], 1, 1)
    qkv.join()
    others.join()
    (g2,) = finish(ffn_out, 1, near_out, 1, 1)
    half_way = finish(others, 0, [], 0, 2)
    qkv.join()
    g1, go = finish(others, 1, half_way, 0, 2)
    gq, *vectors = run(
        finish_qkv_kernel,
        "finish_qkv",
        [(code, SMEM), (qkv.near, VMEM), (qkv.far, VMEM)],
        [((3, GROUPS, GD, GD), F32, VMEM)] + [((D,), F32, VMEM)] * 4,
        [pltpu.VMEM((GROUPS, GD, 128), F32)],
        8,
    )
    return (output, grad_input, gq, go.reshape(D, D), g1, jnp.swapaxes(g2, 1, 2)) + tuple(vectors)


def solution(mesh):
    flat = Mesh(mesh.devices.reshape(-1), ("dev",))
    links = Links(mesh.shape["seq"], [[0, 1, 2], [1, 2, 0]])
    upright = Links(mesh.shape["seq"], [[2, 0, 1], [0, 2, 1]])
    split, copied = P("dev"), P()
    return jax.shard_map(
        partial(per_device, links, upright),
        mesh=flat,
        in_specs=(split, split) + (copied,) * 8 + (split,),
        out_specs=(split, split) + (copied,) * 8,
        check_vma=False,
    )
```

```python
from functools import partial

import jax
import jax.numpy as jnp
from jax import lax
from jax.experimental import pallas as pl
from jax.experimental.pallas import tpu as pltpu
from jax.sharding import Mesh, PartitionSpec as P

F32 = jnp.float32
BF16 = jnp.bfloat16
EPSILON = 1e-05
HEADS = 12
HEAD_DIM = 64
D = 768
GROUPS = 4
GD = D // GROUPS
FF = 3072
GF = FF // GROUPS
TOK = 768
BLK = 256
SHORT = 128
EXT = 512
WIDTH = 640
HALF = D // 2
COST = dict(project=3, attend=9, forward=19, backward=6, weights=4, attention=4, through=3, sum=9, finish=3)


def nn(a, b):
    return lax.dot_general(a, b, (((1,), (0,)), ((), ())), preferred_element_type=F32)


def nt(a, b):
    return lax.dot_general(a, b, (((1,), (1,)), ((), ())), preferred_element_type=F32)


def tn(a, b):
    return lax.dot_general(a, b, (((0,), (0,)), ((), ())), preferred_element_type=F32)


def gelu_parts(u):
    a = jnp.abs(u) * 0.7071067811865476
    t = 1.0 / (1.0 + 0.3275911 * a)
    e = jnp.exp(-0.5 * (u * u))
    poly = t * (
        0.254829592
        + t * (-0.284496736 + t * (1.421413741 + t * (-1.453152027 + t * 1.061405429)))
    )
    tail = 0.5 * poly * e
    phi = jnp.where(u < 0, tail, 1.0 - tail)
    return u * phi, phi + u * (e * 0.3989422804014327)


def pipelined(items, first, second, third, lag, last):
    n = len(items)
    for t in range(n + last):
        if t < n:
            first(items[t])
        if 0 <= t - lag < n:
            second(items[t - lag])
        if 0 <= t - last < n:
            third(items[t - last])


def stages(items, first, second, third, lag, last):
    n = len(items)
    for t in range(n + last):
        if t < n:
            first(items[t])
        if 0 <= t - lag < n:
            second(items[t - lag])
        if 0 <= t - last < n:
            third(items[t - last])
        yield


def weave(*streams):
    streams = list(streams)
    while streams:
        for stream in list(streams):
            if next(stream, streams) is streams:
                streams.remove(stream)


def project_kernel(x_ref, wqkv_ref, xt_ref, q_ref, k_ref, v_ref):
    xt_ref[...] = x_ref[...].T
    for g in range(GROUPS):
        rows = slice(g * GD, (g + 1) * GD)
        xg = xt_ref[rows, :]
        q_ref[rows, :] = (tn(wqkv_ref[0, g], xg).astype(BF16).astype(F32) * 0.125).astype(BF16)
        k_ref[rows, :] = tn(wqkv_ref[1, g], xg).astype(BF16)
        v_ref[rows, :] = tn(wqkv_ref[2, g], xg).astype(BF16)


def pick(ref, far_ref, hr, b, two):
    if b == 0:
        other = far_ref[hr, :BLK]
    elif b == 1:
        other = jnp.where(two, far_ref[hr, BLK:], ref[hr, 2 * BLK :])
    else:
        other = ref[hr, BLK + SHORT : 2 * BLK]
    return jnp.concatenate([ref[hr, b * BLK : (b + 1) * BLK], other], 1)


def attend_kernel(
    seg_ref, ids_ref, xp_ref, wqkv_ref, q_ref, k_ref, v_ref,
    kp_ref, vp_ref, ctx_ref, lse_ref, bias_ref,
):
    two = seg_ref[BLK] == 1
    row = ids_ref[...].reshape(1, TOK)

    def lanes(b):
        return jnp.broadcast_to(row[:, b * BLK : (b + 1) * BLK], (BLK, BLK))

    def same(kb, qb):
        return jnp.where(lanes(kb).T == lanes(qb), 0.0, -1e30).astype(BF16)

    bias_ref[0, :BLK] = same(1, 1)
    bias_ref[0, BLK:] = jnp.where(two, jnp.zeros((BLK, BLK), BF16), same(2, 1))
    bias_ref[1, :BLK] = same(2, 2)
    bias_ref[1, BLK : BLK + SHORT] = same(1, 2)[SHORT:]
    xpt = xp_ref[:EXT, :].T
    for g in range(GROUPS):
        rows = slice(g * GD, (g + 1) * GD)
        kp_ref[rows, :] = tn(wqkv_ref[1, g], xpt[rows]).astype(BF16)
        vp_ref[rows, :] = tn(wqkv_ref[2, g], xpt[rows]).astype(BF16)

    def heads(i, carry):
        items = []
        for u in range(6):
            h = i * 6 + u
            hr = pl.ds(pl.multiple_of(h * HEAD_DIM, HEAD_DIM), HEAD_DIM)
            items += [{"h": h, "hr": hr, "b": b, "qc": slice(b * BLK, (b + 1) * BLK)} for b in range(3)]

        def scores(d):
            s = tn(pick(k_ref, kp_ref, d["hr"], d["b"], two), q_ref[d["hr"], d["qc"]])
            if d["b"]:
                s = s + bias_ref[d["b"] - 1, : s.shape[0]].astype(F32)
            d["s"] = s

        def weights(d):
            s = d.pop("s")
            d["top"] = jnp.max(s, 0, keepdims=True)
            p = jnp.exp(s - d["top"])
            d["total"] = jnp.sum(p, 0, keepdims=True)
            d["p"] = p.astype(BF16)

        def mix(d):
            c = nn(pick(v_ref, vp_ref, d["hr"], d["b"], two), d.pop("p"))
            ctx_ref[d["hr"], d["qc"]] = (c * (1.0 / d["total"])).astype(BF16)
            lse_ref[d["h"], :, d["qc"]] = d["top"] + jnp.log(d["total"])

        pipelined(items, scores, weights, mix, 2, 3)
        return carry

    lax.fori_loop(0, HEADS // 6, heads, 0)


PARTS = [(g, slice(j * BLK, (j + 1) * BLK)) for g in range(GROUPS) for j in range(GF // BLK)]


def columns(ref):
    wide = jnp.broadcast_to(ref[...].reshape(1, D), (128, D)).T
    return jnp.concatenate([wide, wide], 1)


def halves(x):
    return x[:, :128] + x[:, 128:]


def scatter(part, jj, g, keep_ref, send_ref, at, low, far):
    for r in range(4):
        piece = part[48 * r : 48 * (r + 1)].astype(BF16)
        pos = ((g & 1) * 4 + r) ^ (low if jj < 2 else far)
        ref = keep_ref if jj < 2 else send_ref
        ref[pos, at : at + 48] = piece


def forward_kernel(
    code_ref, xt_ref, ctx_ref, wo_ref, w1_ref, w2t_ref, cot_ref, ag_ref, as_ref, fg_ref, fs_ref,
    out_ref, hid_ref, n1_ref, inv1_ref, gpr_ref, gsec_ref, gfeed_ref, keep_ref, send_ref, gvec_ref,
    wot, w1t, act, nb, gacc, held,
):
    core, low, far = code_ref[0], code_ref[3], code_ref[4]
    for j, ref in enumerate((ag_ref, as_ref, fg_ref, fs_ref)):
        nb[j] = columns(ref)
    wot[...] = wo_ref[...].T
    for g in range(GROUPS):
        w1t[g] = w1_ref[g].T
    gacc[...] = jnp.zeros_like(gacc)

    channels = [slice(g * GD, (g + 1) * GD) for g in range(GROUPS)]

    def at(t):
        return pl.ds(pl.multiple_of(t * BLK, BLK), BLK)

    def mean(pieces):
        return sum(jnp.sum(x, 0, keepdims=True) for x in pieces) * (1.0 / D)

    def enter(t):
        tc, r = at(t), []
        for ch in channels:
            r.append(xt_ref[ch, tc].astype(F32) + nn(wot[ch], ctx_ref[:, tc]))
            yield
        average = mean(r)
        centre = [x - average for x in r]
        yield
        inv1 = lax.rsqrt(mean([x * x for x in centre]) + EPSILON)
        inv1_ref[:, tc] = inv1
        yield
        for ch, x in zip(channels, centre):
            n1 = x * inv1
            n1_ref[ch, tc] = n1
            hidden = n1 * nb[0, ch] + nb[1, ch]
            hid_ref[ch, tc] = hidden.astype(BF16)
            held[t & 1, ch] = hidden
            yield

    def middle(t, feeds):
        tc, up = at(t), {}

        def rise(p):
            g, fr = p
            up[g, fr.start] = nn(w1t[g, fr], hid_ref[channels[g], tc])

        def bend(p):
            g, fr = p
            a, slope = gelu_parts(up.pop((g, fr.start)))
            act[g, fr, tc] = a.astype(BF16)
            gpr_ref[g, fr, tc] = slope.astype(BF16)

        def fall(p):
            if p[1].stop == GF:
                feeds.append(nn(w2t_ref[p[0]], act[p[0], :, tc]))

        yield from stages(PARTS, rise, bend, fall, 2, 3)

    def leave(t, feeds):
        tc = at(t)
        r2 = [held[t & 1, ch] + x for ch, x in zip(channels, feeds)]
        average = mean(r2)
        centre = [x - average for x in r2]
        yield
        inv2 = lax.rsqrt(mean([x * x for x in centre]) + EPSILON)
        yield
        n2, low = [], []
        for ch, x in zip(channels, centre):
            n2.append(x * inv2)
            low.append((n2[-1] * nb[2, ch] + nb[3, ch]).astype(BF16))
            yield
        out_ref[tc, :] = jnp.concatenate(low, 0).T
        turned = cot_ref[tc, :].T
        yield
        cg = []
        for ch, n in zip(channels, n2):
            c = turned[ch].astype(F32)
            gacc[0, ch] += halves(c * n)
            gacc[1, ch] += halves(c)
            cg.append(c * nb[2, ch])
            yield
        first = mean(cg)
        second = mean([x * n for x, n in zip(cg, n2)])
        yield
        for ch, x, n in zip(channels, cg, n2):
            gsec = inv2 * (x - first - n * second)
            gsec_ref[ch, tc] = gsec
            gfeed_ref[ch, tc] = gsec.astype(BF16)
            yield

    def tile(t, carry):
        feeds = []
        weave(middle(t, feeds), enter(jnp.minimum(t + 1, TOK // BLK - 1)))
        weave(leave(t, feeds))
        return carry

    weave(enter(0))
    lax.fori_loop(0, TOK // BLK, tile, 0)
    for j in range(2):
        gvec_ref[:, j : j + 1] = jnp.sum(gacc[j], 1, keepdims=True)
    for jj in (2, 3, 0, 1):
        g = jj ^ (2 * core)
        gr = pl.ds(pl.multiple_of(g * GD, GD), GD)
        scatter(nt(gfeed_ref[gr, :], act[g]), jj, g, keep_ref, send_ref, 0, low, far)


def backward_kernel(
    wo_ref, w1_ref, w2t_ref, n1_ref, inv1_ref, gpr_ref, gsec_ref, gfeed_ref, ag_ref,
    gctx_ref, gfirst_ref, gup, gatt, gvec_ref,
    w2, nb, gacc, held,
):
    nb[...] = columns(ag_ref)
    for g in range(GROUPS):
        w2[g] = w2t_ref[g].T
    gacc[...] = jnp.zeros_like(gacc)

    channels = [slice(g * GD, (g + 1) * GD) for g in range(GROUPS)]

    def at(t):
        return pl.ds(pl.multiple_of(t * BLK, BLK), BLK)

    def mean(pieces):
        return sum(jnp.sum(x, 0, keepdims=True) for x in pieces) * (1.0 / D)

    def feed_back(t):
        tc, back = at(t), {}

        def lift(p):
            g, fr = p
            back[g, fr.start] = nn(w2[g, fr], gfeed_ref[channels[g], tc])

        def scale(p):
            g, fr = p
            gup[g, fr, tc] = (back.pop((g, fr.start)) * gpr_ref[g, fr, tc].astype(F32)).astype(BF16)

        def drop(p):
            g, fr = p
            if fr.stop == GF:
                held[t & 1, channels[g]] = gsec_ref[channels[g], tc] + nn(w1_ref[g], gup[g, :, tc])

        yield from stages(PARTS, lift, scale, drop, 2, 3)

    def norm_back(t):
        tc, sc = at(t), []
        for ch in channels:
            ghid = held[t & 1, ch]
            gacc[0, ch] += halves(ghid * n1_ref[ch, tc])
            gacc[1, ch] += halves(ghid)
            sc.append(ghid * nb[ch])
            yield
        first = mean(sc)
        second = mean([x * n1_ref[ch, tc] for ch, x in zip(channels, sc)])
        yield
        for ch, x in zip(channels, sc):
            gfirst = inv1_ref[:, tc] * (x - first - n1_ref[ch, tc] * second)
            gfirst_ref[ch, tc] = gfirst
            gatt[ch, tc] = gfirst.astype(BF16)
            yield
        for ch in channels:
            gctx_ref[ch, tc] = nn(wo_ref[ch, :], gatt[:, tc]).astype(BF16)
            yield

    def tile(t, carry):
        weave(feed_back(t + 1), norm_back(t))
        return carry

    weave(feed_back(0))
    lax.fori_loop(0, TOK // BLK - 1, tile, 0)
    weave(norm_back(TOK // BLK - 1))
    for j in range(2):
        gvec_ref[:, j : j + 1] = jnp.sum(gacc[j], 1, keepdims=True)


def weights_kernel(code_ref, ctx_ref, hid_ref, gup_ref, gatt_ref, keep_ref, send_ref):
    core, low, far = code_ref[0], code_ref[1], code_ref[2]
    for jj in (2, 3, 0, 1):
        g = jj ^ (2 * core)
        gr = pl.ds(pl.multiple_of(g * GD, GD), GD)
        scatter(nt(hid_ref[gr, :], gup_ref[g]), jj, g, keep_ref, send_ref, 0, low, far)
        if jj & 1 == 0:
            rows = pl.ds(pl.multiple_of((jj // 2 ^ core) * HALF, HALF), HALF)
            both = nt(ctx_ref[rows, :], gatt_ref[...])
        mine = both[:GD] if jj & 1 == 0 else both[GD:]
        scatter(mine, jj, g, keep_ref, send_ref, 48, low, far)


def back_kernel(
    seg_ref, q_ref, k_ref, v_ref, kp_ref, vp_ref, gctx_ref, lse_ref, bias_ref,
    dq_ref, dk_ref, dv_ref, far_ref, dk, dv,
):
    two = seg_ref[BLK] == 1
    scale = jnp.where(two, 1.0, 0.0)
    dk[...] = jnp.zeros_like(dk)
    dv[...] = jnp.zeros_like(dv)

    items = []
    for h in range(3):
        hr = slice(h * HEAD_DIM, (h + 1) * HEAD_DIM)
        items += [{"h": h, "hr": hr, "b": b, "qc": slice(b * BLK, (b + 1) * BLK)} for b in range(3)]

    def scores(d):
        hr, qc, b = d["hr"], d["qc"], d["b"]
        s = tn(pick(k_ref, kp_ref, hr, b, two), q_ref[hr, qc])
        if b:
            s = s + bias_ref[b - 1, : s.shape[0]].astype(F32)
        d["s"] = s
        d["dp"] = tn(pick(v_ref, vp_ref, hr, b, two), gctx_ref[hr, qc])

    def weights(d):
        p = jnp.exp(d.pop("s") - lse_ref[d["h"], :, d["qc"]])
        dp = d.pop("dp")
        dots = jnp.sum(p * dp, 0, keepdims=True)
        d["ds"] = (p * (dp - dots)).astype(BF16)
        d["p"] = p.astype(BF16)

    def mix(d):
        hr, qc, b = d["hr"], d["qc"], d["b"]
        ds = d.pop("ds")
        dq_ref[hr, qc] = (nn(pick(k_ref, kp_ref, hr, b, two), ds) * 0.125).astype(BF16)
        gk = nt(q_ref[hr, qc], ds)
        gv = nt(gctx_ref[hr, qc], d.pop("p"))
        for acc, grad, slot in ((dk, gk, 0), (dv, gv, 1)):
            acc[hr, qc] += grad[:, :BLK]
            other = grad[:, BLK:]
            if b == 0:
                far_ref[slot, hr, :BLK] = other.astype(BF16)
            elif b == 1:
                far_ref[slot, hr, BLK:] = (other * scale).astype(BF16)
                acc[hr, 2 * BLK :] += other * (1.0 - scale)
            else:
                acc[hr, BLK + SHORT : 2 * BLK] += other

    pipelined(items, scores, weights, mix, 1, 2)
    dk_ref[...] = dk[...]
    dv_ref[...] = dv[...]


def through_kernel(
    code_ref, xt_ref, dqa_ref, dka_ref, dva_ref, ba_ref, dqb_ref, dkb_ref, dvb_ref, bb_ref, wqkv_ref,
    gfirst_ref, gvec1_ref, gvec2_ref, *refs, half,
):
    core = code_ref[0]
    order = jnp.where(core == half, code_ref[1], code_ref[2])
    if half:
        first_ref, _, gin_ref, keep_ref, send_ref, piece_ref = refs
    else:
        gin_ref, piece_ref = refs
    through = []
    groups = ((dqa_ref, dka_ref, dva_ref, ba_ref), (dqb_ref, dkb_ref, dvb_ref, bb_ref))
    for i, (dq_ref, dk_ref, dv_ref, b_ref) in enumerate(groups):
        rows = slice(i * GD, (i + 1) * GD)
        grads = [dq_ref[...]]
        for slot, ref in ((0, dk_ref), (1, dv_ref)):
            own = ref[...]
            own = jnp.concatenate([own[:, :EXT] + b_ref[slot].astype(F32), own[:, EXT:]], 1)
            grads.append(own.astype(BF16))
        through.append(sum(nn(wqkv_ref[t, i], grads[t]) for t in range(3)))
        row = jnp.concatenate(
            [nt(xt_ref[rows], grad) for grad in grads]
            + [gvec1_ref[rows], gvec2_ref[rows], jnp.zeros((GD, WIDTH - 3 * GD - 4), F32)],
            1,
        )
        for r in range(4):
            piece_ref[(i * 4 + r) ^ order] = row[48 * r : 48 * (r + 1)]
    if half:
        mine, other = piece_ref[...], first_ref[...]
        keep_ref[...] = jnp.where(core == 1, mine, other)
        send_ref[...] = jnp.where(core == 1, other, mine).astype(BF16)
    gin_ref[...] = (gfirst_ref[...] + jnp.concatenate(through, 0)).astype(BF16).T


def chunks(code_ref, near_ref, far_ref):
    core, low, far = code_ref[0], code_ref[1], code_ref[2]
    for other, ref in ((0, near_ref), (1, far_ref)):
        for a in range(8):
            g = (other ^ core) * 2 + a // 4
            rows = slice(48 * (a % 4), 48 * (a % 4 + 1))
            yield g, rows, ref[a ^ (far if other else low)].astype(F32)


def finish_kernel(code_ref, half_ref, *refs, far, way, outs):
    *refs, token_ref = refs
    token_ref[...] = jnp.zeros_like(token_ref)
    order = code_ref[1 + 2 * way + far]
    for a in range(8):
        part = half_ref[a ^ order].astype(F32)
        rows = slice(48 * (a % 4), 48 * (a % 4 + 1))
        for i, ref in enumerate(refs[-outs:]):
            ref[a // 4, rows] = part[48 * i : 48 * (i + 1)]


def finish_qkv_kernel(code_ref, near_ref, far_ref, gq_ref, ag_ref, as_ref, fg_ref, fs_ref, vec):
    for g, rows, part in chunks(code_ref, near_ref, far_ref):
        for t in range(3):
            gq_ref[t, g, rows] = part[:, t * GD : (t + 1) * GD]
        vec[g, rows] = part[:, 512:640]
    turned = vec[...].reshape(D, 128).T
    for i, ref in enumerate((ag_ref, as_ref, fg_ref, fs_ref)):
        ref[...] = turned[64 + i : 65 + i].reshape(D)


def fold_kernel(keep_ref, came_ref, kept_ref, send_ref):
    n = kept_ref.shape[0]
    kept_ref[...] = keep_ref[:n].astype(F32) + came_ref[:n].astype(F32)
    send_ref[...] = (keep_ref[n:].astype(F32) + came_ref[n:].astype(F32)).astype(BF16)


def meet_kernel(*refs):
    *ins, out_ref = refs
    at = 0
    for keep_ref, came_ref in zip(ins[::2], ins[1::2]):
        rows = keep_ref.shape[1]
        out_ref[:, at : at + rows] = (keep_ref[...].astype(F32) + came_ref[...].astype(F32)).astype(BF16)
        at += rows


def join_kernel(near_ref, far_ref, out_ref):
    n = near_ref.shape[0]
    out_ref[:n] = near_ref[...]
    out_ref[n:] = far_ref[...]


SMEM = pl.BlockSpec(memory_space=pltpu.SMEM)
VMEM = pl.BlockSpec(memory_space=pltpu.VMEM)
ANY = pl.BlockSpec(memory_space=pl.ANY)


class Steps:
    def __init__(self):
        self.last = None

    def __call__(self, kernel, name, ins, outs, scratch, limit, grid=(), code=None, aliases=None):
        n, free = len(ins) + (code is not None), self.last is None
        if not free:
            ins = ins + [(self.last, ANY)]
        specs = dict(
            grid=grid,
            in_specs=[spec for _, spec in ins],
            out_specs=[spec for _, _, spec in outs],
            scratch_shapes=scratch,
        )
        if code is not None:
            specs = dict(grid_spec=pltpu.PrefetchScalarGridSpec(num_scalar_prefetch=1, **specs))
        results = pl.pallas_call(
            kernel if free else lambda *refs: kernel(*refs[:n], *refs[n + 1 :]),
            out_shape=[jax.ShapeDtypeStruct(s, d) for s, d, _ in outs],
            compiler_params=pltpu.CompilerParams(vmem_limit_bytes=limit << 20),
            cost_estimate=pl.CostEstimate(flops=int(COST[name.split('_')[0]] * 1e9), bytes_accessed=1024, transcendentals=0),
            input_output_aliases=aliases or {},
            name=name,
            **specs,
        )(*([] if code is None else [code]), *[array for array, _ in ins])
        self.last = results[-1]
        return results


def block(shape, *at):
    return pl.BlockSpec(shape, lambda _: at)


class Links:
    def __init__(self, n_seq, orders):
        bits = n_seq.bit_length() - 1
        self.n = n_seq * 2
        self.orders = [order + list(range(3, bits)) for order in orders]
        self.bits = bits

    def pairs(self, step):
        if step < 0:
            return [(i, i ^ 1) for i in range(self.n)]
        return [(i, i ^ (2 << self.orders[i & 1][step])) for i in range(self.n)]

    def code(self, seq, core):
        first, second = [sum(((seq >> order[step]) & 1) << (2 - step) for step in range(3)) for order in self.orders]
        return jnp.where(core == 0, first, second)


def swap(x, links, step):
    return lax.ppermute(x, "dev", links.pairs(step))


class Total:
    def __init__(self, run, links, name, keep, came):
        self.run, self.links, self.name = run, links, name
        self.keep, self.came = keep, came
        self.step = 0

    def small(self, kernel, ins, outs):
        spec = [(x, VMEM) for x in ins]
        return self.run(kernel, self.name, spec, [o + (VMEM,) for o in outs], [], 4)

    def fold(self):
        shape = (self.keep.shape[0] // 2,) + self.keep.shape[1:]
        self.keep, send = self.small(fold_kernel, [self.keep, self.came], [(shape, F32), (shape, BF16)])
        self.came = swap(send, self.links, self.step)
        self.step += 1

    def meet(self, *others):
        parts = [*others, self]
        shape = (1, sum(p.keep.shape[1] for p in parts), self.keep.shape[2])
        ins = [x for p in parts for x in (p.keep, p.came)]
        (self.near,) = self.small(meet_kernel, ins, [(shape, BF16)])
        for step in range(3, self.links.bits - 1):
            (self.near,) = self.small(meet_kernel, [self.near, swap(self.near, self.links, step)], [(shape, BF16)])
        self.far = swap(self.near, self.links, self.links.bits - 1)

    def whole(self):
        (self.near,) = self.small(meet_kernel, [self.near, self.far], [(self.near.shape, BF16)])
        self.step = 2
        self.far = swap(self.near, self.links, self.step)

    def join(self):
        shape = (self.near.shape[0] * 2,) + self.near.shape[1:]
        (self.near,) = self.small(join_kernel, [self.near, self.far], [(shape, BF16)])
        self.step -= 1
        self.far = swap(self.near, self.links, self.step)


def per_device(
    links, upright, inputs, segment_ids, qkv_weight, out_weight, ffn_in_weight, ffn_out_weight,
    attn_gain, attn_shift, ffn_gain, ffn_shift, out_cotangent,
):
    me = lax.axis_index("dev")
    seq, core = me >> 1, me & 1
    codes = [core]
    for way in (links, upright):
        codes += [way.code(seq, core), way.code(seq, 1 - core)]
    code = jnp.stack(codes).astype(jnp.int32)
    partner = swap(inputs, links, -1)
    square = (D, TOK)
    large = (GROUPS, GF, TOK)
    run = Steps()
    xt, q, k, v = run(
        project_kernel,
        "project",
        [(inputs, VMEM), (qkv_weight, VMEM)],
        [(square, BF16, VMEM)] * 4,
        [],
        12,
    )
    kp, vp, ctx, lse, bias = run(
        attend_kernel,
        "attend",
        [(segment_ids, SMEM), (segment_ids, VMEM), (partner, VMEM), (qkv_weight, VMEM)]
        + [(q, VMEM), (k, VMEM), (v, VMEM)],
        [((D, EXT), BF16, VMEM), ((D, EXT), BF16, VMEM), (square, BF16, VMEM), ((HEADS, 1, TOK), F32, VMEM)]
        + [((2, 2 * BLK, BLK), BF16, VMEM)],
        [],
        12,
    )
    weight2t = jnp.swapaxes(ffn_out_weight, 1, 2)
    output, hid, n1, inv1, gpr, gsec, gfeed, keep, send, gvec2 = run(
        forward_kernel,
        "forward",
        [(code, SMEM), (xt, VMEM), (ctx, VMEM), (out_weight, VMEM), (ffn_in_weight, VMEM), (weight2t, VMEM)]
        + [(out_cotangent, VMEM), (attn_gain, VMEM), (attn_shift, VMEM), (ffn_gain, VMEM), (ffn_shift, VMEM)],
        [((TOK, D), BF16, VMEM), (square, BF16, VMEM), (square, F32, VMEM), ((1, TOK), F32, VMEM), (large, BF16, VMEM)]
        + [(square, F32, VMEM), (square, BF16, VMEM), ((8, 48, D), BF16, VMEM), ((8, 48, D), BF16, VMEM)]
        + [((D, 2), F32, VMEM)],
        [
            pltpu.VMEM((D, D), BF16), pltpu.VMEM((GROUPS, GF, GD), BF16), pltpu.VMEM(large, BF16),
            pltpu.VMEM((4, D, BLK), F32), pltpu.VMEM((2, D, 128), F32), pltpu.VMEM((2, D, BLK), F32),
        ],
        20,
    )
    ffn_out = Total(run, upright, "sum_ffn_out", keep, swap(send, links, -1))
    gctx, gfirst, gup, gatt, gvec1 = run(
        backward_kernel,
        "backward",
        [(out_weight, VMEM), (ffn_in_weight, VMEM), (weight2t, VMEM)]
        + [(n1, VMEM), (inv1, VMEM), (gpr, VMEM), (gsec, VMEM), (gfeed, VMEM), (attn_gain, VMEM)],
        [(square, BF16, VMEM), (square, F32, VMEM), (large, BF16, VMEM), (square, BF16, VMEM), ((D, 2), F32, VMEM)],
        [
            pltpu.VMEM((GROUPS, GF, GD), BF16), pltpu.VMEM((D, BLK), F32), pltpu.VMEM((2, D, 128), F32),
            pltpu.VMEM((2, D, BLK), F32),
        ],
        12,
    )
    ffn_out.fold()
    message = ((8, 96, D), BF16, VMEM)
    keep, send = run(
        weights_kernel,
        "weights",
        [(code, SMEM), (ctx, VMEM), (hid, VMEM), (gup, VMEM), (gatt, VMEM)],
        [message, message],
        [],
        12,
    )
    others = Total(run, links, "sum_others", keep, swap(send, links, -1))

    def attention_back(g):
        rows = partial(lambda width: block((GD, width), g, 0))
        return run(
            back_kernel,
            "attention_back",
            [(segment_ids, SMEM), (q, rows(TOK)), (k, rows(TOK)), (v, rows(TOK)), (kp, rows(EXT)), (vp, rows(EXT))]
            + [(gctx, rows(TOK)), (lse, block((3, 1, TOK), g, 0, 0)), (bias, VMEM)],
            [((GD, TOK), BF16, VMEM), ((GD, TOK), F32, VMEM), ((GD, TOK), F32, VMEM), ((2, GD, EXT), BF16, VMEM)],
            [pltpu.VMEM((GD, TOK), F32), pltpu.VMEM((GD, TOK), F32)],
            10,
            (1,),
        )

    def through(half, parts, first):
        ins = [(code, SMEM), (xt, block((HALF, TOK), half, 0))]
        for dq, dk, dv, far in parts:
            ins += [(dq, VMEM), (dk, VMEM), (dv, VMEM), (swap(far, links, -1), VMEM)]
        ins += [(qkv_weight, block((3, 2, GD, GD), 0, half, 0, 0))]
        ins += [(gfirst, block((HALF, TOK), half, 0)), (gvec1, block((HALF, 2), half, 0))]
        ins += [(gvec2, block((HALF, 2), half, 0))]
        shape = (8, 48, WIDTH)
        outs = [((TOK, D), BF16, block((TOK, HALF), 0, half))]
        if half:
            ins += [(first[1], VMEM), (first[0], ANY)]
            outs += [(shape, F32, VMEM), (shape, BF16, VMEM)]
        else:
            outs += [(shape, F32, VMEM)]
        return run(
            partial(through_kernel, half=half),
            "through_qkv",
            ins,
            outs,
            [pltpu.VMEM(shape, F32)] if half else [],
            10,
            (1,),
            None,
            {len(ins) - 1: 0} if half else None,
        )

    rows = (GROUPS, GD, D)

    def finish(total, far, into, way, n):
        def half(c):
            return (c[0] ^ far, 0, 0)

        outs = [(rows, F32, pl.BlockSpec((2, GD, D), lambda _, c: half(c)))] * n
        outs += [((8, 128), F32, pl.BlockSpec((8, 128), lambda _, c: (0, 0)))]
        ins = [(total.far if far else total.near, pl.BlockSpec((8, 48 * n, D), lambda _, c: (0, 0, 0)))]
        ins += [(x, ANY) for x in into]
        kernel = partial(finish_kernel, far=far, way=way, outs=n)
        return run(kernel, "finish", ins, outs, [], 12, (1,), code, {2 + i: i for i in range(len(into))})[:n]

    parts = [attention_back(0)]
    ffn_out.fold()
    others.fold()
    parts += [attention_back(1)]
    ffn_out.fold()
    parts += [attention_back(2)]
    others.fold()
    first = through(0, parts[:2], None)
    parts += [attention_back(3)]
    others.fold()
    ffn_out.meet()
    grad_input, keep, send = through(1, parts[2:], first)
    others.meet()
    qkv = Total(run, links, "sum_qkv", keep, swap(send, links, -1))
    qkv.fold()
    ffn_out.whole()
    ffn_out.join()
    qkv.fold()
    others.whole()
    qkv.fold()
    others.join()
    qkv.meet()
    ffn_out.join()
    others.join()
    qkv.whole()
    ffn_out.join()
    qkv.join()
    near_out = finish(ffn_out, 0, [], 1, 1)
    qkv.join()
    others.join()
    (g2,) = finish(ffn_out, 1, near_out, 1, 1)
    half_way = finish(others, 0, [], 0, 2)
    qkv.join()
    g1, go = finish(others, 1, half_way, 0, 2)
    gq, *vectors = run(
        finish_qkv_kernel,
        "finish_qkv",
        [(code, SMEM), (qkv.near, VMEM), (qkv.far, VMEM)],
        [((3, GROUPS, GD, GD), F32, VMEM)] + [((D,), F32, VMEM)] * 4,
        [pltpu.VMEM((GROUPS, GD, 128), F32)],
        8,
    )
    return (output, grad_input, gq, go.reshape(D, D), g1, jnp.swapaxes(g2, 1, 2)) + tuple(vectors)


def solution(mesh):
    flat = Mesh(mesh.devices.reshape(-1), ("dev",))
    links = Links(mesh.shape["seq"], [[0, 1, 2], [1, 2, 0]])
    upright = Links(mesh.shape["seq"], [[2, 0, 1], [0, 2, 1]])
    split, copied = P("dev"), P()
    return jax.shard_map(
        partial(per_device, links, upright),
        mesh=flat,
        in_specs=(split, split) + (copied,) * 8 + (split,),
        out_specs=(split, split) + (copied,) * 8,
        check_vma=False,
    )
```
